32 devices in a mesh: dp: 8 (over z, y), cam: 4 (over x, core).
Axes of the slice: x: 2, y: 2, z: 4, core: 2. Of those that a mesh axis runs over, the one named last changes fastest.
Arguments:
- tokens: bfloat16 [32, 4, 304, 512], P('dp', 'cam'), may hold values from -6 to 6
- out_grad: bfloat16 [32, 4, 304, 512], P('dp', 'cam'), may hold values from -6 to 6
- joint_state: float32 [32, 1, 14], P('dp'), may hold values from -4 to 4
- joint_mask: int32 [32, 1, 14], P('dp'), may hold values from 0 to 1, as said below
- attn_master: float32 [4, 512, 512], P(None, ('dp', 'cam')), may hold values from -0.25 to 0.25
- attn_first: float32 [4, 512, 512], P(None, ('dp', 'cam'))
- attn_second: float32 [4, 512, 512], P(None, ('dp', 'cam'))
- attn_average: float32 [4, 512, 512], P(None, ('dp', 'cam')), may hold values from -0.25 to 0.25
- ffn_master: float32 [2, 512, 3200], P(None, ('dp', 'cam')), may hold values from -0.25 to 0.25
- ffn_first: float32 [2, 512, 3200], P(None, ('dp', 'cam'))
- ffn_second: float32 [2, 512, 3200], P(None, ('dp', 'cam'))
- ffn_average: float32 [2, 512, 3200], P(None, ('dp', 'cam')), may hold values from -0.25 to 0.25
- small_params: float32 [14464], replicated
- small_first: float32 [14464], replicated
- small_second: float32 [14464], replicated
- small_average: float32 [14464], replicated, may hold values from -3 to 3
Outputs:
- block_output: bfloat16 [32, 4, 304, 512], P('dp', 'cam')
- input_grad: float32 [32, 4, 304, 512], P('dp', 'cam')
- new_attn: float32 [4, 512, 512], P(None, ('dp', 'cam'))
- new_attn_first: float32 [4, 512, 512], P(None, ('dp', 'cam'))
- new_attn_second: float32 [4, 512, 512], P(None, ('dp', 'cam'))
- new_attn_average: float32 [4, 512, 512], P(None, ('dp', 'cam'))
- new_ffn: float32 [2, 512, 3200], P(None, ('dp', 'cam'))
- new_ffn_first: float32 [2, 512, 3200], P(None, ('dp', 'cam'))
- new_ffn_second: float32 [2, 512, 3200], P(None, ('dp', 'cam'))
- new_ffn_average: float32 [2, 512, 3200], P(None, ('dp', 'cam'))
- new_small: float32 [14464], replicated
- new_small_first: float32 [14464], replicated
- new_small_second: float32 [14464], replicated
- new_small_average: float32 [14464], replicated
The draws below stay inside these ranges and needn't reach their ends.
Inputs may be any that keep to these rules, and one draw needn't show every extreme that they name: `joint_mask`: each item's mask is one on its first 7 joints and zero on the rest, or one on all 14 joints.
All inputs are finite; a program needn't handle non-finite values.
Results may differ from the reference program's by a relative error of at most 0.015.
The reference program's roundings to bfloat16 on the way count: a program that leaves them out, or rounds other values in their place, can miss the bound.
Values may be sent and summed in bfloat16 or wider, within the bound.
No kernel may reach another device: no remote copies, remote signals or barrier semaphores. Data moves between devices by JAX's collectives and lax.ppermute only.
A program may use at most 192 MiB of HBM per device.

```python
import math
import jax
import jax.numpy as jnp
from jax import lax

D = 512
FF = 3200
HEADS = 8
NJ = 14
SEG = 304
ADAM_STEP = 10
HD = 64
IROWS = 32
SUBS = 1
ITEMS = 32
LEN = 1216
TOKENS = 38912
NSMALL = 14464
N_CAM = 4


def attn_grad_scales():
    root_tokens = TOKENS ** 0.5
    return jnp.array([0.7, 0.7, 0.7, 0.7], jnp.float32) * root_tokens


def small_grad_scales():
    root_tokens = TOKENS ** 0.5
    per_row = [0.7, 0.7, 0.7, 1.0, 1.0, 0.55, 1.0, 1.0]
    pieces = [jnp.full((D,), factor, jnp.float32) for factor in per_row]
    pieces.append(jnp.full((NJ * D,), (1.0 / LEN) ** 0.5, jnp.float32))
    pieces.append(jnp.full((FF,), 0.33, jnp.float32))
    return jnp.concatenate(pieces) * root_tokens


def second_draw(key, scales, shape):
    factors = jnp.exp(jax.random.uniform(key, shape, jnp.float32, 0.0, math.log(4.0)))
    return scales * scales * factors


def first_draw(key, scales, shape):
    return jax.random.truncated_normal(key, -4.0, 4.0, shape, jnp.float32) * scales


def draw_joint_mask(key, part):
    key = jax.random.fold_in(key, 19)
    full_robot = jax.random.randint(key, (IROWS, SUBS, 1), 0, 2)
    full_robot = full_robot.at[0, 0, 0].set(0)
    counts = 7 + 7 * full_robot
    joints = jnp.arange(NJ, dtype=jnp.int32)[None, None, :]
    return (joints < counts).astype(jnp.int32)


def draw_attn_first(key, part):
    key = jax.random.fold_in(key, 12)
    return first_draw(key, attn_grad_scales()[:, None, None], (4, D, D))


def draw_attn_second(key, part):
    key = jax.random.fold_in(key, 13)
    return second_draw(key, attn_grad_scales()[:, None, None], (4, D, D))


def draw_ffn_first(key, part):
    key = jax.random.fold_in(key, 14)
    return first_draw(key, 0.33 * TOKENS ** 0.5, (2, D, FF))


def draw_ffn_second(key, part):
    key = jax.random.fold_in(key, 15)
    return second_draw(key, 0.33 * TOKENS ** 0.5, (2, D, FF))


def draw_small_params(key, part):
    key = jax.random.fold_in(key, 16)
    centres = jnp.zeros((NSMALL,), jnp.float32)
    centres = centres.at[3 * D:4 * D].set(1.0).at[6 * D:7 * D].set(1.0)
    spreads = jnp.full((NSMALL,), 0.1, jnp.float32)
    spreads = spreads.at[3 * D:4 * D].set(0.25).at[6 * D:7 * D].set(0.25)
    spreads = spreads.at[8 * D:(8 + NJ) * D].set(NJ ** (-0.5))
    unit = jax.random.uniform(key, (NSMALL,), jnp.float32, -math.sqrt(3.0), math.sqrt(3.0))
    return centres + spreads * unit


def draw_small_first(key, part):
    key = jax.random.fold_in(key, 17)
    return first_draw(key, small_grad_scales(), (NSMALL,))


def draw_small_second(key, part):
    key = jax.random.fold_in(key, 18)
    return second_draw(key, small_grad_scales(), (NSMALL,))


def steps_of(key, shape, cuts, smallest, top_value):
    def one(position, shards_of):
        steps = jax.random.uniform(jax.random.fold_in(jax.random.fold_in(key, 6), position), (shards_of,), jnp.float32, smallest / len(cuts), top_value / len(cuts))
        return jnp.repeat(jnp.exp(steps), shape[position] // shards_of).reshape((-1,) + (1,) * (len(shape) - position - 1))

    factor_of = one(*cuts[0])
    for cut in cuts[1:]:
        factor_of = factor_of * one(*cut)
    return factor_of


def gaussian(own_key, shape, scale, reach, shards=(), kind=jnp.bfloat16):
    loudness = steps_of(own_key, shape, shards, -0.22, 0.18) if shards else 1.0
    entries = jax.random.normal(own_key, shape, jnp.float32) * scale * loudness
    return jnp.minimum(jnp.maximum(entries, -reach), reach).astype(kind)


def setup_inputs(seed: int = 0) -> dict:
    keys = jax.random.split(jax.random.key(seed), 17)
    tokens = gaussian(keys[0], (IROWS, N_CAM, SEG, D), 1.0, 6.0, ((0, 8), (1, 4)))
    out_grad = gaussian(keys[1], (IROWS, N_CAM, SEG, D), 1.0, 6.0, ((0, 8), (1, 4)))
    joint_state = gaussian(keys[2], (IROWS, SUBS, NJ), 1.0, 4.0, ((0, 8),), jnp.float32)
    joint_mask = draw_joint_mask(jax.random.fold_in(keys[16], 71), 0)
    attn_master = gaussian(keys[4], (4, D, D), D ** -0.5, 0.25, ((1, 32),), jnp.float32)
    attn_first = draw_attn_first(jax.random.fold_in(keys[16], 71), 0)
    attn_second = draw_attn_second(jax.random.fold_in(keys[16], 71), 0)
    attn_average = gaussian(keys[7], (4, D, D), D ** -0.5, 0.25, ((1, 32),), jnp.float32)
    ffn_master = gaussian(keys[8], (2, D, FF), D ** -0.5, 0.25, ((1, 32),), jnp.float32)
    ffn_first = draw_ffn_first(jax.random.fold_in(keys[16], 71), 0)
    ffn_second = draw_ffn_second(jax.random.fold_in(keys[16], 71), 0)
    ffn_average = gaussian(keys[11], (2, D, FF), D ** -0.5, 0.25, ((1, 32),), jnp.float32)
    small_params = draw_small_params(jax.random.fold_in(keys[16], 71), 0)
    small_first = draw_small_first(jax.random.fold_in(keys[16], 71), 0)
    small_second = draw_small_second(jax.random.fold_in(keys[16], 71), 0)
    small_average = gaussian(keys[15], (NSMALL,), 0.3, 3.0, (), jnp.float32)
    return dict(tokens=tokens, out_grad=out_grad, joint_state=joint_state, joint_mask=joint_mask, attn_master=attn_master, attn_first=attn_first, attn_second=attn_second, attn_average=attn_average, ffn_master=ffn_master, ffn_first=ffn_first, ffn_second=ffn_second, ffn_average=ffn_average, small_params=small_params, small_first=small_first, small_second=small_second, small_average=small_average)


@jax.custom_vjp
def low(v):
    return lax.optimization_barrier(v.astype(jnp.bfloat16)).astype(jnp.float32)

@jax.custom_vjp
def low_back(v):
    return v

def low_keep(v):
    return (low(v), None)

def low_pass(kept, grad):
    return (grad,)

def back_keep(v):
    return (v, None)

def back_low(kept, grad):
    return (low(grad),)
low.defvjp(low_keep, low_pass)
low_back.defvjp(back_keep, back_low)
highest = lax.Precision.HIGHEST
norm_eps = 1e-05
beta_first = 0.5
beta_second = 0.5
adam_eps = 1e-08
rate_matrix = 0.02
rate_small = 0.05
decay_matrix = 0.1
ema_decay = 0.75

def norm_rows(values, gain_row, shift_row):
    centred = values - lax.optimization_barrier(jnp.mean(values, axis=-1, keepdims=True))
    spread = lax.optimization_barrier(jnp.mean(centred * centred, axis=-1, keepdims=True))
    return centred * lax.rsqrt(spread + norm_eps) * gain_row + shift_row

def smooth_gate(values):
    return jax.nn.gelu(values, approximate=False)

def both_ways(values):
    return low_back(low(values))

def encoder_layer(sequence, joint_active, attn_full, ffn_full, small_full):
    vectors = small_full[:8 * D].reshape(8, D)
    joint_rows = small_full[8 * D:(8 + NJ) * D].reshape(NJ, D)
    hidden_bias = small_full[(8 + NJ) * D:]
    out_scale = (LEN / 3.0) ** 0.5
    joint_token = jnp.dot(joint_active, joint_rows, precision=highest)
    summed_in = sequence.at[1].add(joint_token)
    rounded = low(summed_in)
    queries = both_ways(jnp.dot(rounded, attn_full[0], precision=highest) + vectors[0]).reshape(LEN, HEADS, HD)
    keys_all = both_ways(jnp.dot(rounded, attn_full[1], precision=highest)).reshape(LEN, HEADS, HD)
    values_all = both_ways(jnp.dot(rounded, attn_full[2], precision=highest) + vectors[1]).reshape(LEN, HEADS, HD)
    scores = low_back(jnp.einsum('qhd,khd->hqk', queries, keys_all, precision=highest) * HD ** (-0.5))
    probs = low(jax.nn.softmax(scores, axis=-1))
    mixed = both_ways(jnp.einsum('hqk,khd->qhd', probs, values_all, precision=highest).reshape(LEN, D))
    branch = low_back(jnp.dot(mixed, attn_full[3], precision=highest) * out_scale + vectors[2])
    normed = norm_rows(summed_in + branch, vectors[3], vectors[4])
    inner = low_back(jnp.dot(low(normed), ffn_full[0], precision=highest) + hidden_bias)
    activated = low(smooth_gate(inner))
    output_branch = low_back(jnp.dot(activated, ffn_full[1].T, precision=highest) + vectors[5])
    return norm_rows(normed + output_branch, vectors[6], vectors[7])

def adam_update(master, grad_total, first_old, second_old, average_old, rate, decay):
    first_new = beta_first * first_old + (1.0 - beta_first) * grad_total
    second_new = beta_second * second_old + (1.0 - beta_second) * grad_total * grad_total
    first_hat = first_new / (1.0 - beta_first ** ADAM_STEP)
    second_hat = second_new / (1.0 - beta_second ** ADAM_STEP)
    master_new = master - rate * (first_hat / (jnp.sqrt(second_hat) + adam_eps) + decay * master)
    average_new = ema_decay * average_old + (1.0 - ema_decay) * master_new
    return (master_new, first_new, second_new, average_new)

def reference(tokens, out_grad, joint_state, joint_mask, attn_master, attn_first, attn_second, attn_average, ffn_master, ffn_first, ffn_second, ffn_average, small_params, small_first, small_second, small_average):
    sequences = tokens.astype(jnp.float32).reshape(IROWS, SUBS, 4, SEG, D).reshape(ITEMS, LEN, D)
    cotangents = out_grad.astype(jnp.float32).reshape(IROWS, SUBS, 4, SEG, D).reshape(ITEMS, LEN, D)
    joint_active = (joint_state * joint_mask.astype(jnp.float32)).reshape(ITEMS, NJ)
    attn_low = attn_master.astype(jnp.bfloat16).astype(jnp.float32)
    ffn_low = ffn_master.astype(jnp.bfloat16).astype(jnp.float32)

    def per_item(totals, inputs):
        sequence, cotangent, active_row = inputs

        def apply_layer(seq_in, attn_in, ffn_in, small_in):
            return encoder_layer(seq_in, active_row, attn_in, ffn_in, small_in)
        output, pullback = jax.vjp(apply_layer, sequence, attn_low, ffn_low, small_params)
        seq_grad, attn_grad, ffn_grad, small_grad = pullback(cotangent)
        totals = (totals[0] + attn_grad, totals[1] + ffn_grad, totals[2] + small_grad)
        return (totals, (output.astype(jnp.bfloat16), seq_grad))
    start = (jnp.zeros(attn_master.shape, jnp.float32), jnp.zeros(ffn_master.shape, jnp.float32), jnp.zeros(small_params.shape, jnp.float32))
    totals, (outputs, seq_grads) = lax.scan(per_item, start, (sequences, cotangents, joint_active))
    block_output = outputs.reshape(IROWS, SUBS, 4, SEG, D).reshape(IROWS, N_CAM, SEG, D)
    input_grad = seq_grads.reshape(IROWS, SUBS, 4, SEG, D).reshape(IROWS, N_CAM, SEG, D)
    new_attn, new_attn_first, new_attn_second, new_attn_average = adam_update(attn_master, totals[0], attn_first, attn_second, attn_average, rate_matrix, decay_matrix)
    new_ffn, new_ffn_first, new_ffn_second, new_ffn_average = adam_update(ffn_master, totals[1], ffn_first, ffn_second, ffn_average, rate_matrix, decay_matrix)
    new_small, new_small_first, new_small_second, new_small_average = adam_update(small_params, totals[2], small_first, small_second, small_average, rate_small, 0.0)
    return (block_output, input_grad, new_attn, new_attn_first, new_attn_second, new_attn_average, new_ffn, new_ffn_first, new_ffn_second, new_ffn_average, new_small, new_small_first, new_small_second, new_small_average)
```

```python
import functools

import jax
import jax.numpy as jnp
from jax import lax
from jax.experimental import pallas as pl
from jax.experimental.pallas import tpu as pltpu
from jax.sharding import PartitionSpec as P

D = 512
HEADS = 8
NJ = 14
ADAM_STEP = 10
HD = 64
PAIR = 2 * HD
PAIRS = HEADS // 2
GROUPS = 2
GROUP_PAIRS = PAIRS // GROUPS
GROUP_COLS = GROUP_PAIRS * PAIR
BLOCKS = 32
ROWS = D // BLOCKS
HALF = BLOCKS // 2
CHUNK = 640

norm_eps = 1e-05
beta_first = 0.5
beta_second = 0.5
adam_eps = 1e-08
rate_matrix = 0.02
rate_small = 0.05
decay_matrix = 0.1
ema_decay = 0.75
log2e = 1.4426950408889634
score_scale = HD**-0.5
F32 = jnp.float32
BF16 = jnp.bfloat16
VMEM_LIMIT = 60 * 2**20


def adam_update(master, grad_total, first_old, second_old, average_old, rate, decay):
    first_new = beta_first * first_old + (1.0 - beta_first) * grad_total
    second_new = beta_second * second_old + (1.0 - beta_second) * grad_total * grad_total
    first_hat = first_new / (1.0 - beta_first**ADAM_STEP)
    second_hat = second_new / (1.0 - beta_second**ADAM_STEP)
    master_new = master - rate * (first_hat / (jnp.sqrt(second_hat) + adam_eps) + decay * master)
    average_new = ema_decay * average_old + (1.0 - ema_decay) * master_new
    return (master_new, first_new, second_new, average_new)


def dot(left, right, left_dim, right_dim):
    return lax.dot_general(
        left, right, (((left_dim,), (right_dim,)), ((), ())), preferred_element_type=F32
    )


def apart(position, order, core):
    outer, inner, depth = position // 8, position // 4 % 2, position % 4
    x_bit, y_bit = (outer, inner) if order == "xy" else (inner, outer)
    return depth * 8 + y_bit * 4 + x_bit * 2 + core


def row_blocks(device, order):
    for core in range(2):
        for position in range(HALF):
            start = (device ^ apart(position, order, core)) * ROWS
            yield core, position, pl.ds(pl.multiple_of(start, ROWS), ROWS)


def put_rows(target, sides, order, device, part=None):
    for core, position, rows in row_blocks(device, order):
        block = sides[core].at[position] if part is None else sides[core].at[position, part]
        target[rows, :] = block[...]


def take_rows(source, sides, order, device):
    for core, position, rows in row_blocks(device, order):
        sides[core][position] = source[rows, :].astype(BF16)


def mean_last(values):
    return jnp.sum(values, axis=-1, keepdims=True) * (1.0 / D)


def normal_rows(values):
    centred = values - mean_last(values)
    inverse = lax.rsqrt(mean_last(centred * centred) + norm_eps)
    return centred * inverse, inverse


def normal_back(normal, inverse, grad):
    return inverse * (grad - mean_last(grad) - normal * mean_last(grad * normal))


def column_sum(values):
    return jnp.sum(values, axis=0, keepdims=True)


def spread_heads(values, other):
    lane = lax.broadcasted_iota(jnp.int32, (1, PAIR), 1)
    low = lane < HD
    return jnp.where(low, values, other), jnp.where(low, other, values)


def attend_kernel(first, seg_len, where, *refs):
    if first:
        pieces, joint, refs = refs[:4], refs[4], refs[5:]
    else:
        rounded, refs = refs[0], refs[1:]
    qk_sides, vo_sides, bias_q, bias_v, refs = refs[:2], refs[2:4], refs[4], refs[5], refs[6:]
    if first:
        rounded, top_rows, refs = refs[0], refs[1], refs[2:]
    q_out, k_out, v_out, a_out, l_out, weight, logs = refs
    device, slot = where[0], where[1]

    if first:

        @pl.when(pl.program_id(0) == 0)
        def _():
            for k in range(4):
                start = pl.multiple_of((slot ^ k) * seg_len, 16)
                rounded[pl.ds(start, seg_len), :] = pieces[k][...]
            top = rounded[:16, :].astype(F32)
            at = lax.broadcasted_iota(jnp.int32, (16, 1), 0)
            top = jnp.where(at == 1, top + joint[...], top)
            top_rows[...] = top[:8]
            rounded[:16, :] = top.astype(BF16)

    put_rows(weight.at[:, :PAIR], qk_sides, "xy", device, 0)
    put_rows(weight.at[:, PAIR : 2 * PAIR], qk_sides, "xy", device, 1)
    put_rows(weight.at[:, 2 * PAIR :], vo_sides, "yx", device, 0)
    projected = dot(rounded[...], weight[...], 1, 0)
    q_out[...] = (projected[:, :PAIR] + bias_q[...]).astype(BF16)
    keys = projected[:, PAIR : 2 * PAIR].astype(BF16)
    values = (projected[:, 2 * PAIR :] + bias_v[...]).astype(BF16)
    k_out[...] = keys
    v_out[...] = values
    lane = lax.broadcasted_iota(jnp.int32, (1, PAIR), 1)
    low = lane < HD
    value_heads = spread_heads(values, jnp.ones_like(values))
    scale = log2e * score_scale
    for step in range(4):
        rows = pl.ds(step * seg_len, seg_len)
        query = q_out[rows, :]
        mixed, tops = [], []
        for query_head, value_head in zip(spread_heads(query, jnp.zeros_like(query)), value_heads):
            scores = dot(query_head, keys, 1, 1)
            top = jnp.max(scores, axis=1, keepdims=True) * scale
            probs = jnp.exp2(scores * scale - top).astype(BF16)
            mixed.append(dot(probs, value_head, 1, 0))
            tops.append(top)
        total = pltpu.roll(jnp.where(low, mixed[1], mixed[0]), HD, 1)
        a_out[rows, :] = (jnp.where(low, mixed[0], mixed[1]) / total).astype(BF16)
        logs[rows, :] = jnp.where(low, tops[0], tops[1]) + jnp.log2(total)
    turned = logs[...].T
    l_out[0:1, :] = turned[0:1]
    l_out[1:2, :] = turned[HD : HD + 1]


def gate_both(values):
    size = jnp.abs(values)
    fraction = 1.0 / (1.0 + (0.3275911 * 0.5**0.5) * size)
    bell = jnp.exp2(values * values * (-0.5 * log2e))
    series = 0.5 * 1.061405429 * fraction - 0.5 * 1.453152027
    series = series * fraction + 0.5 * 1.421413741
    series = series * fraction - 0.5 * 0.284496736
    series = series * fraction + 0.5 * 0.254829592
    tail = series * fraction * bell
    below = jnp.where(values > 0.0, 1.0 - tail, tail)
    return values * below, below + values * bell * 0.3989422804014327


def forward_kernel(seg_len, where, *refs):
    rounded, top_rows, refs = refs[0], refs[1], refs[2:]
    mixed, refs = refs[:GROUPS], refs[GROUPS:]
    vo_sides, up_sides, down_sides, refs = refs[:2], refs[2:4], refs[4:6], refs[6:]
    vectors, hidden_bias, cotangents, refs = refs[0], refs[1], refs[2:6], refs[6:]
    h1_out, y1_out, g_out, slope_out, pieces, refs = refs[0], refs[1], refs[2], refs[3], refs[4:8], refs[8:]
    dh2_out, vector_grads, normed, total, w_out, w_up, w_down = refs
    device, slot = where[0], where[1]
    seq_len = 4 * seg_len
    out_scale = (seq_len / 3.0) ** 0.5
    chunk = pl.program_id(0)

    @pl.when(chunk == 0)
    def _():
        put_rows(w_out, vo_sides, "yx", device, 1)
        for step in range(4):
            rows = pl.ds(step * seg_len, seg_len)
            summed = rounded[rows, :].astype(F32)
            if step == 0:
                summed = jnp.concatenate([top_rows[...], summed[8:]], axis=0)
            branch = sum(
                dot(mixed[g][rows, :], w_out[g * GROUP_COLS : (g + 1) * GROUP_COLS, :], 1, 0)
                for g in range(GROUPS)
            )
            summed = summed + (branch * out_scale + vectors[2:3, :])
            h1_out[rows, :] = summed
            normal, _ = normal_rows(summed)
            result = normal * vectors[3:4, :] + vectors[4:5, :]
            normed[rows, :] = result
            y1_out[rows, :] = result.astype(BF16)
        total[...] = jnp.zeros_like(total)

    put_rows(w_up, up_sides, "xy", device)
    put_rows(w_down, down_sides, "yx", device)
    for step in range(4):
        rows = pl.ds(step * seg_len, seg_len)
        inner = dot(y1_out[rows, :], w_up[...], 1, 0) + hidden_bias[...]
        active, slope = gate_both(inner)
        active = active.astype(BF16)
        g_out[rows, :] = active
        slope_out[rows, :] = slope.astype(BF16)
        total[rows, :] += dot(active, w_down[...], 1, 1)

    @pl.when(chunk == pl.num_programs(0) - 1)
    def _():
        gain_grad = shift_grad = bias_grad = 0.0
        for k in range(4):
            rows = pl.ds(pl.multiple_of((slot ^ k) * seg_len, 16), seg_len)
            normal, inverse = normal_rows(normed[rows, :] + (total[rows, :] + vectors[5:6, :]))
            pieces[k][...] = (normal * vectors[6:7, :] + vectors[7:8, :]).astype(BF16)
            cotangent = cotangents[k][...].astype(F32)
            gain_grad += column_sum(cotangent * normal)
            shift_grad += column_sum(cotangent)
            middle = normal_back(normal, inverse, cotangent * vectors[6:7, :])
            dh2_out[rows, :] = middle
            bias_grad += column_sum(middle.astype(BF16).astype(F32))
        vector_grads[0:1, :] = gain_grad
        vector_grads[1:2, :] = shift_grad
        vector_grads[2:3, :] = bias_grad


def backward_kernel(seg_len, where, *refs):
    dh2, h1, y1, active, slope, refs = refs[0], refs[1], refs[2], refs[3], refs[4], refs[5:]
    mixed, refs = refs[:GROUPS], refs[GROUPS:]
    vo_sides, up_sides, down_sides, vectors, refs = refs[:2], refs[2:4], refs[4:6], refs[6], refs[7:]
    up_grads, down_grads, out_grads, refs = refs[:2], refs[2:4], refs[4:6], refs[6:]
    hidden_grad, dh1_out, da_out, vector_grads, refs = refs[0], refs[1], refs[2], refs[3], refs[4:]
    y1_turned, df_turned, df, dz, total, w_out, w_up, w_down, grad = refs
    device = where[0]
    seq_len = 4 * seg_len
    out_scale = (seq_len / 3.0) ** 0.5
    chunk = pl.program_id(0)

    @pl.when(chunk == 0)
    def _():
        rounded = dh2[...].astype(BF16)
        df[...] = rounded
        df_turned[...] = rounded.T
        y1_turned[...] = y1[...].T
        total[...] = dh2[...]

    put_rows(w_up, up_sides, "xy", device)
    put_rows(w_down, down_sides, "yx", device)
    bias_grad = 0.0
    for step in range(4):
        rows = pl.ds(step * seg_len, seg_len)
        inner = (dot(df[rows, :], w_down[...], 1, 0) * slope[rows, :].astype(F32)).astype(BF16)
        dz[rows, :] = inner
        bias_grad += column_sum(inner.astype(F32))
        total[rows, :] += dot(inner, w_up[...], 1, 1)
    hidden_grad[...] = bias_grad
    grad[...] = dot(df_turned[...], active[...], 1, 0)
    take_rows(grad, down_grads, "yx", device)
    grad[...] = dot(y1_turned[...], dz[...], 1, 0)
    take_rows(grad, up_grads, "xy", device)

    @pl.when(chunk == pl.num_programs(0) - 1)
    def _():
        put_rows(w_out, vo_sides, "yx", device, 1)
        gain_grad = shift_grad = bias_grad = 0.0
        for step in range(4):
            rows = pl.ds(step * seg_len, seg_len)
            normal, inverse = normal_rows(h1[rows, :])
            above = total[rows, :]
            gain_grad += column_sum(above * normal)
            shift_grad += column_sum(above)
            summed = normal_back(normal, inverse, above * vectors[3:4, :])
            dh1_out[rows, :] = summed
            rounded = summed.astype(BF16)
            df[rows, :] = rounded
            bias_grad += column_sum(rounded.astype(F32))
            da_out[rows, :] = (dot(rounded, w_out[...], 1, 1) * out_scale).astype(BF16)
        vector_grads[0:1, :] = gain_grad
        vector_grads[1:2, :] = shift_grad
        vector_grads[2:3, :] = bias_grad
        for g in range(GROUPS):
            cols = pl.ds(g * GROUP_COLS, GROUP_COLS)
            grad[cols, :D] = dot(mixed[g][...], df[...], 0, 0) * out_scale
        take_rows(grad.at[:, :D], out_grads, "yx", device)


def attend_back_kernel(last, seg_len, where, *refs):
    q, k, v, a, da, logs, rounded, before, refs = *refs[:8], refs[8:]
    qk_sides, vo_sides, refs = refs[:2], refs[2:4], refs[4:]
    sides, refs = refs[: 2 * GROUP_PAIRS], refs[2 * GROUP_PAIRS :]
    bias_grads, refs = refs[0], refs[1:]
    if last:
        own, sends, top_rows, total, refs = refs[0], refs[1:4], refs[4], refs[5], refs[6:]
    else:
        total, refs = refs[0], refs[1:]
    turned, weight, parts, query_turned, grad = refs
    device, slot = where[0], where[1]
    seq_len = 4 * seg_len
    pair = pl.program_id(0)

    @pl.when(pair == 0)
    def _():
        turned[...] = rounded[...].T
        total[...] = before[...]

    put_rows(weight.at[:, :PAIR], qk_sides, "xy", device, 0)
    put_rows(weight.at[:, PAIR : 2 * PAIR], qk_sides, "xy", device, 1)
    put_rows(weight.at[:, 2 * PAIR :], vo_sides, "yx", device, 0)

    queries, mixed_grads = q[...], da[...]
    zeros = jnp.zeros_like(queries)
    query_heads = spread_heads(queries, zeros)
    grad_heads = spread_heads(mixed_grads, zeros)
    product = (mixed_grads.astype(F32) * a[...].astype(F32)).T
    inner = (column_sum(product[:HD]), column_sum(product[HD:]))
    start = 0
    while start < seq_len:
        size = min(256, seq_len - start)
        rows = pl.ds(start, size)
        none = jnp.zeros((size, PAIR), BF16)
        key_grad = value_grad = query_grad = 0.0
        heads = zip(spread_heads(k[rows, :], none), spread_heads(v[rows, :], none))
        for h, (key_head, value_head) in enumerate(heads):
            scores = dot(key_head, queries, 1, 1)
            probs = jnp.exp2(scores * (log2e * score_scale) - logs[h : h + 1, :])
            grads = (probs * (dot(value_head, mixed_grads, 1, 1) - inner[h])).astype(BF16)
            value_grad += dot(probs.astype(BF16), grad_heads[h], 1, 0)
            key_grad += dot(grads, query_heads[h], 1, 0)
            query_grad += dot(key_head, grads, 0, 0)
        parts[rows, PAIR : 2 * PAIR] = (key_grad * score_scale).astype(BF16)
        parts[rows, 2 * PAIR :] = value_grad.astype(BF16)
        if start == 0:
            query_turned[...] = query_grad
        else:
            query_turned[...] += query_grad
        start += size
    parts[:, :PAIR] = (query_turned[...].T * score_scale).astype(BF16)
    bias_grads[0:1, :] = column_sum(parts[:, :PAIR].astype(F32))
    bias_grads[1:2, :] = column_sum(parts[:, 2 * PAIR :].astype(F32))
    total[...] += dot(parts[...], weight[...], 1, 1)
    grad[...] = dot(turned[...], parts[...], 1, 0)
    for n in range(GROUP_PAIRS):

        @pl.when(pair == n)
        def _(n=n):
            take_rows(grad, sides[2 * n : 2 * n + 2], pair_order(n), device)

    if last:

        @pl.when(pair == pl.num_programs(0) - 1)
        def _():
            top_rows[...] = total[:8, :]
            for n in range(4):
                piece = total[pl.ds(pl.multiple_of((slot ^ n) * seg_len, 16), seg_len), :]
                if n == 0:
                    own[...] = piece
                else:
                    sends[n - 1][...] = piece.astype(BF16)


def pair_order(pair):
    return "yx" if pair % 2 else "xy"


def call(kernel, name, where, grid, operands, results, scratch, flops, exps=0):
    def spec(block, index):
        return pl.BlockSpec(block, lambda i, _: index(i))

    moved = sum(x.size * x.dtype.itemsize for x, _, _ in (*operands, *results))
    return pl.pallas_call(
        kernel,
        grid_spec=pltpu.PrefetchScalarGridSpec(
            num_scalar_prefetch=1,
            grid=(grid,),
            in_specs=[spec(block, index) for _, block, index in operands],
            out_specs=[spec(block, index) for _, block, index in results],
            scratch_shapes=[pltpu.VMEM(shape, kind) for shape, kind in scratch],
        ),
        out_shape=[shape for shape, _, _ in results],
        compiler_params=pltpu.CompilerParams(vmem_limit_bytes=VMEM_LIMIT),
        cost_estimate=pl.CostEstimate(flops=flops, bytes_accessed=moved, transcendentals=exps),
        name=name,
    )(where, *(x for x, _, _ in operands))


def whole(x):
    return (x, x.shape, lambda i: (0,) * len(x.shape))


def shape_of(shape, kind):
    return jax.ShapeDtypeStruct(shape, kind)


def whole_out(shape, kind):
    return whole(shape_of(shape, kind))


def attend(group, where, source, sides, vectors, seg_len):
    seq_len = 4 * seg_len
    first = group == 0
    base = group * GROUP_PAIRS

    def at(i):
        return (0, i + base)

    operands = [whole(x) for x in source]
    operands += [(x, (HALF, 2, ROWS, PAIR), lambda i: (0, 0, 0, i + base)) for x in sides]
    operands += [(vectors[n : n + 1], (1, PAIR), at) for n in range(2)]
    results = []
    if first:
        results += [whole_out((seq_len, D), BF16), whole_out((8, D), F32)]
    columns = (shape_of((seq_len, GROUP_COLS), BF16), (seq_len, PAIR), lambda i: (0, i))
    results += [columns] * 4
    results += [(shape_of((GROUP_PAIRS, 2, seq_len), F32), (None, 2, seq_len), lambda i: (i, 0, 0))]
    scratch = [((D, 3 * PAIR), BF16), ((seq_len, PAIR), F32)]
    scores = seq_len * seq_len * 2 * GROUP_PAIRS
    return call(
        functools.partial(attend_kernel, first, seg_len),
        f"attend_{group}",
        where,
        GROUP_PAIRS,
        operands,
        results,
        scratch,
        scores * 16 * HD,
        scores,
    )


def feed_forward(where, rounded, top_rows, mixed, vo, up, down, vectors, hidden_bias, cotangents):
    seq_len = rounded.shape[0]
    seg_len = seq_len // 4
    hidden = up[0].shape[-1]
    operands = [whole(x) for x in (rounded, top_rows, *mixed, *vo)]
    operands += [(x, (HALF, ROWS, CHUNK), lambda i: (0, 0, i)) for x in (*up, *down)]
    operands += [whole(vectors), (hidden_bias, (1, CHUNK), lambda i: (0, i))]
    operands += [whole(x) for x in cotangents]
    wide = (shape_of((seq_len, hidden), BF16), (seq_len, CHUNK), lambda i: (0, i))
    results = [whole_out((seq_len, D), F32), whole_out((seq_len, D), BF16), wide, wide]
    results += [whole_out((seg_len, D), BF16)] * 4
    results += [whole_out((seq_len, D), F32), whole_out((8, D), F32)]
    scratch = [((seq_len, D), F32), ((seq_len, D), F32), ((D, D), BF16)]
    scratch += [((D, CHUNK), BF16)] * 2
    return call(
        functools.partial(forward_kernel, seg_len),
        "feed_forward",
        where,
        hidden // CHUNK,
        operands,
        results,
        scratch,
        seq_len * D * (D + 2 * hidden) * 2,
        2 * seq_len * hidden,
    )


def feed_back(where, dh2, h1, y1, active, slope, mixed, vo, up, down, vectors):
    seq_len = dh2.shape[0]
    seg_len = seq_len // 4
    hidden = up[0].shape[-1]
    operands = [whole(x) for x in (dh2, h1, y1)]
    operands += [(x, (seq_len, CHUNK), lambda i: (0, i)) for x in (active, slope)]
    operands += [whole(x) for x in (*mixed, *vo)]
    operands += [(x, (HALF, ROWS, CHUNK), lambda i: (0, 0, i)) for x in (*up, *down)]
    operands += [whole(vectors)]
    wide = (shape_of((HALF, ROWS, hidden), BF16), (HALF, ROWS, CHUNK), lambda i: (0, 0, i))
    results = [wide] * 4 + [whole_out((HALF, ROWS, D), BF16)] * 2
    results += [(shape_of((1, hidden), F32), (1, CHUNK), lambda i: (0, i))]
    results += [whole_out((seq_len, D), F32), whole_out((seq_len, D), BF16), whole_out((8, D), F32)]
    scratch = [((D, seq_len), BF16)] * 2 + [((seq_len, D), BF16), ((seq_len, CHUNK), BF16)]
    scratch += [((seq_len, D), F32), ((D, D), BF16)] + [((D, CHUNK), BF16)] * 2 + [((D, CHUNK), F32)]
    return call(
        functools.partial(backward_kernel, seg_len),
        "feed_back",
        where,
        hidden // CHUNK,
        operands,
        results,
        scratch,
        seq_len * D * (2 * D + 4 * hidden) * 2,
    )


def attend_back(group, where, heads, da, logs, rounded, before, sides, seg_len):
    seq_len = 4 * seg_len
    last = group == GROUPS - 1
    base = group * GROUP_PAIRS
    operands = [(x, (seq_len, PAIR), lambda i: (0, i)) for x in heads]
    operands += [(da, (seq_len, PAIR), lambda i: (0, i + base))]
    operands += [(logs, (None, 2, seq_len), lambda i: (i, 0, 0)), whole(rounded), whole(before)]
    operands += [(x, (HALF, 2, ROWS, PAIR), lambda i: (0, 0, 0, i + base)) for x in sides]
    results = [whole_out((HALF, ROWS, 3 * PAIR), BF16)] * (2 * GROUP_PAIRS)
    results += [(shape_of((8, GROUP_COLS), F32), (8, PAIR), lambda i: (0, i))]
    scratch = []
    if last:
        results += [whole_out((seg_len, D), F32)] + [whole_out((seg_len, D), BF16)] * 3
        results += [whole_out((8, D), F32)]
        scratch += [((seq_len, D), F32)]
    else:
        results += [whole_out((seq_len, D), F32)]
    scratch += [((D, seq_len), BF16), ((D, 3 * PAIR), BF16), ((seq_len, 3 * PAIR), BF16)]
    scratch += [((PAIR, seq_len), F32), ((D, 3 * PAIR), F32)]
    scores = seq_len * seq_len * 2 * GROUP_PAIRS
    return call(
        functools.partial(attend_back_kernel, last, seg_len),
        f"attend_back_{group}",
        where,
        GROUP_PAIRS,
        operands,
        results,
        scratch,
        scores * 40 * HD,
        scores,
    )


def partner(value, axis, mask):
    pairs = [(source, source ^ mask) for source in range(lax.axis_size(axis))]
    return lax.ppermute(value, axis, pairs)


def over_core(value):
    return partner(value, "cam", 1)


def over_x(value):
    return partner(value, "cam", 2)


def over_y(value):
    return partner(value, "dp", 1)


def over_z(value, apart_by):
    return partner(value, "dp", 2 * apart_by)


def stages_of(order):
    return (over_x, over_y) if order == "xy" else (over_y, over_x)


def by_blocks():
    return lax.axis_size("dp") * lax.axis_size("cam") == BLOCKS


def gather(shard, order):
    outer, inner = stages_of(order)
    if by_blocks():
        held = jnp.stack([shard] + [over_z(shard, n) for n in range(1, 4)])
        held = jnp.concatenate([held, inner(held)])
        held = jnp.concatenate([held, outer(held)])
        return held, over_core(held)
    full = lax.all_gather(shard, ("dp", "cam"), axis=shard.ndim - 2, tiled=True)
    full = full.reshape(*full.shape[:-2], 4, 2, 2, 2, ROWS, full.shape[-1])
    at = shard.ndim - 2
    x_at, y_at = at + 2, at + 1
    front = (at + 3, x_at, y_at, at) if order == "xy" else (at + 3, y_at, x_at, at)
    full = jnp.moveaxis(full, front, (0, 1, 2, 3))
    full = full.reshape(2, HALF, *full.shape[4:])
    return full[0], full[1]


def scatter(sides, order):
    outer, inner = stages_of(order)
    keep, send = sides
    if by_blocks():
        held = keep.astype(F32) + over_core(send).astype(F32)
        for stage in (outer, inner):
            half = held.shape[0] // 2
            held = held[:half] + stage(held[half:].astype(BF16)).astype(F32)
        sends = [over_z(held[n].astype(BF16), n).astype(F32) for n in range(1, 4)]
        return (held[0] + sends[0]) + (sends[1] + sends[2])
    full = jnp.stack([keep, send]).reshape(2, 2, 2, 4, ROWS, keep.shape[-1])
    places = (3, 2, 1, 0) if order == "xy" else (3, 1, 2, 0)
    full = jnp.moveaxis(full, (0, 1, 2, 3), places).reshape(D, keep.shape[-1])
    return lax.psum_scatter(full.astype(F32), ("dp", "cam"), scatter_dimension=0, tiled=True)


def total_of(vector):
    if by_blocks():
        for stage in (over_core, over_x, over_y):
            vector = vector + stage(vector)
        others = [over_z(vector, n) for n in range(1, 4)]
        return (vector + others[0]) + (others[1] + others[2])
    return lax.psum(vector, ("dp", "cam"))


def local(
    tokens,
    out_grad,
    joint_state,
    joint_mask,
    attn_master,
    attn_first,
    attn_second,
    attn_average,
    ffn_master,
    ffn_first,
    ffn_second,
    ffn_average,
    small_params,
    small_first,
    small_second,
    small_average,
):
    cam_index = lax.axis_index("cam")
    slot, group_index = cam_index % 4, cam_index // 4
    items_here, _, seg_len, _ = tokens.shape
    assert items_here == 4
    device = lax.axis_index("dp") * lax.axis_size("cam") + cam_index if by_blocks() else 0
    where = jnp.stack([jnp.int32(device), jnp.int32(slot)])

    def piece_for(array, n):
        return lax.dynamic_index_in_dim(array, slot ^ n, 0, keepdims=False)

    def trade(pieces):
        return [pieces[0]] + [partner(pieces[n], "cam", n) for n in range(1, 4)]

    def arrange(pieces):
        full = jnp.stack(pieces)
        return jnp.stack([lax.dynamic_index_in_dim(full, slot ^ n, 0, keepdims=False) for n in range(4)])

    sequence = trade([piece_for(tokens[:, 0], n) for n in range(4)])
    attn_low = attn_master.astype(BF16)
    ffn_low = ffn_master.astype(BF16)
    query_key = gather(attn_low[:2], "xy")
    value_out = gather(attn_low[2:], "yx")
    sides = (*query_key, *value_out)
    up = gather(ffn_low[0], "xy")
    down = gather(ffn_low[1], "yx")
    cotangents = trade([piece_for(out_grad[:, 0], n) for n in range(4)])

    vectors = small_params[: 8 * D].reshape(8, D)
    joint_rows = small_params[8 * D : (8 + NJ) * D].reshape(NJ, D)
    hidden_bias = small_params[(8 + NJ) * D :].reshape(1, -1)
    active = (joint_state * joint_mask.astype(F32))[slot, group_index]
    joint = jnp.sum(active[:, None] * joint_rows, axis=0, keepdims=True)

    rounded, top_rows, *heads = attend(0, where, [*sequence, joint], sides, vectors, seg_len)
    heads = [heads]
    for group in range(1, GROUPS):
        heads.append(attend(group, where, [rounded], sides, vectors, seg_len))
    mixed = [x[3] for x in heads]
    h1, y1, gated, slope, *rest = feed_forward(
        where, rounded, top_rows, mixed, value_out, up, down, vectors, hidden_bias, cotangents
    )
    out_pieces, dh2, grads_two = rest[:4], rest[4], rest[5]
    *weight_grads, hidden_grad, dh1, da, grads_one = feed_back(
        where, dh2, h1, y1, gated, slope, mixed, value_out, up, down, vectors
    )
    block_output = arrange(trade(out_pieces)).reshape(tokens.shape)
    up_grad = scatter(weight_grads[0:2], "xy")
    down_grad = scatter(weight_grads[2:4], "yx")
    out_proj_grad = scatter(weight_grads[4:6], "yx")

    before, pair_grads, bias_grads = dh1, [], []
    for group in range(GROUPS):
        results = attend_back(
            group, where, heads[group][:4], da, heads[group][4], rounded, before, sides, seg_len
        )
        pair_sides, rest = results[: 2 * GROUP_PAIRS], results[2 * GROUP_PAIRS :]
        bias_grad, before, rest = rest[0], rest[1], rest[2:]
        bias_grads.append(bias_grad)
        for n in range(GROUP_PAIRS):
            pair_grads.append(scatter(pair_sides[2 * n : 2 * n + 2], pair_order(n)))
    *sends, item_top = rest
    grad_pieces = [x.astype(F32) for x in trade([before, *sends])[1:]]
    input_grad = arrange([before, *grad_pieces]).reshape(tokens.shape)

    bias_grads = jnp.concatenate(bias_grads, axis=1)
    small_grad = jnp.concatenate(
        [
            bias_grads[0],
            bias_grads[1],
            grads_one[2],
            grads_one[0],
            grads_one[1],
            grads_two[2],
            grads_two[0],
            grads_two[1],
            (active[:, None] * item_top[1:2]).reshape(-1),
            hidden_grad[0],
        ]
    )
    small_total = total_of(small_grad)
    rows_here = attn_master.shape[1]
    proj_grad = jnp.stack(pair_grads, axis=1).reshape(rows_here, PAIRS, 3, PAIR)
    proj_grad = jnp.moveaxis(proj_grad, 2, 0).reshape(3, rows_here, D)
    attn_shard = jnp.concatenate([proj_grad, out_proj_grad[None]])
    ffn_shard = jnp.stack([up_grad, down_grad])
    new_attn = adam_update(
        attn_master, attn_shard, attn_first, attn_second, attn_average, rate_matrix, decay_matrix
    )
    new_ffn = adam_update(
        ffn_master, ffn_shard, ffn_first, ffn_second, ffn_average, rate_matrix, decay_matrix
    )
    new_small = adam_update(
        small_params, small_total, small_first, small_second, small_average, rate_small, 0.0
    )
    return (block_output, input_grad, *new_attn, *new_ffn, *new_small)


def solution(mesh):
    in_specs = (
        P("dp", "cam", None, None),
        P("dp", "cam", None, None),
        P("dp", None, None),
        P("dp", None, None),
        P(None, ("dp", "cam"), None),
        P(None, ("dp", "cam"), None),
        P(None, ("dp", "cam"), None),
        P(None, ("dp", "cam"), None),
        P(None, ("dp", "cam"), None),
        P(None, ("dp", "cam"), None),
        P(None, ("dp", "cam"), None),
        P(None, ("dp", "cam"), None),
        P(),
        P(),
        P(),
        P(),
    )
    out_specs = (
        P("dp", "cam", None, None),
        P("dp", "cam", None, None),
        P(None, ("dp", "cam"), None),
        P(None, ("dp", "cam"), None),
        P(None, ("dp", "cam"), None),
        P(None, ("dp", "cam"), None),
        P(None, ("dp", "cam"), None),
        P(None, ("dp", "cam"), None),
        P(None, ("dp", "cam"), None),
        P(None, ("dp", "cam"), None),
        P(),
        P(),
        P(),
        P(),
    )
    return jax.shard_map(local, mesh=mesh, in_specs=in_specs, out_specs=out_specs, check_vma=False)
```

```python
import functools

import jax
import jax.numpy as jnp
from jax import lax
from jax.experimental import pallas as pl
from jax.experimental.pallas import tpu as pltpu
from jax.sharding import PartitionSpec as P

D = 512
HEADS = 8
NJ = 14
ADAM_STEP = 10
HD = 64
PAIR = 2 * HD
PAIRS = HEADS // 2
GROUPS = 2
GROUP_PAIRS = PAIRS // GROUPS
GROUP_COLS = GROUP_PAIRS * PAIR
BLOCKS = 32
ROWS = D // BLOCKS
HALF = BLOCKS // 2
CHUNK = 640
OUT_COLS = D // GROUPS
SIDE_COLS = 3 * GROUP_COLS + OUT_COLS
ORDERS = ("xy", "yx")

norm_eps = 1e-05
beta_first = 0.5
beta_second = 0.5
adam_eps = 1e-08
rate_matrix = 0.02
rate_small = 0.05
decay_matrix = 0.1
ema_decay = 0.75
log2e = 1.4426950408889634
score_scale = HD**-0.5
F32 = jnp.float32
BF16 = jnp.bfloat16
VMEM_LIMIT = 60 * 2**20


def adam_update(master, grad_total, first_old, second_old, average_old, rate, decay):
    first_new = beta_first * first_old + (1.0 - beta_first) * grad_total
    second_new = beta_second * second_old + (1.0 - beta_second) * grad_total * grad_total
    first_hat = first_new / (1.0 - beta_first**ADAM_STEP)
    second_hat = second_new / (1.0 - beta_second**ADAM_STEP)
    master_new = master - rate * (first_hat / (jnp.sqrt(second_hat) + adam_eps) + decay * master)
    average_new = ema_decay * average_old + (1.0 - ema_decay) * master_new
    return (master_new, first_new, second_new, average_new)


def dot(left, right, left_dim, right_dim):
    return lax.dot_general(
        left, right, (((left_dim,), (right_dim,)), ((), ())), preferred_element_type=F32
    )


def apart(position, order, core):
    outer, inner, low_z, high_z = (position >> bit & 1 for bit in (3, 2, 1, 0))
    x_bit, y_bit = (outer, inner) if order == "xy" else (inner, outer)
    return high_z * 16 + low_z * 8 + y_bit * 4 + x_bit * 2 + core


def row_blocks(device, order):
    for core in range(2):
        for position in range(HALF):
            start = (device ^ apart(position, order, core)) * ROWS
            yield core, position, pl.ds(pl.multiple_of(start, ROWS), ROWS)


def put_rows(target, sides, order, device, part=None):
    for core, position, rows in row_blocks(device, order):
        block = sides[core].at[position] if part is None else sides[core].at[position, part]
        target[rows, :] = block[...]


def take_rows(source, sides, order, device):
    for core, position, rows in row_blocks(device, order):
        sides[core][position] = source[rows, :].astype(BF16)


def mean_last(values):
    return jnp.sum(values, axis=-1, keepdims=True) * (1.0 / D)


def normal_rows(values):
    centred = values - mean_last(values)
    inverse = lax.rsqrt(mean_last(centred * centred) + norm_eps)
    return centred * inverse, inverse


def normal_back(normal, inverse, grad):
    return inverse * (grad - mean_last(grad) - normal * mean_last(grad * normal))


def column_sum(values):
    return jnp.sum(values, axis=0, keepdims=True)


def spread_heads(values, other):
    lane = lax.broadcasted_iota(jnp.int32, (1, PAIR), 1)
    low = lane < HD
    return jnp.where(low, values, other), jnp.where(low, other, values)


def attend_kernel(first, seg_len, where, *refs):
    if first:
        pieces, joint, refs = refs[:4], refs[4], refs[5:]
    else:
        rounded, refs = refs[0], refs[1:]
    sides, bias_q, bias_v, refs = refs[:2], refs[2], refs[3], refs[4:]
    if first:
        rounded, top_rows, refs = refs[0], refs[1], refs[2:]
    q_out, k_out, v_out, a_out, l_out, weight, logs = refs
    device, slot = where[0], where[1]

    if first:

        @pl.when(pl.program_id(0) == 0)
        def _():
            for k in range(4):
                start = pl.multiple_of((slot ^ k) * seg_len, 16)
                rounded[pl.ds(start, seg_len), :] = pieces[k][...]
            top = rounded[:16, :].astype(F32)
            at = lax.broadcasted_iota(jnp.int32, (16, 1), 0)
            top = jnp.where(at == 1, top + joint[...], top)
            top_rows[...] = top[:8]
            rounded[:16, :] = top.astype(BF16)

    for part in range(3):
        put_rows(weight.at[:, part * PAIR : (part + 1) * PAIR], sides, "xy", device, part)
    projected = dot(rounded[...], weight[...], 1, 0)
    q_out[...] = (projected[:, :PAIR] + bias_q[...]).astype(BF16)
    keys = projected[:, PAIR : 2 * PAIR].astype(BF16)
    values = (projected[:, 2 * PAIR :] + bias_v[...]).astype(BF16)
    k_out[...] = keys
    v_out[...] = values
    lane = lax.broadcasted_iota(jnp.int32, (1, PAIR), 1)
    low = lane < HD
    value_heads = spread_heads(values, jnp.ones_like(values))
    scale = log2e * score_scale
    for step in range(4):
        rows = pl.ds(step * seg_len, seg_len)
        query = q_out[rows, :]
        mixed, tops = [], []
        for query_head, value_head in zip(spread_heads(query, jnp.zeros_like(query)), value_heads):
            scores = dot(query_head, keys, 1, 1)
            top = jnp.max(scores, axis=1, keepdims=True) * scale
            probs = jnp.exp2(scores * scale - top).astype(BF16)
            mixed.append(dot(probs, value_head, 1, 0))
            tops.append(top)
        total = pltpu.roll(jnp.where(low, mixed[1], mixed[0]), HD, 1)
        a_out[rows, :] = (jnp.where(low, mixed[0], mixed[1]) / total).astype(BF16)
        logs[rows, :] = jnp.where(low, tops[0], tops[1]) + jnp.log2(total)
    turned = logs[...].T
    l_out[0:1, :] = turned[0:1]
    l_out[1:2, :] = turned[HD : HD + 1]


def gate_both(values):
    size = jnp.abs(values)
    fraction = 1.0 / (1.0 + (0.3275911 * 0.5**0.5) * size)
    bell = jnp.exp2(values * values * (-0.5 * log2e))
    series = 0.5 * 1.061405429 * fraction - 0.5 * 1.453152027
    series = series * fraction + 0.5 * 1.421413741
    series = series * fraction - 0.5 * 0.284496736
    series = series * fraction + 0.5 * 0.254829592
    tail = series * fraction * bell
    below = jnp.where(values > 0.0, 1.0 - tail, tail)
    return values * below, below + values * bell * 0.3989422804014327


def project_kernel(seg_len, where, *refs):
    rounded, top_rows, mixed, refs = refs[0], refs[1], refs[2 : 2 + GROUPS], refs[2 + GROUPS :]
    out_sides, vectors, h1_out, normed_out, y1_out, w_out = refs[:2], *refs[2:]
    out_scale = (4 * seg_len / 3.0) ** 0.5
    put_rows(w_out, out_sides, "xy", where[0], 0)
    for step in range(4):
        rows = pl.ds(step * seg_len, seg_len)
        summed = rounded[rows, :].astype(F32)
        if step == 0:
            summed = jnp.concatenate([top_rows[...], summed[8:]], axis=0)
        branch = sum(
            dot(mixed[g][rows, :], w_out[g * GROUP_COLS : (g + 1) * GROUP_COLS, :], 1, 0)
            for g in range(GROUPS)
        )
        summed = summed + (branch * out_scale + vectors[2:3, :])
        h1_out[rows, :] = summed
        normal, _ = normal_rows(summed)
        result = normal * vectors[3:4, :] + vectors[4:5, :]
        normed_out[rows, :] = result
        y1_out[rows, :] = result.astype(BF16)


def forward_kernel(seg_len, where, *refs):
    y1, up_sides, down_sides, hidden_bias, refs = refs[0], refs[1:3], refs[3:5], refs[5], refs[6:]
    g_out, slope_out, total, w_up, w_down = refs
    device = where[0]

    @pl.when(pl.program_id(0) == 0)
    def _():
        total[...] = jnp.zeros_like(total)

    put_rows(w_up, up_sides, "xy", device)
    put_rows(w_down, down_sides, "yx", device)
    for step in range(4):
        rows = pl.ds(step * seg_len, seg_len)
        inner = dot(y1[rows, :], w_up[...], 1, 0) + hidden_bias[...]
        active, slope = gate_both(inner)
        active = active.astype(BF16)
        g_out[rows, :] = active
        slope_out[rows, :] = slope.astype(BF16)
        total[rows, :] += dot(active, w_down[...], 1, 1)


def second_kernel(seg_len, where, *refs):
    normed, forward, active, vectors, cotangents, refs = *refs[:4], refs[4:8], refs[8:]
    pieces, dh2_out, df_out, vector_grads, refs = refs[:4], refs[4], refs[5], refs[6], refs[7:]
    down_grads, df_turned, grad = refs[:2], refs[2], refs[3]
    device, slot = where[0], where[1]

    @pl.when(pl.program_id(0) == 0)
    def _():
        gain_grad = shift_grad = bias_grad = 0.0
        for k in range(4):
            rows = pl.ds(pl.multiple_of((slot ^ k) * seg_len, 16), seg_len)
            normal, inverse = normal_rows(normed[rows, :] + (forward[rows, :] + vectors[5:6, :]))
            pieces[k][...] = (normal * vectors[6:7, :] + vectors[7:8, :]).astype(BF16)
            cotangent = cotangents[k][...].astype(F32)
            gain_grad += column_sum(cotangent * normal)
            shift_grad += column_sum(cotangent)
            middle = normal_back(normal, inverse, cotangent * vectors[6:7, :])
            dh2_out[rows, :] = middle
            rounded = middle.astype(BF16)
            df_out[rows, :] = rounded
            bias_grad += column_sum(rounded.astype(F32))
        vector_grads[0:1, :] = gain_grad
        vector_grads[1:2, :] = shift_grad
        vector_grads[2:3, :] = bias_grad
        df_turned[...] = df_out[...].T

    grad[...] = dot(df_turned[...], active[...], 1, 0)
    take_rows(grad, down_grads, "yx", device)


def backward_kernel(seg_len, where, *refs):
    dh2, df, y1, slope, up_sides, down_sides, refs = *refs[:4], refs[4:6], refs[6:8], refs[8:]
    up_grads, hidden_grad, total, refs = refs[:2], refs[2], refs[3], refs[4:]
    y1_turned, dz, w_up, w_down, grad = refs
    device = where[0]

    @pl.when(pl.program_id(0) == 0)
    def _():
        y1_turned[...] = y1[...].T
        total[...] = dh2[...]

    put_rows(w_up, up_sides, "xy", device)
    put_rows(w_down, down_sides, "yx", device)
    bias_grad = 0.0
    for step in range(4):
        rows = pl.ds(step * seg_len, seg_len)
        inner = (dot(df[rows, :], w_down[...], 1, 0) * slope[rows, :].astype(F32)).astype(BF16)
        dz[rows, :] = inner
        bias_grad += column_sum(inner.astype(F32))
        total[rows, :] += dot(inner, w_up[...], 1, 1)
    hidden_grad[...] = bias_grad
    grad[...] = dot(y1_turned[...], dz[...], 1, 0)
    take_rows(grad, up_grads, "xy", device)


def first_kernel(seg_len, where, *refs):
    above_in, h1, mixed, refs = refs[0], refs[1], refs[2 : 2 + GROUPS], refs[2 + GROUPS :]
    out_sides, vectors, dh1_out, da_out, vector_grads, refs = refs[:2], *refs[2:6], refs[6:]
    sides, do, w_out, grad = refs[: 2 * GROUPS], *refs[2 * GROUPS :]
    device = where[0]
    out_scale = (4 * seg_len / 3.0) ** 0.5
    put_rows(w_out, out_sides, "xy", device, 0)
    gain_grad = shift_grad = bias_grad = 0.0
    for step in range(4):
        rows = pl.ds(step * seg_len, seg_len)
        normal, inverse = normal_rows(h1[rows, :])
        above = above_in[rows, :]
        gain_grad += column_sum(above * normal)
        shift_grad += column_sum(above)
        summed = normal_back(normal, inverse, above * vectors[3:4, :])
        dh1_out[rows, :] = summed
        rounded = summed.astype(BF16)
        do[rows, :] = rounded
        bias_grad += column_sum(rounded.astype(F32))
        da_out[rows, :] = (dot(rounded, w_out[...], 1, 1) * out_scale).astype(BF16)
    vector_grads[0:1, :] = gain_grad
    vector_grads[1:2, :] = shift_grad
    vector_grads[2:3, :] = bias_grad
    for g in range(GROUPS):
        cols = pl.ds(g * GROUP_COLS, GROUP_COLS)
        grad[cols, :] = dot(mixed[g][...], do[...], 0, 0) * out_scale
    for g in range(GROUPS):
        part = grad.at[:, g * OUT_COLS : (g + 1) * OUT_COLS]
        take_rows(part, sides[2 * g : 2 * g + 2], ORDERS[g], device)


def attend_back_kernel(group, seg_len, where, *refs):
    q, k, v, a, da, logs, rounded, before, refs = *refs[:8], refs[8:]
    sides, grad_sides, bias_grads, refs = refs[:2], refs[4:6], refs[6], refs[7:]
    last = group == GROUPS - 1
    if last:
        own, sends, top_rows, total, refs = refs[0], refs[1:4], refs[4], refs[5], refs[6:]
    else:
        total, refs = refs[0], refs[1:]
    turned, weight, parts, query_turned, grad = refs
    device, slot = where[0], where[1]
    seq_len = 4 * seg_len
    pair = pl.program_id(0)

    @pl.when(pair == 0)
    def _():
        turned[...] = rounded[...].T
        total[...] = before[...]

    for part in range(3):
        put_rows(weight.at[:, part * PAIR : (part + 1) * PAIR], sides, "xy", device, part)

    queries, mixed_grads = q[...], da[...]
    zeros = jnp.zeros_like(queries)
    query_heads = spread_heads(queries, zeros)
    grad_heads = spread_heads(mixed_grads, zeros)
    product = (mixed_grads.astype(F32) * a[...].astype(F32)).T
    inner = (column_sum(product[:HD]), column_sum(product[HD:]))
    start = 0
    while start < seq_len:
        size = min(256, seq_len - start)
        rows = pl.ds(start, size)
        none = jnp.zeros((size, PAIR), BF16)
        key_grad = value_grad = query_grad = 0.0
        heads = zip(spread_heads(k[rows, :], none), spread_heads(v[rows, :], none))
        for h, (key_head, value_head) in enumerate(heads):
            scores = dot(key_head, queries, 1, 1)
            probs = jnp.exp2(scores * (log2e * score_scale) - logs[h : h + 1, :])
            grads = (probs * (dot(value_head, mixed_grads, 1, 1) - inner[h])).astype(BF16)
            value_grad += dot(probs.astype(BF16), grad_heads[h], 1, 0)
            key_grad += dot(grads, query_heads[h], 1, 0)
            query_grad += dot(key_head, grads, 0, 0)
        parts[rows, PAIR : 2 * PAIR] = (key_grad * score_scale).astype(BF16)
        parts[rows, 2 * PAIR :] = value_grad.astype(BF16)
        if start == 0:
            query_turned[...] = query_grad
        else:
            query_turned[...] += query_grad
        start += size
    parts[:, :PAIR] = (query_turned[...].T * score_scale).astype(BF16)
    bias_grads[0:1, :] = column_sum(parts[:, :PAIR].astype(F32))
    bias_grads[1:2, :] = column_sum(parts[:, 2 * PAIR :].astype(F32))
    total[...] += dot(parts[...], weight[...], 1, 1)
    grad[...] = dot(turned[...], parts[...], 1, 0)
    take_rows(grad, grad_sides, ORDERS[group], device)

    if last:

        @pl.when(pair == pl.num_programs(0) - 1)
        def _():
            top_rows[...] = total[:8, :]
            for n in range(4):
                piece = total[pl.ds(pl.multiple_of((slot ^ n) * seg_len, 16), seg_len), :]
                if n == 0:
                    own[...] = piece
                else:
                    sends[n - 1][...] = piece.astype(BF16)


def call(kernel, name, where, grid, operands, results, scratch, flops, exps=0, aliases=None):
    def spec(block, index):
        if block is None:
            return pl.BlockSpec(memory_space=pl.ANY)
        return pl.BlockSpec(block, lambda i, _: index(i))

    moved = sum(x.size * x.dtype.itemsize for x, _, _ in (*operands, *results))
    return pl.pallas_call(
        kernel,
        grid_spec=pltpu.PrefetchScalarGridSpec(
            num_scalar_prefetch=1,
            grid=(grid,),
            in_specs=[spec(block, index) for _, block, index in operands],
            out_specs=[spec(block, index) for _, block, index in results],
            scratch_shapes=[pltpu.VMEM(shape, kind) for shape, kind in scratch],
        ),
        out_shape=[shape for shape, _, _ in results],
        input_output_aliases={source + 1: target for source, target in (aliases or {}).items()},
        compiler_params=pltpu.CompilerParams(vmem_limit_bytes=VMEM_LIMIT),
        cost_estimate=pl.CostEstimate(flops=flops, bytes_accessed=moved, transcendentals=exps),
        name=name,
    )(where, *(x for x, _, _ in operands))


def whole(x):
    return (x, x.shape, lambda i: (0,) * len(x.shape))


def shape_of(shape, kind):
    return jax.ShapeDtypeStruct(shape, kind)


def whole_out(shape, kind):
    return whole(shape_of(shape, kind))


def attend(group, where, source, sides, vectors, seg_len):
    seq_len = 4 * seg_len
    first = group == 0
    base = group * GROUP_PAIRS

    def at(i):
        return (0, i + base)

    operands = [whole(x) for x in source]
    operands += [(x, (HALF, 3, ROWS, PAIR), lambda i: (0, 0, 0, i + base)) for x in sides]
    operands += [(vectors[n : n + 1], (1, PAIR), at) for n in range(2)]
    results = []
    if first:
        results += [whole_out((seq_len, D), BF16), whole_out((8, D), F32)]
    columns = (shape_of((seq_len, GROUP_COLS), BF16), (seq_len, PAIR), lambda i: (0, i))
    results += [columns] * 4
    results += [(shape_of((GROUP_PAIRS, 2, seq_len), F32), (None, 2, seq_len), lambda i: (i, 0, 0))]
    scratch = [((D, 3 * PAIR), BF16), ((seq_len, PAIR), F32)]
    scores = seq_len * seq_len * 2 * GROUP_PAIRS
    return call(
        functools.partial(attend_kernel, first, seg_len),
        f"attend_{group}",
        where,
        GROUP_PAIRS,
        operands,
        results,
        scratch,
        scores * 16 * HD,
        scores,
    )


def by_chunk(x):
    if x.ndim == 3:
        return (x, (HALF, ROWS, CHUNK), lambda i: (0, 0, i))
    return (x, (x.shape[0], CHUNK), lambda i: (0, i))


def out_weight(sides):
    return [(x, (HALF, 1, ROWS, D), lambda i: (0, 3, 0, 0)) for x in sides]


def project(where, rounded, top_rows, mixed, sides, vectors):
    seq_len = rounded.shape[0]
    return call(
        functools.partial(project_kernel, seq_len // 4),
        "project",
        where,
        1,
        [whole(x) for x in (rounded, top_rows, *mixed)] + [*out_weight(sides), whole(vectors)],
        [whole_out((seq_len, D), kind) for kind in (F32, F32, BF16)],
        [((D, D), BF16)],
        seq_len * D * D * 2,
    )


def feed_forward(where, y1, up, down, hidden_bias):
    seq_len = y1.shape[0]
    hidden = up[0].shape[-1]
    wide = by_chunk(shape_of((seq_len, hidden), BF16))
    return call(
        functools.partial(forward_kernel, seq_len // 4),
        "feed_forward",
        where,
        hidden // CHUNK,
        [whole(y1)] + [by_chunk(x) for x in (*up, *down, hidden_bias)],
        [wide, wide, whole_out((seq_len, D), F32)],
        [((D, CHUNK), BF16)] * 2,
        seq_len * D * hidden * 4,
        2 * seq_len * hidden,
    )


def second_norm(where, normed, forward, active, vectors, cotangents):
    seq_len, hidden = active.shape
    seg_len = seq_len // 4
    operands = [whole(normed), whole(forward), by_chunk(active), whole(vectors)]
    results = [whole_out((seg_len, D), BF16)] * 4
    results += [whole_out((seq_len, D), F32), whole_out((seq_len, D), BF16), whole_out((8, D), F32)]
    results += [by_chunk(shape_of((HALF, ROWS, hidden), BF16))] * 2
    return call(
        functools.partial(second_kernel, seg_len),
        "second_norm",
        where,
        hidden // CHUNK,
        operands + [whole(x) for x in cotangents],
        results,
        [((D, seq_len), BF16), ((D, CHUNK), F32)],
        seq_len * D * hidden * 2,
    )


def feed_back(where, dh2, df, y1, slope, up, down):
    seq_len, hidden = slope.shape
    operands = [whole(dh2), whole(df), whole(y1)] + [by_chunk(x) for x in (slope, *up, *down)]
    results = [by_chunk(shape_of((HALF, ROWS, hidden), BF16))] * 2
    results += [by_chunk(shape_of((1, hidden), F32)), whole_out((seq_len, D), F32)]
    scratch = [((D, seq_len), BF16), ((seq_len, CHUNK), BF16)]
    scratch += [((D, CHUNK), BF16)] * 2 + [((D, CHUNK), F32)]
    return call(
        functools.partial(backward_kernel, seq_len // 4),
        "feed_back",
        where,
        hidden // CHUNK,
        operands,
        results,
        scratch,
        seq_len * D * hidden * 6,
    )


def first_norm_back(where, above, h1, mixed, sides, vectors):
    seq_len = h1.shape[0]
    results = [whole_out((seq_len, D), F32), whole_out((seq_len, D), BF16), whole_out((8, D), F32)]
    side = shape_of((HALF, ROWS, SIDE_COLS), BF16)
    results += [(side, (HALF, ROWS, OUT_COLS), lambda i: (0, 0, 3 * GROUP_COLS // OUT_COLS))] * (2 * GROUPS)
    return call(
        functools.partial(first_kernel, seq_len // 4),
        "first_norm_back",
        where,
        1,
        [whole(x) for x in (above, h1, *mixed)] + [*out_weight(sides), whole(vectors)],
        results,
        [((seq_len, D), BF16), ((D, D), BF16), ((D, D), F32)],
        seq_len * D * D * 4,
    )


def attend_back(group, where, heads, da, logs, rounded, before, sides, grads, seg_len):
    seq_len = 4 * seg_len
    last = group == GROUPS - 1
    base = group * GROUP_PAIRS
    operands = [(x, (seq_len, PAIR), lambda i: (0, i)) for x in heads]
    operands += [(da, (seq_len, PAIR), lambda i: (0, i + base))]
    operands += [(logs, (None, 2, seq_len), lambda i: (i, 0, 0)), whole(rounded), whole(before)]
    operands += [(x, (HALF, 3, ROWS, PAIR), lambda i: (0, 0, 0, i + base)) for x in sides]
    aliases = {len(operands) + n: n for n in range(2)}
    operands += [(x, None, None) for x in grads]
    results = [(shape_of(x.shape, BF16), (HALF, ROWS, 3 * PAIR), lambda i: (0, 0, i)) for x in grads]
    results += [(shape_of((8, GROUP_COLS), F32), (8, PAIR), lambda i: (0, i))]
    scratch = []
    if last:
        results += [whole_out((seg_len, D), F32)] + [whole_out((seg_len, D), BF16)] * 3
        results += [whole_out((8, D), F32)]
        scratch += [((seq_len, D), F32)]
    else:
        results += [whole_out((seq_len, D), F32)]
    scratch += [((D, seq_len), BF16), ((D, 3 * PAIR), BF16), ((seq_len, 3 * PAIR), BF16)]
    scratch += [((PAIR, seq_len), F32), ((D, 3 * PAIR), F32)]
    scores = seq_len * seq_len * 2 * GROUP_PAIRS
    return call(
        functools.partial(attend_back_kernel, group, seg_len),
        f"attend_back_{group}",
        where,
        GROUP_PAIRS,
        operands,
        results,
        scratch,
        scores * 40 * HD,
        scores,
        aliases,
    )


def arrange_kernel(where, *refs):
    pieces, out = refs[:4], refs[4]
    for n in range(4):

        @pl.when(pl.program_id(0) == n)
        def _(n=n):
            out[...] = pieces[n][...].astype(out.dtype)


def arrange(where, pieces, kind):
    seg_len = pieces[0].shape[0]
    return pl.pallas_call(
        arrange_kernel,
        grid_spec=pltpu.PrefetchScalarGridSpec(
            num_scalar_prefetch=1,
            grid=(4,),
            in_specs=[pl.BlockSpec(x.shape, lambda i, _: (0, 0)) for x in pieces],
            out_specs=pl.BlockSpec((None, None, seg_len, D), lambda i, at: (at[1] ^ i, 0, 0, 0)),
        ),
        out_shape=jax.ShapeDtypeStruct((4, 1, seg_len, D), kind),
        compiler_params=pltpu.CompilerParams(vmem_limit_bytes=VMEM_LIMIT),
        name="arrange",
    )(where, *pieces)


def partner(value, axis, mask):
    pairs = [(source, source ^ mask) for source in range(lax.axis_size(axis))]
    return lax.ppermute(value, axis, pairs)


def over_core(value):
    return partner(value, "cam", 1)


def over_x(value):
    return partner(value, "cam", 2)


def over_y(value):
    return partner(value, "dp", 1)


def over_z(value, apart_by):
    return partner(value, "dp", 2 * apart_by)


def stages_of(order):
    return (over_x, over_y) if order == "xy" else (over_y, over_x)


def by_blocks():
    return lax.axis_size("dp") * lax.axis_size("cam") == BLOCKS


def doubled(held, stage, axis=0):
    return jnp.concatenate([held, stage(held)], axis=axis)


def gather_plain(shard, order):
    at = shard.ndim - 2
    full = lax.all_gather(shard, ("dp", "cam"), axis=at, tiled=True)
    full = full.reshape(*full.shape[:at], 2, 2, 2, 2, 2, ROWS, full.shape[-1])
    high_z, low_z, y_at, x_at, core = range(at, at + 5)
    outer, inner = (x_at, y_at) if order == "xy" else (y_at, x_at)
    full = jnp.moveaxis(full, (core, outer, inner, low_z, high_z), range(5))
    full = full.reshape(2, HALF, *full.shape[5:])
    return full[0], full[1]


def scatter_plain(sides, order):
    full = jnp.stack(sides).reshape(2, 2, 2, 2, 2, ROWS, sides[0].shape[-1])
    places = (4, 3, 2, 1, 0) if order == "xy" else (4, 2, 3, 1, 0)
    full = jnp.moveaxis(full, range(5), places).reshape(D, sides[0].shape[-1])
    return lax.psum_scatter(full.astype(F32), ("dp", "cam"), scatter_dimension=0, tiled=True)


def halve(held, received):
    held = held + received.astype(F32)
    half = held.shape[0] // 2
    return held[:half], held[half:].astype(BF16)


def scatter_rest(held, send, stages):
    for stage in stages:
        held, send = halve(held, stage(send))
    return (held + over_z(send, 2).astype(F32))[0]


def over_low_z(value):
    return over_z(value, 1)


def over_high_z(value):
    return over_z(value, 2)


def finish(vector, held_a, send_a, held_b, send_b):
    size, columns = vector.size, send_a.shape[-1]
    block = (1, ROWS, columns)
    vector = jnp.pad(vector, (0, ROWS * columns - size)).reshape(block)

    def low(values):
        return lax.optimization_barrier(values.astype(BF16))

    def add(mine, other):
        return low(mine.astype(F32) + other.astype(F32))

    vector = low(vector)
    vector = add(vector, over_core(vector))
    for stage_a, stage_b in ((over_x, over_y), (over_y, over_x)):
        got = stage_a(jnp.concatenate([send_a, vector]))
        got_b = stage_b(send_b)
        held_a, send_a = halve(held_a, got[:-1])
        held_b, send_b = halve(held_b, got_b)
        vector = add(vector, got[-1:])
    got = over_low_z(jnp.concatenate([send_a, send_b, vector]))
    vector = add(vector, got[-1:])
    held_a, send_a = halve(held_a, got[:2])
    held_b, send_b = halve(held_b, got[2:4])
    got = over_high_z(jnp.concatenate([send_a, send_b, vector]))
    vector = add(vector, got[2:])
    total = vector.astype(F32).reshape(-1)[:size]
    return total, held_a[0] + got[0].astype(F32), held_b[0] + got[1].astype(F32)


def after(value, *others):
    return lax.optimization_barrier((value, *others))[0]


def local(
    tokens,
    out_grad,
    joint_state,
    joint_mask,
    attn_master,
    attn_first,
    attn_second,
    attn_average,
    ffn_master,
    ffn_first,
    ffn_second,
    ffn_average,
    small_params,
    small_first,
    small_second,
    small_average,
):
    cam_index = lax.axis_index("cam")
    slot, group_index = cam_index % 4, cam_index // 4
    items_here, _, seg_len, _ = tokens.shape
    assert items_here == 4
    device = lax.axis_index("dp") * lax.axis_size("cam") + cam_index if by_blocks() else 0
    where = jnp.stack([jnp.int32(device), jnp.int32(slot)])

    def piece_for(array, n):
        return lax.dynamic_index_in_dim(array, slot ^ n, 0, keepdims=False)

    def trade(pieces):
        return [pieces[0]] + [partner(pieces[n], "cam", n) for n in range(1, 4)]

    blocks = by_blocks()
    sequence = trade([piece_for(tokens[:, 0], n) for n in range(4)])
    attn_low = attn_master.astype(BF16)
    ffn_low = ffn_master.astype(BF16)
    if blocks:
        held = attn_low[None]
        for stage in (over_high_z, over_low_z):
            held = doubled(held, stage)
        wide = after(ffn_low[:, None], held)
        for stage in (over_high_z, over_low_z):
            wide = doubled(wide, stage, 1)
        for stage in (over_y, over_x):
            held = doubled(held, stage)
        sides = (held, over_core(held))
        up, down = after(wide[0], sides[1]), after(wide[1], sides[1])
    else:
        sides = gather_plain(attn_low, "xy")
        up, down = gather_plain(ffn_low[0], "xy"), gather_plain(ffn_low[1], "yx")

    vectors = small_params[: 8 * D].reshape(8, D)
    joint_rows = small_params[8 * D : (8 + NJ) * D].reshape(NJ, D)
    hidden_bias = small_params[(8 + NJ) * D :].reshape(1, -1)
    active = (joint_state * joint_mask.astype(F32))[slot, group_index]
    joint = jnp.sum(active[:, None] * joint_rows, axis=0, keepdims=True)

    here = after(where, up, down)
    rounded, top_rows, *heads = attend(0, here, [*sequence, joint], sides, vectors, seg_len)
    if blocks:
        up, down = doubled(up, over_y), doubled(down, over_x)
        here = after(where, up, down)
        up, down = after(up, top_rows), after(down, top_rows)
    heads = [heads, attend(1, here, [rounded], sides, vectors, seg_len)]
    mixed = [x[3] for x in heads]
    if blocks:
        up, down = doubled(up, over_x), doubled(down, over_y)
        here = after(where, up, down)
        up, down = after(up, mixed[1]), after(down, mixed[1])
        up, down = (up, over_core(up)), (down, over_core(down))
    h1, normed, y1 = project(here, rounded, top_rows, mixed, sides, vectors)
    cotangents = trade([after(piece_for(out_grad[:, 0], n), y1) for n in range(4)])
    gated, slope, forward = feed_forward(where, y1, up, down, hidden_bias)
    *results, dh2, df, grads_two, down_keep, down_send = second_norm(
        where, normed, forward, gated, vectors, cotangents
    )
    outputs = trade(results)
    down_core = over_core(down_send) if blocks else down_send
    up_keep, up_send, hidden_grad, above = feed_back(where, dh2, df, y1, slope, up, down)
    up_core = over_core(up_send) if blocks else up_send
    dh1, da, grads_one, *attn_grads = first_norm_back(
        after(where, down_core, *outputs), above, h1, mixed, sides, vectors
    )
    block_output = arrange(where, outputs, BF16)

    def back(group, where, before, grads):
        return attend_back(
            group, where, heads[group][:4], da, heads[group][4], rounded, before, sides, grads, seg_len
        )

    if blocks:
        up_held, up_send = halve(up_keep.astype(F32), up_core)
        down_held, down_send = halve(down_keep.astype(F32), down_core)
        up_send, down_send = after(up_send, da), after(down_send, da)
    here = after(where, up_send, down_send)
    if blocks:
        up_core, down_core = over_x(up_send), over_y(down_send)
    keep_a, send_a, bias_a, before = back(0, here, dh1, attn_grads[:2])
    if blocks:
        up_held, up_send = halve(up_held, up_core)
        down_held, down_send = halve(down_held, down_core)
        up_send, down_send = after(up_send, before), after(down_send, before)
        core_a = over_core(send_a)
    here = after(where, up_send, down_send)
    if blocks:
        up_core, down_core = over_y(up_send), over_x(down_send)
    keep_b, send_b, bias_b, own, *sends, item_top = back(1, here, before, attn_grads[2:])
    grad_pieces = trade([own, *sends])
    small_grad = jnp.concatenate(
        [
            bias_a[0],
            bias_b[0],
            bias_a[1],
            bias_b[1],
            grads_one[2],
            grads_one[0],
            grads_one[1],
            grads_two[2],
            grads_two[0],
            grads_two[1],
            (active[:, None] * item_top[1:2]).reshape(-1),
            hidden_grad[0],
        ]
    )
    if blocks:
        up_core, down_core, core_a = (after(x, own) for x in (up_core, down_core, core_a))
        up_held, up_send = halve(up_held, up_core)
        down_held, down_send = halve(down_held, down_core)
        ffn_held = jnp.stack([up_held, down_held], axis=1)
        ffn_shard = scatter_rest(ffn_held, jnp.stack([up_send, down_send], axis=1), (over_low_z,))
        held_a, send_a = halve(keep_a.astype(F32), core_a)
        held_b, send_b = halve(keep_b.astype(F32), over_core(send_b))
        small_total, grads_a, grads_b = finish(small_grad, held_a, send_a, held_b, send_b)
    else:
        small_total = lax.psum(small_grad, ("dp", "cam"))
        ffn_shard = jnp.stack(
            [scatter_plain((up_keep, up_core), "xy"), scatter_plain((down_keep, down_core), "yx")]
        )
        grads_a = scatter_plain((keep_a, send_a), "xy")
        grads_b = scatter_plain((keep_b, send_b), "yx")
    input_grad = arrange(where, grad_pieces, F32)

    rows_here = attn_master.shape[1]
    split = 3 * GROUP_COLS
    proj_grad = jnp.concatenate([grads_a[:, :split], grads_b[:, :split]], axis=1)
    proj_grad = jnp.moveaxis(proj_grad.reshape(rows_here, PAIRS, 3, PAIR), 2, 0).reshape(3, rows_here, D)
    out_proj_grad = jnp.concatenate([grads_a[:, split:], grads_b[:, split:]], axis=1)
    attn_shard = jnp.concatenate([proj_grad, out_proj_grad[None]])
    new_attn = adam_update(
        attn_master, attn_shard, attn_first, attn_second, attn_average, rate_matrix, decay_matrix
    )
    new_ffn = adam_update(
        ffn_master, ffn_shard, ffn_first, ffn_second, ffn_average, rate_matrix, decay_matrix
    )
    new_small = adam_update(
        small_params, small_total, small_first, small_second, small_average, rate_small, 0.0
    )
    return (block_output, input_grad, *new_attn, *new_ffn, *new_small)


def solution(mesh):
    in_specs = (
        P("dp", "cam", None, None),
        P("dp", "cam", None, None),
        P("dp", None, None),
        P("dp", None, None),
        P(None, ("dp", "cam"), None),
        P(None, ("dp", "cam"), None),
        P(None, ("dp", "cam"), None),
        P(None, ("dp", "cam"), None),
        P(None, ("dp", "cam"), None),
        P(None, ("dp", "cam"), None),
        P(None, ("dp", "cam"), None),
        P(None, ("dp", "cam"), None),
        P(),
        P(),
        P(),
        P(),
    )
    out_specs = (
        P("dp", "cam", None, None),
        P("dp", "cam", None, None),
        P(None, ("dp", "cam"), None),
        P(None, ("dp", "cam"), None),
        P(None, ("dp", "cam"), None),
        P(None, ("dp", "cam"), None),
        P(None, ("dp", "cam"), None),
        P(None, ("dp", "cam"), None),
        P(None, ("dp", "cam"), None),
        P(None, ("dp", "cam"), None),
        P(),
        P(),
        P(),
        P(),
    )
    return jax.shard_map(local, mesh=mesh, in_specs=in_specs, out_specs=out_specs, check_vma=False)
```

```python
import functools

import jax
import jax.numpy as jnp
from jax import lax
from jax.experimental import pallas as pl
from jax.experimental.pallas import tpu as pltpu
from jax.sharding import PartitionSpec as P

D = 512
HEADS = 8
NJ = 14
ADAM_STEP = 10
HD = 64
PAIR = 2 * HD
PAIRS = HEADS // 2
BLOCKS = 32
ROWS = D // BLOCKS
HALF = BLOCKS // 2
CHUNK = 640
SIDE_PAIRS = 2

norm_eps = 1e-05
beta_first = 0.5
beta_second = 0.5
adam_eps = 1e-08
rate_matrix = 0.02
rate_small = 0.05
decay_matrix = 0.1
ema_decay = 0.75
log2e = 1.4426950408889634
score_scale = HD**-0.5
F32 = jnp.float32
BF16 = jnp.bfloat16
VMEM_LIMIT = 60 * 2**20
NEXT_TO_NOTHING = pl.CostEstimate(flops=1, bytes_accessed=1, transcendentals=0)


def adam_update(master, grad_total, first_old, second_old, average_old, rate, decay):
    first_new = beta_first * first_old + (1.0 - beta_first) * grad_total
    second_new = beta_second * second_old + (1.0 - beta_second) * grad_total * grad_total
    first_hat = first_new / (1.0 - beta_first**ADAM_STEP)
    second_hat = second_new / (1.0 - beta_second**ADAM_STEP)
    master_new = master - rate * (first_hat / (jnp.sqrt(second_hat) + adam_eps) + decay * master)
    average_new = ema_decay * average_old + (1.0 - ema_decay) * master_new
    return (master_new, first_new, second_new, average_new)


def dot(left, right, left_dim, right_dim):
    return lax.dot_general(
        left, right, (((left_dim,), (right_dim,)), ((), ())), preferred_element_type=F32
    )


DEVICE_BITS = {"x": 2, "y": 4, "z": 8, "Z": 16}
BY_X, BY_Y, BY_YZ = "xyzZ", "yxzZ", "yzZx"


def apart(position, order, core):
    bits = (DEVICE_BITS[name] for n, name in enumerate(order) if position >> (3 - n) & 1)
    return core + sum(bits)


def row_blocks(device, order):
    for core in range(2):
        for position in range(HALF):
            start = (device ^ apart(position, order, core)) * ROWS
            yield core, position, pl.ds(pl.multiple_of(start, ROWS), ROWS)


def put_rows(target, sides, order, device, part=None):
    for core, position, rows in row_blocks(device, order):
        which, at = divmod(position, HALF // len(sides[core]))
        array = sides[core][which]
        target[rows, :] = array[at] if part is None else array[part, at]


def take_rows(source, sides, order, device):
    for core, position, rows in row_blocks(device, order):
        sides[core][position] = source[rows, :].astype(BF16)


def mean_last(values):
    return jnp.sum(values, axis=-1, keepdims=True) * (1.0 / D)


def normal_rows(values):
    centred = values - mean_last(values)
    inverse = lax.rsqrt(mean_last(centred * centred) + norm_eps)
    return centred * inverse, inverse


def normal_back(normal, inverse, grad):
    return inverse * (grad - mean_last(grad) - normal * mean_last(grad * normal))


def column_sum(values):
    return jnp.sum(values, axis=0, keepdims=True)


def spread_heads(values, other):
    lane = lax.broadcasted_iota(jnp.int32, (1, PAIR), 1)
    low = lane < HD
    return jnp.where(low, values, other), jnp.where(low, other, values)


def attend_kernel(base, seg_len, where, *refs):
    first = base == 0
    if first:
        pieces, active, refs = refs[:4], refs[4], refs[5:]
    else:
        rounded, refs = refs[0], refs[6:]
    qk_sides, vo_sides = (refs[0:2], refs[2:4]), (refs[4:6], refs[6:8])
    vectors, refs = refs[8], refs[9:]
    if first:
        rounded, top_rows, refs = refs[0], refs[1], refs[2:]
    q_out, k_out, v_out, a_out, l_out, weight, logs = refs
    device, slot = where[0], where[1]

    if first:

        @pl.when(pl.program_id(0) == 0)
        def _():
            for k in range(4):
                start = pl.multiple_of((slot ^ k) * seg_len, 16)
                rounded[pl.ds(start, seg_len), :] = pieces[k][...]
            joint = column_sum(active[...] * vectors[8:, :])
            top = rounded[:16, :].astype(F32)
            at = lax.broadcasted_iota(jnp.int32, (16, 1), 0)
            top = jnp.where(at == 1, top + joint, top)
            top_rows[...] = top[:8]
            rounded[:16, :] = top.astype(BF16)

    put_rows(weight.at[:, :PAIR], qk_sides, BY_X, device, 0)
    put_rows(weight.at[:, PAIR : 2 * PAIR], qk_sides, BY_X, device, 1)
    put_rows(weight.at[:, 2 * PAIR :], vo_sides, BY_Y, device, 0)
    cols = pl.ds(pl.multiple_of((pl.program_id(0) + base) * PAIR, PAIR), PAIR)
    bias_q, bias_v = vectors[0:1, cols], vectors[1:2, cols]
    projected = dot(rounded[...], weight[...], 1, 0)
    q_out[...] = (projected[:, :PAIR] + bias_q).astype(BF16)
    keys = projected[:, PAIR : 2 * PAIR].astype(BF16)
    values = (projected[:, 2 * PAIR :] + bias_v).astype(BF16)
    k_out[...] = keys
    v_out[...] = values
    lane = lax.broadcasted_iota(jnp.int32, (1, PAIR), 1)
    low = lane < HD
    value_heads = spread_heads(values, jnp.ones_like(values))
    scale = log2e * score_scale
    for step in range(4):
        rows = pl.ds(step * seg_len, seg_len)
        query = q_out[rows, :]
        mixed, tops = [], []
        for query_head, value_head in zip(spread_heads(query, jnp.zeros_like(query)), value_heads):
            scores = dot(query_head, keys, 1, 1)
            top = jnp.max(scores, axis=1, keepdims=True) * scale
            probs = jnp.exp2(scores * scale - top).astype(BF16)
            mixed.append(dot(probs, value_head, 1, 0))
            tops.append(top)
        total = pltpu.roll(jnp.where(low, mixed[1], mixed[0]), HD, 1)
        a_out[rows, :] = (jnp.where(low, mixed[0], mixed[1]) / total).astype(BF16)
        logs[rows, :] = jnp.where(low, tops[0], tops[1]) + jnp.log2(total)
    turned = logs[...].T
    l_out[0:1, :] = turned[0:1]
    l_out[1:2, :] = turned[HD : HD + 1]


def gate_both(values):
    size = jnp.abs(values)
    fraction = 1.0 / (1.0 + (0.3275911 * 0.5**0.5) * size)
    bell = jnp.exp2(values * values * (-0.5 * log2e))
    series = 0.5 * 1.061405429 * fraction - 0.5 * 1.453152027
    series = series * fraction + 0.5 * 1.421413741
    series = series * fraction - 0.5 * 0.284496736
    series = series * fraction + 0.5 * 0.254829592
    tail = series * fraction * bell
    below = jnp.where(values > 0.0, 1.0 - tail, tail)
    return values * below, below + values * bell * 0.3989422804014327


def project_kernel(seg_len, where, *refs):
    rounded, top_rows, mixed, vo_sides, vectors = *refs[:3], (refs[3:5], refs[5:7]), refs[7]
    h1_out, normed_out, y1_out, w_out = refs[8:]
    out_scale = (4 * seg_len / 3.0) ** 0.5

    @pl.when(pl.program_id(0) == 0)
    def _():
        put_rows(w_out, vo_sides, BY_Y, where[0], 0)

    summed = rounded[...].astype(F32)
    top = jnp.where(pl.program_id(0) == 0, top_rows[...], summed[:8])
    summed = jnp.concatenate([top, summed[8:]], axis=0)
    summed = summed + (dot(mixed[...], w_out[...], 1, 0) * out_scale + vectors[2:3, :])
    h1_out[...] = summed
    normal, _ = normal_rows(summed)
    result = normal * vectors[3:4, :] + vectors[4:5, :]
    normed_out[...] = result
    y1_out[...] = result.astype(BF16)


def forward_kernel(seg_len, where, *refs):
    y1, up_sides, down_sides = refs[0], (refs[1:3], refs[3:5]), (refs[5:7], refs[7:9])
    hidden_bias, refs = refs[9], refs[10:]
    g_out, slope_out, total, w_up, w_down = refs
    device = where[0]

    @pl.when(pl.program_id(0) == 0)
    def _():
        total[...] = jnp.zeros_like(total)

    put_rows(w_up, up_sides, BY_X, device)
    put_rows(w_down, down_sides, BY_Y, device)
    for step in range(4):
        rows = pl.ds(step * seg_len, seg_len)
        inner = dot(y1[rows, :], w_up[...], 1, 0) + hidden_bias[...]
        active, slope = gate_both(inner)
        active = active.astype(BF16)
        g_out[rows, :] = active
        slope_out[rows, :] = slope.astype(BF16)
        total[rows, :] += dot(active, w_down[...], 1, 1)


def second_kernel(seg_len, where, *refs):
    normed, forward, active, vectors, cotangents, refs = *refs[:4], refs[4:8], refs[8:]
    pieces, dh2_out, df_out, vector_grads, refs = refs[:4], refs[4], refs[5], refs[6], refs[7:]
    down_grads, df_turned, grad = refs[:2], refs[2], refs[3]
    device, slot = where[0], where[1]

    @pl.when(pl.program_id(0) == 0)
    def _():
        gain_grad = shift_grad = bias_grad = 0.0
        for k in range(4):
            rows = pl.ds(pl.multiple_of((slot ^ k) * seg_len, 16), seg_len)
            normal, inverse = normal_rows(normed[rows, :] + (forward[rows, :] + vectors[5:6, :]))
            pieces[k][...] = (normal * vectors[6:7, :] + vectors[7:8, :]).astype(BF16)
            cotangent = cotangents[k][...].astype(F32)
            gain_grad += column_sum(cotangent * normal)
            shift_grad += column_sum(cotangent)
            middle = normal_back(normal, inverse, cotangent * vectors[6:7, :])
            dh2_out[rows, :] = middle
            rounded = middle.astype(BF16)
            df_out[rows, :] = rounded
            bias_grad += column_sum(rounded.astype(F32))
        vector_grads[0:1, :] = gain_grad
        vector_grads[1:2, :] = shift_grad
        vector_grads[2:3, :] = bias_grad
        df_turned[...] = df_out[...].T

    grad[...] = dot(df_turned[...], active[...], 1, 0)
    take_rows(grad, down_grads, BY_Y, device)


def backward_kernel(seg_len, where, *refs):
    dh2, df, y1, slope, refs = *refs[:4], refs[4:]
    up_sides, down_sides, refs = (refs[0:2], refs[2:4]), (refs[4:6], refs[6:8]), refs[8:]
    up_grads, hidden_grad, total, refs = refs[:2], refs[2], refs[3], refs[4:]
    y1_turned, dz, w_up, w_down, grad = refs
    device = where[0]

    @pl.when(pl.program_id(0) == 0)
    def _():
        y1_turned[...] = y1[...].T
        total[...] = dh2[...]

    put_rows(w_up, up_sides, BY_X, device)
    put_rows(w_down, down_sides, BY_Y, device)
    bias_grad = 0.0
    for step in range(4):
        rows = pl.ds(step * seg_len, seg_len)
        inner = (dot(df[rows, :], w_down[...], 1, 0) * slope[rows, :].astype(F32)).astype(BF16)
        dz[rows, :] = inner
        bias_grad += column_sum(inner.astype(F32))
        total[rows, :] += dot(inner, w_up[...], 1, 1)
    hidden_grad[...] = bias_grad
    grad[...] = dot(y1_turned[...], dz[...], 1, 0)
    take_rows(grad, up_grads, BY_X, device)


def first_kernel(seg_len, where, *refs):
    above_in, h1, mixed, vo_sides, vectors = *refs[:3], (refs[3:5], refs[5:7]), refs[7]
    dh1_out, da_out, vector_grads, grad_sides, w_out, grad = *refs[8:11], refs[11:13], *refs[13:]
    device, step = where[0], pl.program_id(0)
    out_scale = (4 * seg_len / 3.0) ** 0.5

    @pl.when(step == 0)
    def _():
        put_rows(w_out, vo_sides, BY_Y, device, 0)
        vector_grads[...] = jnp.zeros_like(vector_grads)
        grad[...] = jnp.zeros_like(grad)

    normal, inverse = normal_rows(h1[...])
    above = above_in[...]
    vector_grads[0:1, :] += column_sum(above * normal)
    vector_grads[1:2, :] += column_sum(above)
    summed = normal_back(normal, inverse, above * vectors[3:4, :])
    dh1_out[...] = summed
    rounded = summed.astype(BF16)
    vector_grads[2:3, :] += column_sum(rounded.astype(F32))
    da_out[...] = (dot(rounded, w_out[...], 1, 1) * out_scale).astype(BF16)
    grad[...] += dot(mixed[...], rounded, 0, 0) * out_scale

    @pl.when(step == pl.num_programs(0) - 1)
    def _():
        take_rows(grad, grad_sides, BY_YZ, device)


def attend_back_kernel(last, goes_on, seg_len, where, *refs):
    q, k, v, a, da, logs, rounded, before, refs = *refs[:8], refs[8:]
    qk_sides, vo_sides = (refs[0:2], refs[2:4]), (refs[4:6], refs[6:8])
    refs = refs[8 + goes_on * 2 :]
    if last:
        parts_of_small, refs = refs[:7], refs[7:]
    grad_sides, bias_grads, refs = refs[:2], refs[2], refs[3:]
    if last:
        own, sends, small_out, total, joined, refs = refs[0], refs[1:4], refs[4], refs[5], refs[6], refs[7:]
    else:
        total, refs = refs[0], refs[1:]
    turned, weight, parts, query_turned, grad = refs
    device, slot = where[0], where[1]
    seq_len = 4 * seg_len
    pair = pl.program_id(0)

    @pl.when(pair == 0)
    def _():
        turned[...] = rounded[...].T
        total[...] = before[...]

    put_rows(weight.at[:, :PAIR], qk_sides, BY_X, device, 0)
    put_rows(weight.at[:, PAIR : 2 * PAIR], qk_sides, BY_X, device, 1)
    put_rows(weight.at[:, 2 * PAIR :], vo_sides, BY_Y, device, 0)

    queries, mixed_grads = q[...], da[...]
    zeros = jnp.zeros_like(queries)
    query_heads = spread_heads(queries, zeros)
    grad_heads = spread_heads(mixed_grads, zeros)
    product = (mixed_grads.astype(F32) * a[...].astype(F32)).T
    inner = (column_sum(product[:HD]), column_sum(product[HD:]))
    start = 0
    while start < seq_len:
        size = min(256, seq_len - start)
        rows = pl.ds(start, size)
        none = jnp.zeros((size, PAIR), BF16)
        key_grad = value_grad = query_grad = 0.0
        heads = zip(spread_heads(k[rows, :], none), spread_heads(v[rows, :], none))
        for h, (key_head, value_head) in enumerate(heads):
            scores = dot(key_head, queries, 1, 1)
            probs = jnp.exp2(scores * (log2e * score_scale) - logs[h : h + 1, :])
            grads = (probs * (dot(value_head, mixed_grads, 1, 1) - inner[h])).astype(BF16)
            value_grad += dot(probs.astype(BF16), grad_heads[h], 1, 0)
            key_grad += dot(grads, query_heads[h], 1, 0)
            query_grad += dot(key_head, grads, 0, 0)
        parts[rows, PAIR : 2 * PAIR] = (key_grad * score_scale).astype(BF16)
        parts[rows, 2 * PAIR :] = value_grad.astype(BF16)
        if start == 0:
            query_turned[...] = query_grad
        else:
            query_turned[...] += query_grad
        start += size
    parts[:, :PAIR] = (query_turned[...].T * score_scale).astype(BF16)
    bias_grads[0:1, :] = column_sum(parts[:, :PAIR].astype(F32))
    bias_grads[1:2, :] = column_sum(parts[:, 2 * PAIR :].astype(F32))
    total[...] += dot(parts[...], weight[...], 1, 1)
    grad[...] = dot(turned[...], parts[...], 1, 0)
    take_rows(grad, grad_sides, BY_YZ, device)

    if last:

        @pl.when(pair == pl.num_programs(0) - 1)
        def _():
            join_small(joined, parts_of_small, bias_grads, total[1:2, :])
            small_out[0] = two_parts(joined[...])
            for n in range(4):
                piece = total[pl.ds(pl.multiple_of((slot ^ n) * seg_len, 16), seg_len), :]
                if n == 0:
                    own[...] = piece
                else:
                    sends[n - 1][...] = piece.astype(BF16)


def call(kernel, name, where, grid, operands, results, scratch, aliases=None):
    def spec(block, index):
        if block is None:
            return pl.BlockSpec(memory_space=pl.ANY)
        return pl.BlockSpec(block, lambda i, _: index(i))

    return pl.pallas_call(
        kernel,
        grid_spec=pltpu.PrefetchScalarGridSpec(
            num_scalar_prefetch=1,
            grid=(grid,),
            in_specs=[spec(block, index) for _, block, index in operands],
            out_specs=[spec(block, index) for _, block, index in results],
            scratch_shapes=[pltpu.VMEM(shape, kind) for shape, kind in scratch],
        ),
        out_shape=[shape for shape, _, _ in results],
        input_output_aliases={source + 1: target for source, target in (aliases or {}).items()},
        compiler_params=pltpu.CompilerParams(vmem_limit_bytes=VMEM_LIMIT),
        cost_estimate=NEXT_TO_NOTHING,
        name=name,
    )(where, *(x for x, _, _ in operands))


def whole(x):
    return (x, x.shape, lambda i: (0,) * len(x.shape))


def shape_of(shape, kind):
    return jax.ShapeDtypeStruct(shape, kind)


def whole_out(shape, kind):
    return whole(shape_of(shape, kind))


def flat(sides):
    return [x for side in sides for x in side]


def pair_weights(qk, vo, base):
    def spec(x, parts):
        return (x, (parts, x.shape[1], ROWS, PAIR), lambda i: (0, 0, 0, i + base))

    return [spec(x, 2) for x in flat(qk)] + [spec(x, 1) for x in flat(vo)]


def attend(base, pairs, where, source, qk, vo, vectors, seg_len):
    seq_len = 4 * seg_len
    first = base == 0

    def column(x):
        return (x, (seq_len, PAIR), lambda i: (0, i + base))

    operands = [whole(x) for x in (source if first else source[:1])]
    operands += [] if first else [(x, None, None) for x in source[1:]]
    operands += pair_weights(qk, vo, base) + [whole(vectors)]
    results = [whole_out((seq_len, D), BF16), whole_out((8, D), F32)] if first else []
    results += [column(shape_of((seq_len, D), BF16))] * 4
    logs = shape_of((PAIRS, 2, seq_len), F32)
    results += [(logs, (None, 2, seq_len), lambda i: (i + base, 0, 0))]
    scratch = [((D, 3 * PAIR), BF16), ((seq_len, PAIR), F32)]
    return call(
        functools.partial(attend_kernel, base, seg_len),
        f"attend_{base}",
        where,
        pairs,
        operands,
        results,
        scratch,
        {} if first else {1 + n: n for n in range(5)},
    )


def by_chunk(x):
    if x.ndim == 3:
        return (x, (x.shape[0], ROWS, CHUNK), lambda i: (0, 0, i))
    return (x, (x.shape[0], CHUNK), lambda i: (0, i))


def out_weight(vo):
    return [(x, (1, x.shape[1], ROWS, D), lambda i: (1, 0, 0, 0)) for x in flat(vo)]


def by_rows(x):
    return (x, (x.shape[0] // 4, D), lambda i: (i, 0))


def project(where, rounded, top_rows, mixed, vo, vectors):
    seq_len = rounded.shape[0]
    return call(
        functools.partial(project_kernel, seq_len // 4),
        "project",
        where,
        4,
        [by_rows(rounded), whole(top_rows), by_rows(mixed), *out_weight(vo), whole(vectors)],
        [by_rows(shape_of((seq_len, D), kind)) for kind in (F32, F32, BF16)],
        [((D, D), BF16)],
    )


def feed_forward(where, y1, up, down, hidden_bias):
    seq_len = y1.shape[0]
    hidden = up[0][0].shape[-1]
    wide = by_chunk(shape_of((seq_len, hidden), BF16))
    return call(
        functools.partial(forward_kernel, seq_len // 4),
        "feed_forward",
        where,
        hidden // CHUNK,
        [whole(y1)] + [by_chunk(x) for x in (*flat(up), *flat(down), hidden_bias)],
        [wide, wide, whole_out((seq_len, D), F32)],
        [((D, CHUNK), BF16)] * 2,
    )


def second_norm(where, normed, forward, active, vectors, cotangents):
    seq_len, hidden = active.shape
    seg_len = seq_len // 4
    operands = [whole(normed), whole(forward), by_chunk(active), whole(vectors)]
    results = [whole_out((seg_len, D), BF16)] * 4
    results += [whole_out((seq_len, D), F32), whole_out((seq_len, D), BF16), whole_out((8, D), F32)]
    results += [by_chunk(shape_of((HALF, ROWS, hidden), BF16))] * 2
    return call(
        functools.partial(second_kernel, seg_len),
        "second_norm",
        where,
        hidden // CHUNK,
        operands + [whole(x) for x in cotangents],
        results,
        [((D, seq_len), BF16), ((D, CHUNK), F32)],
    )


def feed_back(where, dh2, df, y1, slope, up, down):
    seq_len, hidden = slope.shape
    operands = [whole(dh2), whole(df), whole(y1)] + [by_chunk(x) for x in (slope, *flat(up), *flat(down))]
    results = [by_chunk(shape_of((HALF, ROWS, hidden), BF16))] * 2
    results += [by_chunk(shape_of((1, hidden), F32)), whole_out((seq_len, D), F32)]
    scratch = [((D, seq_len), BF16), ((seq_len, CHUNK), BF16)]
    scratch += [((D, CHUNK), BF16)] * 2 + [((D, CHUNK), F32)]
    return call(
        functools.partial(backward_kernel, seq_len // 4),
        "feed_back",
        where,
        hidden // CHUNK,
        operands,
        results,
        scratch,
    )


def first_norm_back(where, above, h1, mixed, vo, vectors):
    seq_len = h1.shape[0]
    results = [by_rows(shape_of((seq_len, D), kind)) for kind in (F32, BF16)]
    results += [whole_out((8, D), F32)]
    results += [whole_out((HALF, ROWS, D), BF16)] * 2
    return call(
        functools.partial(first_kernel, seq_len // 4),
        "first_norm_back",
        where,
        4,
        [by_rows(x) for x in (above, h1, mixed)] + [*out_weight(vo), whole(vectors)],
        results,
        [((D, D), BF16), ((D, D), F32)],
    )


def attend_back(base, pairs, where, heads, da, logs, rounded, before, qk, vo, filled, small):
    seq_len = rounded.shape[0]
    seg_len = seq_len // 4
    last = base + pairs == PAIRS
    operands = [(x, (seq_len, PAIR), lambda i: (0, i + base)) for x in (*heads, da)]
    operands += [(logs, (None, 2, seq_len), lambda i: (i + base, 0, 0))]
    operands += [whole(rounded), whole(before), *pair_weights(qk, vo, base)]
    aliases = {len(operands) + n: n for n in range(len(filled))}
    operands += [(x, None, None) for x in filled]
    side = shape_of((HALF, ROWS, 3 * PAIR * SIDE_PAIRS), BF16)
    results = [(side, (HALF, ROWS, 3 * PAIR), lambda i: (0, 0, (i + base) % SIDE_PAIRS))] * 2
    results += [(shape_of((8, pairs * PAIR), F32), (8, PAIR), lambda i: (0, i))]
    scratch = []
    if last:
        operands += [whole(x) for x in small]
        results += [whole_out((seg_len, D), F32)] + [whole_out((seg_len, D), BF16)] * 3
        results += [whole_out((1, ROWS, 4 * D), BF16)]
        scratch += [((seq_len, D), F32), ((ROWS // 2, 4 * D), F32)]
    else:
        results += [whole_out((seq_len, D), F32)]
    scratch += [((D, seq_len), BF16), ((D, 3 * PAIR), BF16), ((seq_len, 3 * PAIR), BF16)]
    scratch += [((PAIR, seq_len), F32), ((D, 3 * PAIR), F32)]
    return call(
        functools.partial(attend_back_kernel, last, bool(filled), seg_len),
        f"attend_back_{base}",
        where,
        pairs,
        operands,
        results,
        scratch,
        aliases,
    )


def join_small(joined, parts, bias_last, top):
    *biases, first, second, active, hidden = parts
    units = [x[n : n + 1, :] for n in range(2) for x in (*biases, bias_last)]
    units += [first[n : n + 1, :] for n in (2, 0, 1)] + [second[n : n + 1, :] for n in (2, 0, 1)]
    units += [active[n : n + 1, :] * top for n in range(NJ)] + [hidden[...]]
    joined[...] = jnp.zeros_like(joined)
    at, width = 0, joined.shape[1]
    for unit in units:
        taken = 0
        while taken < unit.shape[1]:
            row, column = divmod(at, width)
            size = min(width - column, unit.shape[1] - taken)
            joined[row : row + 1, column : column + size] = unit[:, taken : taken + size]
            taken, at = taken + size, at + size


def two_parts(values):
    high = lax.reduce_precision(values, 8, 7)
    return jnp.concatenate([high, lax.reduce_precision(values - high, 8, 7)], axis=0).astype(BF16)


def of_parts(parts):
    half = parts.shape[0] // 2
    return parts[:half].astype(F32) + parts[half:].astype(F32)


def arrange_kernel(where, *refs):
    pieces, out, landed, widened, sem_in, sem_out = refs[:4], *refs[4:]
    loads = [pltpu.make_async_copy(x, landed.at[n], sem_in.at[n]) for n, x in enumerate(pieces[1:])]
    loads.append(pltpu.make_async_copy(pieces[0], widened.at[3], sem_in.at[3]))
    for load in loads:
        load.start()
    stores = []
    for n, load in enumerate(loads):
        load.wait()
        if n < 3:
            widened[n] = landed[n].astype(out.dtype)
        target = out.at[where[1] ^ ((n + 1) % 4), 0]
        stores.append(pltpu.make_async_copy(widened.at[n], target, sem_out.at[n]))
        stores[n].start()
    for store in stores:
        store.wait()


def arrange(where, pieces, kind):
    seg_len = pieces[1].shape[0]
    return pl.pallas_call(
        arrange_kernel,
        grid_spec=pltpu.PrefetchScalarGridSpec(
            num_scalar_prefetch=1,
            grid=(1,),
            in_specs=[pl.BlockSpec(memory_space=pl.ANY)] * 4,
            out_specs=pl.BlockSpec(memory_space=pl.ANY),
            scratch_shapes=[
                pltpu.VMEM((3, seg_len, D), BF16),
                pltpu.VMEM((4, seg_len, D), kind),
                pltpu.SemaphoreType.DMA((4,)),
                pltpu.SemaphoreType.DMA((4,)),
            ],
        ),
        out_shape=jax.ShapeDtypeStruct((4, 1, seg_len, D), kind),
        compiler_params=pltpu.CompilerParams(vmem_limit_bytes=VMEM_LIMIT),
        cost_estimate=NEXT_TO_NOTHING,
        name="arrange",
    )(where, *pieces)


def partner(value, axis, mask):
    pairs = [(source, source ^ mask) for source in range(lax.axis_size(axis))]
    return lax.ppermute(value, axis, pairs)


def over_core(value):
    return partner(value, "cam", 1)


def over_x(value):
    return partner(value, "cam", 2)


def over_y(value):
    return partner(value, "dp", 1)


def over_z(value, apart_by):
    return partner(value, "dp", 2 * apart_by)


def stages_of(order):
    return (over_x, over_y) if order == BY_X else (over_y, over_x)


def by_blocks():
    return lax.axis_size("dp") * lax.axis_size("cam") == BLOCKS


def doubled(held, stage, axis=0):
    return jnp.concatenate([held, stage(held)], axis=axis)


def gather_plain(shard, order):
    at = shard.ndim - 2
    full = lax.all_gather(shard, ("dp", "cam"), axis=at, tiled=True)
    full = full.reshape(*full.shape[:at], 2, 2, 2, 2, 2, ROWS, full.shape[-1])
    places = ["Zzyx".index(name) + at for name in order]
    full = jnp.moveaxis(full, (at + 4, *places), (0, *range(at + 1, at + 5)))
    full = full.reshape(2, *shard.shape[:at], HALF, *full.shape[-2:])
    return full[0], full[1]


def split_sides(shard, order, at):
    return tuple(tuple(jnp.split(x, 2, axis=at)) for x in gather_plain(shard, order))


def scatter_plain(sides, order):
    full = jnp.stack(sides).reshape(2, 2, 2, 2, 2, ROWS, sides[0].shape[-1])
    places = (4, *("Zzyx".index(name) for name in order))
    full = jnp.moveaxis(full, range(5), places).reshape(D, sides[0].shape[-1])
    return lax.psum_scatter(full.astype(F32), ("dp", "cam"), scatter_dimension=0, tiled=True)


def halve(held, received):
    half = held.shape[0] // 2

    def part(rows):
        return (held[rows].astype(F32) + received[rows].astype(F32)).astype(BF16)

    return part(slice(0, half)), part(slice(half, None))


def over_low_z(value):
    return over_z(value, 1)


def over_high_z(value):
    return over_z(value, 2)


def add_low(mine, other):
    return mine.astype(F32) + other.astype(F32)


def together(*values):
    return lax.optimization_barrier(values)


def joined(left, right):
    return jnp.concatenate([left, right], axis=-1)


def add_parts(mine, other):
    return two_parts(of_parts(mine[0]) + of_parts(other[0]))[None]


def after(value, *others):
    return lax.optimization_barrier((value, *others))[0]


def local(
    tokens,
    out_grad,
    joint_state,
    joint_mask,
    attn_master,
    attn_first,
    attn_second,
    attn_average,
    ffn_master,
    ffn_first,
    ffn_second,
    ffn_average,
    small_params,
    small_first,
    small_second,
    small_average,
):
    cam_index = lax.axis_index("cam")
    slot, group_index = cam_index % 4, cam_index // 4
    items_here, _, seg_len, _ = tokens.shape
    assert items_here == 4
    device = lax.axis_index("dp") * lax.axis_size("cam") + cam_index if by_blocks() else 0
    where = jnp.stack([jnp.int32(device), jnp.int32(slot)])

    def piece_for(array, n):
        return lax.dynamic_index_in_dim(array, slot ^ n, 0, keepdims=False)

    def trade(pieces):
        return [pieces[0]] + [partner(pieces[n], "cam", n) for n in range(1, 4)]

    blocks = by_blocks()
    sequence = trade([piece_for(tokens[:, 0], n) for n in range(4)])
    attn_low = attn_master.astype(BF16)
    ffn_low = ffn_master.astype(BF16)
    small = small_params
    if blocks:
        held = doubled(attn_low[:, None], over_high_z, 1)
        held, ffn_low = together(held, ffn_low)
        wide = doubled(ffn_low[:, None], over_high_z, 1)
        held, small, sequence[2] = together(doubled(held, over_low_z, 1), small, sequence[2])
        qk, vo = doubled(held[:2], over_y, 1), doubled(held[2:], over_x, 1)
        qk, vo, wide, *sequence = together(qk, vo, wide, *sequence)
        qk, vo = (qk, over_x(qk)), (vo, over_y(vo))
        wide = doubled(wide, over_low_z, 1)
        qk = (qk, tuple(over_core(x) for x in qk))
        vo = (vo, tuple(over_core(x) for x in vo))
        up, down = after(wide[0], *qk[1], *vo[1]), after(wide[1], *qk[1], *vo[1])
    else:
        qk, vo = split_sides(attn_low[:2], BY_X, 1), split_sides(attn_low[2:], BY_Y, 1)
        up, down = split_sides(ffn_low[0], BY_X, 0), split_sides(ffn_low[1], BY_Y, 0)

    vectors = small[: (8 + NJ) * D].reshape(8 + NJ, D)
    hidden_bias = small[(8 + NJ) * D :].reshape(1, -1)
    active = (joint_state * joint_mask.astype(F32))[slot, group_index].reshape(NJ, 1)

    here = after(where, *flat(up), *flat(down)) if not blocks else where
    if blocks:
        here, up, down = together(where, up, down)
        up, down = doubled(up, over_y), doubled(down, over_x)
    rounded, top_rows, *heads = attend(0, 1, here, [*sequence, active], qk, vo, vectors, seg_len)
    here = where
    if blocks:
        here, up, down, *heads = together(where, up, down, *heads)
        up, down = (up, over_x(up)), (down, over_y(down))
        far = over_core(up[0]), over_core(down[0])
    *heads, logs = attend(1, PAIRS - 1, here, [rounded, *heads], qk, vo, vectors, seg_len)
    here = where
    if blocks:
        here, up_got, down_got, logs, *far = together(where, up[1], down[1], logs, *far)
        up = ((up[0], up_got), (far[0], over_core(up_got)))
        down = ((down[0], down_got), (far[1], over_core(down_got)))
    h1, normed, y1 = project(here, rounded, top_rows, heads[3], vo, vectors)
    cotangents = trade([after(piece_for(out_grad[:, 0], n), y1) for n in range(4)])
    gated, slope, forward = feed_forward(where, y1, up, down, hidden_bias)
    *results, dh2, df, grads_two, down_keep, down_send = second_norm(
        where, normed, forward, gated, vectors, cotangents
    )
    outputs = trade(results)
    down_got = over_core(down_send) if blocks else down_send
    up_keep, up_send, hidden_grad, above = feed_back(where, dh2, df, y1, slope, up, down)
    here, up_send, down_got, *outputs = together(where, up_send, down_got, *outputs)

    def back(base, pairs, here, before, filled, small=()):
        return attend_back(
            base, pairs, here, heads, da, logs, rounded, before, qk, vo, filled, small
        )

    up_got = up_send
    if blocks:
        up_got = over_core(up_send)
        down_keep, down_send = halve(down_keep, down_got)
        up_keep, up_send = halve(up_keep, up_got)
        here, up_send, down_send = together(here, up_send, down_send)
        up_got, down_got = over_x(up_send), over_y(down_send)
    dh1, da, grads_one, out_keep, out_send = first_norm_back(here, above, h1, heads[3], vo, vectors)
    *a_sides, bias_0, before = back(0, 1, where, dh1, ())
    here = where
    if blocks:
        up_got, down_got, before = together(up_got, down_got, before)
        up_keep, up_send = halve(up_keep, up_got)
        down_keep, down_send = halve(down_keep, down_got)
        here, up_send, down_send = together(where, up_send, down_send)
        up_got, down_got = over_y(up_send), over_x(down_send)
    a_keep, a_send, bias_1, before = back(1, 1, here, before, a_sides)
    here = where
    if blocks:
        up_got, down_got, before = together(up_got, down_got, before)
        up_keep, up_send = halve(up_keep, up_got)
        down_keep, down_send = halve(down_keep, down_got)
        keep, send = jnp.stack([up_keep, down_keep], 1), jnp.stack([up_send, down_send], 1)
        here, send, a_send, out_send = together(where, send, a_send, out_send)
        got, a_got, out_got = over_low_z(send), over_core(a_send), over_core(out_send)
    b_keep, b_send, bias_2, before = back(2, 1, here, before, ())
    here = where
    if blocks:
        got, a_got, out_got, before = together(got, a_got, out_got, before)
        keep, send = halve(keep, got)
        a_keep, a_send = halve(joined(a_keep, out_keep), joined(a_got, out_got))
        here, send, a_send = together(where, send, a_send)
        got, a_got = over_high_z(send), over_y(a_send)
    small = (bias_0, bias_1, bias_2, grads_one, grads_two, active, hidden_grad)
    b_keep, b_send, _, own, *sends, tiny = back(3, 1, here, before, (b_keep, b_send), small)
    if blocks:
        got, a_got, b_send, tiny, *sends = together(got, a_got, b_send, tiny, *sends)
        grad_pieces = trade([own, *sends])
        b_got, tiny_got = together(over_core(b_send), over_core(tiny))
        b_keep, b_send = halve(b_keep, b_got)
        tiny = add_parts(tiny, tiny_got)
        b_send, tiny, keep, got = together(b_send, tiny, keep, got)
        ffn_shard = add_low(keep[0], got[0])
        b_got, tiny_got, ffn_shard, grad_pieces[2] = together(
            over_y(b_send), over_y(tiny), ffn_shard, grad_pieces[2]
        )
        a_keep, a_send = halve(a_keep, a_got)
        b_keep, b_send = halve(b_keep, b_got)
        keep, send = joined(a_keep, b_keep), joined(a_send, b_send)
        tiny = add_parts(tiny, tiny_got)
        send, outputs = together(jnp.concatenate([send, tiny]), together(*outputs))
        got, block_output, *grad_pieces = together(
            over_low_z(send), arrange(where, outputs, BF16), *grad_pieces
        )
        keep, send = halve(keep, got[:-1])
        tiny = add_parts(tiny, got[-1:])
        send, *grad_pieces = together(jnp.concatenate([send, tiny]), *grad_pieces)
        got, input_grad = together(over_high_z(send), arrange(where, grad_pieces, F32))
        keep, send = halve(keep, got[:-1])
        tiny = add_parts(tiny, got[-1:])
        got = over_x(jnp.concatenate([send, tiny]))
        attn_shard = add_low(keep[0], got[0])
        small_total = of_parts(tiny[0]) + of_parts(got[-1])
    else:
        grad_pieces = trade([own, *sends])
        small_total = lax.psum(of_parts(tiny[0]), ("dp", "cam"))
        ffn_shard = jnp.stack(
            [scatter_plain((up_keep, up_got), BY_X), scatter_plain((down_keep, down_got), BY_Y)]
        )
        attn_keep = joined(joined(a_keep, out_keep), b_keep)
        attn_send = joined(joined(a_send, out_send), b_send)
        attn_shard = scatter_plain((attn_keep, attn_send), BY_YZ)
        block_output, input_grad = arrange(where, outputs, BF16), arrange(where, grad_pieces, F32)
    small_total = small_total.reshape(-1)[: small_params.size]

    rows_here = attn_master.shape[1]
    split = 3 * PAIR * SIDE_PAIRS
    proj_grad = joined(attn_shard[:, :split], attn_shard[:, split + D :])
    proj_grad = jnp.moveaxis(proj_grad.reshape(rows_here, PAIRS, 3, PAIR), 2, 0).reshape(3, rows_here, D)
    attn_shard = jnp.concatenate([proj_grad, attn_shard[None, :, split : split + D]])
    new_attn = adam_update(
        attn_master, attn_shard, attn_first, attn_second, attn_average, rate_matrix, decay_matrix
    )
    new_ffn = adam_update(
        ffn_master, ffn_shard, ffn_first, ffn_second, ffn_average, rate_matrix, decay_matrix
    )
    new_small = adam_update(
        small_params, small_total, small_first, small_second, small_average, rate_small, 0.0
    )
    return (block_output, input_grad, *new_attn, *new_ffn, *new_small)


def solution(mesh):
    in_specs = (
        P("dp", "cam", None, None),
        P("dp", "cam", None, None),
        P("dp", None, None),
        P("dp", None, None),
        P(None, ("dp", "cam"), None),
        P(None, ("dp", "cam"), None),
        P(None, ("dp", "cam"), None),
        P(None, ("dp", "cam"), None),
        P(None, ("dp", "cam"), None),
        P(None, ("dp", "cam"), None),
        P(None, ("dp", "cam"), None),
        P(None, ("dp", "cam"), None),
        P(),
        P(),
        P(),
        P(),
    )
    out_specs = (
        P("dp", "cam", None, None),
        P("dp", "cam", None, None),
        P(None, ("dp", "cam"), None),
        P(None, ("dp", "cam"), None),
        P(None, ("dp", "cam"), None),
        P(None, ("dp", "cam"), None),
        P(None, ("dp", "cam"), None),
        P(None, ("dp", "cam"), None),
        P(None, ("dp", "cam"), None),
        P(None, ("dp", "cam"), None),
        P(),
        P(),
        P(),
        P(),
    )
    return jax.shard_map(local, mesh=mesh, in_specs=in_specs, out_specs=out_specs, check_vma=False)
```

```python
import functools

import jax
import jax.numpy as jnp
from jax import lax
from jax.experimental import pallas as pl
from jax.experimental.pallas import tpu as pltpu
from jax.sharding import PartitionSpec as P

D = 512
HEADS = 8
NJ = 14
ADAM_STEP = 10
HD = 64
PAIR = 2 * HD
PAIRS = HEADS // 2
BLOCKS = 32
ROWS = D // BLOCKS
HALF = BLOCKS // 2
CHUNK = 640
SIDE_PAIRS = 2
ROW_STEPS = 2

norm_eps = 1e-05
beta_first = 0.5
beta_second = 0.5
adam_eps = 1e-08
rate_matrix = 0.02
rate_small = 0.05
decay_matrix = 0.1
ema_decay = 0.75
log2e = 1.4426950408889634
score_scale = HD**-0.5
F32 = jnp.float32
BF16 = jnp.bfloat16
VMEM_LIMIT = 60 * 2**20
NEXT_TO_NOTHING = pl.CostEstimate(flops=1, bytes_accessed=1, transcendentals=0)


def adam_update(master, grad_total, first_old, second_old, average_old, rate, decay):
    first_new = beta_first * first_old + (1.0 - beta_first) * grad_total
    second_new = beta_second * second_old + (1.0 - beta_second) * grad_total * grad_total
    first_hat = first_new / (1.0 - beta_first**ADAM_STEP)
    second_hat = second_new / (1.0 - beta_second**ADAM_STEP)
    master_new = master - rate * (first_hat / (jnp.sqrt(second_hat) + adam_eps) + decay * master)
    average_new = ema_decay * average_old + (1.0 - ema_decay) * master_new
    return (master_new, first_new, second_new, average_new)


def dot(left, right, left_dim, right_dim):
    return lax.dot_general(
        left, right, (((left_dim,), (right_dim,)), ((), ())), preferred_element_type=F32
    )


DEVICE_BITS = {"x": 2, "y": 4, "z": 8, "Z": 16}
BY_X, BY_Y, BY_YZ = "xyzZ", "yxzZ", "yzZx"


def apart(position, order, core):
    bits = (DEVICE_BITS[name] for n, name in enumerate(order) if position >> (3 - n) & 1)
    return core + sum(bits)


def row_blocks(device, order):
    for core in range(2):
        for position in range(HALF):
            start = (device ^ apart(position, order, core)) * ROWS
            yield core, position, pl.ds(pl.multiple_of(start, ROWS), ROWS)


def put_rows(target, sides, order, device, part=None, cols=slice(None)):
    for core, position, rows in row_blocks(device, order):
        which, at = divmod(position, HALF // len(sides[core]))
        array = sides[core][which]
        target[rows, :] = array[at] if part is None else array[part, at, :, cols]


def take_rows(source, sides, order, device):
    for core, position, rows in row_blocks(device, order):
        sides[core][position] = source[rows, :].astype(BF16)


def mean_last(values):
    return jnp.sum(values, axis=-1, keepdims=True) * (1.0 / D)


def normal_rows(values):
    centred = values - mean_last(values)
    inverse = lax.rsqrt(mean_last(centred * centred) + norm_eps)
    return centred * inverse, inverse


def normal_back(normal, inverse, grad):
    return inverse * (grad - mean_last(grad) - normal * mean_last(grad * normal))


def column_sum(values):
    return jnp.sum(values, axis=0, keepdims=True)


def turn_row(row):
    shape = (row.shape[1], row.shape[1])
    same = lax.broadcasted_iota(jnp.int32, shape, 0) == lax.broadcasted_iota(jnp.int32, shape, 1)
    return jnp.sum(jnp.where(same, row, 0.0), axis=1, keepdims=True)


def spread_heads(values, other):
    lane = lax.broadcasted_iota(jnp.int32, (1, PAIR), 1)
    low = lane < HD
    return jnp.where(low, values, other), jnp.where(low, other, values)


def attend_kernel(base, seg_len, where, *refs):
    first = base == 0
    if first:
        pieces, active, refs = refs[:4], refs[4], refs[5:]
    else:
        rounded, refs = refs[0], refs[6:]
    qk_sides, vo_sides = (refs[0:2], refs[2:4]), (refs[4:6], refs[6:8])
    vectors, refs = refs[8], refs[9:]
    if first:
        rounded, top_rows, refs = refs[0], refs[1], refs[2:]
    q_out, k_out, v_out, a_out, l_out, weight, logs = refs
    device, slot = where[0], where[1]

    if first:

        @pl.when(pl.program_id(0) == 0)
        def _():
            for k in range(4):
                start = pl.multiple_of((slot ^ k) * seg_len, 16)
                rounded[pl.ds(start, seg_len), :] = pieces[k][...]
            joint = column_sum(turn_row(active[...]) * vectors[8:, :])
            top = rounded[:16, :].astype(F32)
            at = lax.broadcasted_iota(jnp.int32, (16, 1), 0)
            top = jnp.where(at == 1, top + joint, top)
            top_rows[...] = top[:8]
            rounded[:16, :] = top.astype(BF16)

    put_rows(weight.at[:, :PAIR], qk_sides, BY_X, device, 0)
    put_rows(weight.at[:, PAIR : 2 * PAIR], qk_sides, BY_X, device, 1)
    put_rows(weight.at[:, 2 * PAIR :], vo_sides, BY_Y, device, 0)
    cols = pl.ds(pl.multiple_of((pl.program_id(0) + base) * PAIR, PAIR), PAIR)
    bias_q, bias_v = vectors[0:1, cols], vectors[1:2, cols]
    projected = dot(rounded[...], weight[...], 1, 0)
    q_out[...] = (projected[:, :PAIR] + bias_q).astype(BF16)
    keys = projected[:, PAIR : 2 * PAIR].astype(BF16)
    values = (projected[:, 2 * PAIR :] + bias_v).astype(BF16)
    k_out[...] = keys
    v_out[...] = values
    lane = lax.broadcasted_iota(jnp.int32, (1, PAIR), 1)
    low = lane < HD
    value_heads = spread_heads(values, jnp.ones_like(values))
    scale = log2e * score_scale
    for step in range(4):
        rows = pl.ds(step * seg_len, seg_len)
        query = q_out[rows, :]
        mixed, tops = [], []
        for query_head, value_head in zip(spread_heads(query, jnp.zeros_like(query)), value_heads):
            scores = dot(query_head, keys, 1, 1)
            top = jnp.max(scores, axis=1, keepdims=True) * scale
            probs = jnp.exp2(scores * scale - top).astype(BF16)
            mixed.append(dot(probs, value_head, 1, 0))
            tops.append(top)
        total = pltpu.roll(jnp.where(low, mixed[1], mixed[0]), HD, 1)
        a_out[rows, :] = (jnp.where(low, mixed[0], mixed[1]) / total).astype(BF16)
        logs[rows, :] = jnp.where(low, tops[0], tops[1]) + jnp.log2(total)
    turned = logs[...].T
    l_out[0:1, :] = turned[0:1]
    l_out[1:2, :] = turned[HD : HD + 1]


def gate_both(values):
    def low(constant):
        return jnp.asarray(constant, BF16)

    values = values.astype(BF16)
    size = jnp.abs(values)
    fraction = low(1.0) / (low(1.0) + low(0.3275911 * 0.5**0.5) * size)
    bell = jnp.exp2(values * values * low(-0.5 * log2e))
    series = low(0.5 * 1.061405429) * fraction - low(0.5 * 1.453152027)
    series = series * fraction + low(0.5 * 1.421413741)
    series = series * fraction - low(0.5 * 0.284496736)
    series = series * fraction + low(0.5 * 0.254829592)
    tail = series * fraction * bell
    bend = size * bell * low(0.3989422804014327) - tail
    slope = jnp.where(values > low(0.0), low(1.0) + bend, -bend)
    return jnp.maximum(values, low(0.0)) - size * tail, slope


def project_kernel(seg_len, where, *refs):
    rounded, top_rows, mixed, vo_sides, vectors = *refs[:3], (refs[3:5], refs[5:7]), refs[7]
    h1_out, normed_out, y1_out, w_out = refs[8:]
    out_scale = (4 * seg_len / 3.0) ** 0.5

    @pl.when(pl.program_id(0) == 0)
    def _():
        put_rows(w_out, vo_sides, BY_Y, where[0], 0)

    summed = rounded[...].astype(F32)
    top = jnp.where(pl.program_id(0) == 0, top_rows[...], summed[:8])
    summed = jnp.concatenate([top, summed[8:]], axis=0)
    summed = summed + (dot(mixed[...], w_out[...], 1, 0) * out_scale + vectors[2:3, :])
    h1_out[...] = summed
    normal, _ = normal_rows(summed)
    result = normal * vectors[3:4, :] + vectors[4:5, :]
    normed_out[...] = result
    y1_out[...] = result.astype(BF16)


def forward_kernel(seg_len, where, *refs):
    y1, up_sides, down_sides = refs[0], (refs[1:3], refs[3:5]), (refs[5:7], refs[7:9])
    hidden_bias, refs = refs[9], refs[10:]
    g_out, slope_out, total, w_up, w_down = refs
    device = where[0]

    @pl.when(pl.program_id(0) == 0)
    def _():
        total[...] = jnp.zeros_like(total)

    put_rows(w_up, up_sides, BY_X, device)
    put_rows(w_down, down_sides, BY_Y, device)
    for step in range(4):
        rows = pl.ds(step * seg_len, seg_len)
        inner = dot(y1[rows, :], w_up[...], 1, 0) + hidden_bias[...]
        active, slope = gate_both(inner)
        active = active.astype(BF16)
        g_out[rows, :] = active
        slope_out[rows, :] = slope.astype(BF16)
        total[rows, :] += dot(active, w_down[...], 1, 1)


def second_kernel(seg_len, where, *refs):
    normed, forward, active, vectors, cotangents, refs = *refs[:4], refs[4:8], refs[8:]
    pieces, dh2_out, df_out, vector_grads, refs = refs[:4], refs[4], refs[5], refs[6], refs[7:]
    down_grads, df_turned, grad = refs[:2], refs[2], refs[3]
    device, slot = where[0], where[1]

    @pl.when(pl.program_id(0) == 0)
    def _():
        gain_grad = shift_grad = bias_grad = 0.0
        for k in range(4):
            rows = pl.ds(pl.multiple_of((slot ^ k) * seg_len, 16), seg_len)
            normal, inverse = normal_rows(normed[rows, :] + (forward[rows, :] + vectors[5:6, :]))
            pieces[k][...] = (normal * vectors[6:7, :] + vectors[7:8, :]).astype(BF16)
            cotangent = cotangents[k][...].astype(F32)
            gain_grad += column_sum(cotangent * normal)
            shift_grad += column_sum(cotangent)
            middle = normal_back(normal, inverse, cotangent * vectors[6:7, :])
            dh2_out[rows, :] = middle
            rounded = middle.astype(BF16)
            df_out[rows, :] = rounded
            bias_grad += column_sum(rounded.astype(F32))
        vector_grads[0:1, :] = gain_grad
        vector_grads[1:2, :] = shift_grad
        vector_grads[2:3, :] = bias_grad
        df_turned[...] = df_out[...].T

    grad[...] = dot(df_turned[...], active[...], 1, 0)
    take_rows(grad, down_grads, BY_Y, device)


def backward_kernel(seg_len, where, *refs):
    dh2, df, y1, slope, refs = *refs[:4], refs[4:]
    up_sides, down_sides, refs = (refs[0:2], refs[2:4]), (refs[4:6], refs[6:8]), refs[8:]
    up_grads, hidden_grad, total, refs = refs[:2], refs[2], refs[3], refs[4:]
    y1_turned, dz, w_up, w_down, grad = refs
    device = where[0]

    @pl.when(pl.program_id(0) == 0)
    def _():
        y1_turned[...] = y1[...].T
        total[...] = dh2[...]

    put_rows(w_up, up_sides, BY_X, device)
    put_rows(w_down, down_sides, BY_Y, device)
    bias_grad = 0.0
    for step in range(4):
        rows = pl.ds(step * seg_len, seg_len)
        inner = (dot(df[rows, :], w_down[...], 1, 0) * slope[rows, :].astype(F32)).astype(BF16)
        dz[rows, :] = inner
        bias_grad += column_sum(inner.astype(F32))
        total[rows, :] += dot(inner, w_up[...], 1, 1)
    hidden_grad[...] = bias_grad
    grad[...] = dot(y1_turned[...], dz[...], 1, 0)
    take_rows(grad, up_grads, BY_X, device)


def first_kernel(seg_len, where, *refs):
    above_in, h1, mixed, vo_sides, vectors = *refs[:3], (refs[3:5], refs[5:7]), refs[7]
    dh1_out, da_out, vector_grads, grad_sides, w_out, grad = *refs[8:11], refs[11:13], *refs[13:]
    device, step = where[0], pl.program_id(0)
    out_scale = (4 * seg_len / 3.0) ** 0.5

    @pl.when(step == 0)
    def _():
        put_rows(w_out, vo_sides, BY_Y, device, 0)
        vector_grads[...] = jnp.zeros_like(vector_grads)
        grad[...] = jnp.zeros_like(grad)

    normal, inverse = normal_rows(h1[...])
    above = above_in[...]
    vector_grads[0:1, :] += column_sum(above * normal)
    vector_grads[1:2, :] += column_sum(above)
    summed = normal_back(normal, inverse, above * vectors[3:4, :])
    dh1_out[...] = summed
    rounded = summed.astype(BF16)
    vector_grads[2:3, :] += column_sum(rounded.astype(F32))
    da_out[...] = (dot(rounded, w_out[...], 1, 1) * out_scale).astype(BF16)
    grad[...] += dot(mixed[...], rounded, 0, 0) * out_scale

    @pl.when(step == pl.num_programs(0) - 1)
    def _():
        take_rows(grad, grad_sides, BY_YZ, device)


def attend_back_kernel(first, aliased, where, *refs):
    q, k, v, a, da, logs, refs = *refs[:6], refs[6:]
    rounded, (keep, send, parts, bias_grads), refs = refs[0], refs[1 + aliased : 5 + aliased], refs[5 + aliased :]
    if first:
        turned, refs = refs[0], refs[1:]
        turned[...] = rounded[...].T
    else:
        turned = rounded
    query_turned, grad = refs
    seq_len = q.shape[0]

    queries, mixed_grads = q[...], da[...]
    zeros = jnp.zeros_like(queries)
    query_heads = spread_heads(queries, zeros)
    grad_heads = spread_heads(mixed_grads, zeros)
    product = (mixed_grads.astype(F32) * a[...].astype(F32)).T
    inner = (column_sum(product[:HD]), column_sum(product[HD:]))
    start = 0
    while start < seq_len:
        size = min(256, seq_len - start)
        rows = pl.ds(start, size)
        none = jnp.zeros((size, PAIR), BF16)
        key_grad = value_grad = query_grad = 0.0
        heads = zip(spread_heads(k[rows, :], none), spread_heads(v[rows, :], none))
        for h, (key_head, value_head) in enumerate(heads):
            scores = dot(key_head, queries, 1, 1)
            probs = jnp.exp2(scores * (log2e * score_scale) - logs[h : h + 1, :])
            grads = (probs * (dot(value_head, mixed_grads, 1, 1) - inner[h])).astype(BF16)
            value_grad += dot(probs.astype(BF16), grad_heads[h], 1, 0)
            key_grad += dot(grads, query_heads[h], 1, 0)
            query_grad += dot(key_head, grads, 0, 0)
        parts[rows, PAIR : 2 * PAIR] = (key_grad * score_scale).astype(BF16)
        parts[rows, 2 * PAIR :] = value_grad.astype(BF16)
        if start == 0:
            query_turned[...] = query_grad
        else:
            query_turned[...] += query_grad
        start += size
    parts[:, :PAIR] = (query_turned[...].T * score_scale).astype(BF16)
    bias_grads[0:1, :] = column_sum(parts[:, :PAIR].astype(F32))
    bias_grads[1:2, :] = column_sum(parts[:, 2 * PAIR :].astype(F32))
    grad[...] = dot(turned[...], parts[...], 1, 0)
    take_rows(grad, (keep, send), BY_YZ, where[0])


def input_back_kernel(seg_len, where, *refs):
    dh1, parts, qk_sides, vo_sides = refs[0], refs[1], (refs[2:4], refs[4:6]), (refs[6:8], refs[8:10])
    small_parts, own, sends, small_out = refs[10:18], refs[18], refs[19:22], refs[22]
    weight, total, joined = refs[23:]
    device, slot, step = where[0], where[1], pl.program_id(0)
    size = dh1.shape[0]

    @pl.when(step == 0)
    def _():
        for pair in range(PAIRS):
            for part, (sides, order, n) in enumerate(
                ((qk_sides, BY_X, 0), (qk_sides, BY_X, 1), (vo_sides, BY_Y, 0))
            ):
                start = (3 * pair + part) * PAIR
                cols = pl.ds(pair * PAIR, PAIR)
                put_rows(weight.at[:, start : start + PAIR], sides, order, device, n, cols)

    rows = pl.ds(pl.multiple_of(step * size, 16), size)
    total[rows, :] = dh1[...] + dot(parts[...], weight[...], 1, 1)

    @pl.when(step == pl.num_programs(0) - 1)
    def _():
        join_small(joined, small_parts, total[1:2, :])
        small_out[0] = two_parts(joined[...])
        for n in range(4):
            piece = total[pl.ds(pl.multiple_of((slot ^ n) * seg_len, 16), seg_len), :]
            if n == 0:
                own[...] = piece
            else:
                sends[n - 1][...] = piece.astype(BF16)


def call(kernel, name, where, grid, operands, results, scratch, aliases=None):
    def spec(block, index):
        if block is None:
            return pl.BlockSpec(memory_space=pl.ANY)
        return pl.BlockSpec(block, lambda i, _: index(i))

    return pl.pallas_call(
        kernel,
        grid_spec=pltpu.PrefetchScalarGridSpec(
            num_scalar_prefetch=1,
            grid=(grid,),
            in_specs=[spec(block, index) for _, block, index in operands],
            out_specs=[spec(block, index) for _, block, index in results],
            scratch_shapes=[pltpu.VMEM(shape, kind) for shape, kind in scratch],
        ),
        out_shape=[shape for shape, _, _ in results],
        input_output_aliases={source + 1: target for source, target in (aliases or {}).items()},
        compiler_params=pltpu.CompilerParams(vmem_limit_bytes=VMEM_LIMIT),
        cost_estimate=NEXT_TO_NOTHING,
        name=name,
    )(where, *(x for x, _, _ in operands))


def whole(x):
    return (x, x.shape, lambda i: (0,) * len(x.shape))


def shape_of(shape, kind):
    return jax.ShapeDtypeStruct(shape, kind)


def whole_out(shape, kind):
    return whole(shape_of(shape, kind))


def flat(sides):
    return [x for side in sides for x in side]


def pair_weights(qk, vo, base):
    def spec(x, parts):
        return (x, (parts, x.shape[1], ROWS, PAIR), lambda i: (0, 0, 0, i + base))

    return [spec(x, 2) for x in flat(qk)] + [spec(x, 1) for x in flat(vo)]


def attend(base, pairs, where, source, qk, vo, vectors, seg_len):
    seq_len = 4 * seg_len
    first = base == 0

    def column(x):
        return (x, (seq_len, PAIR), lambda i: (0, i + base))

    operands = [whole(x) for x in (source if first else source[:1])]
    operands += [] if first else [(x, None, None) for x in source[1:]]
    operands += pair_weights(qk, vo, base) + [whole(vectors)]
    results = [whole_out((seq_len, D), BF16), whole_out((8, D), F32)] if first else []
    results += [column(shape_of((seq_len, D), BF16))] * 4
    logs = shape_of((PAIRS, 2, seq_len), F32)
    results += [(logs, (None, 2, seq_len), lambda i: (i + base, 0, 0))]
    scratch = [((D, 3 * PAIR), BF16), ((seq_len, PAIR), F32)]
    return call(
        functools.partial(attend_kernel, base, seg_len),
        f"attend_{base}",
        where,
        pairs,
        operands,
        results,
        scratch,
        {} if first else {1 + n: n for n in range(5)},
    )


def by_chunk(x):
    if x.ndim == 3:
        return (x, (x.shape[0], ROWS, CHUNK), lambda i: (0, 0, i))
    return (x, (x.shape[0], CHUNK), lambda i: (0, i))


def out_weight(vo):
    return [(x, (1, x.shape[1], ROWS, D), lambda i: (1, 0, 0, 0)) for x in flat(vo)]


def by_rows(x):
    return (x, (x.shape[0] // ROW_STEPS, x.shape[1]), lambda i: (i, 0))


def project(where, rounded, top_rows, mixed, vo, vectors):
    seq_len = rounded.shape[0]
    return call(
        functools.partial(project_kernel, seq_len // 4),
        "project",
        where,
        ROW_STEPS,
        [by_rows(rounded), whole(top_rows), by_rows(mixed), *out_weight(vo), whole(vectors)],
        [by_rows(shape_of((seq_len, D), kind)) for kind in (F32, F32, BF16)],
        [((D, D), BF16)],
    )


def feed_forward(where, y1, up, down, hidden_bias):
    seq_len = y1.shape[0]
    hidden = up[0][0].shape[-1]
    wide = by_chunk(shape_of((seq_len, hidden), BF16))
    return call(
        functools.partial(forward_kernel, seq_len // 4),
        "feed_forward",
        where,
        hidden // CHUNK,
        [whole(y1)] + [by_chunk(x) for x in (*flat(up), *flat(down), hidden_bias)],
        [wide, wide, whole_out((seq_len, D), F32)],
        [((D, CHUNK), BF16)] * 2,
    )


def second_norm(where, normed, forward, active, vectors, cotangents):
    seq_len, hidden = active.shape
    seg_len = seq_len // 4
    operands = [whole(normed), whole(forward), by_chunk(active), whole(vectors)]
    results = [whole_out((seg_len, D), BF16)] * 4
    results += [whole_out((seq_len, D), F32), whole_out((seq_len, D), BF16), whole_out((8, D), F32)]
    results += [by_chunk(shape_of((HALF, ROWS, hidden), BF16))] * 2
    return call(
        functools.partial(second_kernel, seg_len),
        "second_norm",
        where,
        hidden // CHUNK,
        operands + [whole(x) for x in cotangents],
        results,
        [((D, seq_len), BF16), ((D, CHUNK), F32)],
    )


def feed_back(where, dh2, df, y1, slope, up, down):
    seq_len, hidden = slope.shape
    operands = [whole(dh2), whole(df), whole(y1)] + [by_chunk(x) for x in (slope, *flat(up), *flat(down))]
    results = [by_chunk(shape_of((HALF, ROWS, hidden), BF16))] * 2
    results += [by_chunk(shape_of((1, hidden), F32)), whole_out((seq_len, D), F32)]
    scratch = [((D, seq_len), BF16), ((seq_len, CHUNK), BF16)]
    scratch += [((D, CHUNK), BF16)] * 2 + [((D, CHUNK), F32)]
    return call(
        functools.partial(backward_kernel, seq_len // 4),
        "feed_back",
        where,
        hidden // CHUNK,
        operands,
        results,
        scratch,
    )


def first_norm_back(where, above, h1, mixed, vo, vectors):
    seq_len = h1.shape[0]
    results = [by_rows(shape_of((seq_len, D), kind)) for kind in (F32, BF16)]
    results += [whole_out((8, D), F32)]
    results += [whole_out((HALF, ROWS, D), BF16)] * 2
    return call(
        functools.partial(first_kernel, seq_len // 4),
        "first_norm_back",
        where,
        ROW_STEPS,
        [by_rows(x) for x in (above, h1, mixed)] + [*out_weight(vo), whole(vectors)],
        results,
        [((D, D), BF16), ((D, D), F32)],
    )


def attend_back(pair, where, heads, da, logs, rounded, sides=(), parts=()):
    first = pair == 0
    seq_len = da.shape[0]
    operands = [(x, (seq_len, PAIR), lambda i: (0, pair)) for x in (*heads, da)]
    operands += [(logs, (None, 2, seq_len), lambda i: (pair, 0, 0)), whole(rounded)]
    aliases = {len(operands) + n: 2 - len(sides) + n for n in range(len(sides))}
    aliases |= {len(operands) + len(sides) + n: 2 for n in range(len(parts))}
    operands += [(x, None, None) for x in (*sides, *parts)]
    side = shape_of((HALF, ROWS, 3 * PAIR * SIDE_PAIRS), BF16)
    results = [(side, (HALF, ROWS, 3 * PAIR), lambda i: (0, 0, pair % SIDE_PAIRS))] * 2
    results += [(shape_of((seq_len, 3 * D), BF16), (seq_len, 3 * PAIR), lambda i: (0, pair))]
    results += [whole_out((8, PAIR), F32)]
    results += [whole_out((D, seq_len), BF16)] if first else []
    return call(
        functools.partial(attend_back_kernel, first, len(sides) + len(parts)),
        f"attend_back_{pair}",
        where,
        1,
        operands,
        results,
        [((PAIR, seq_len), F32), ((D, 3 * PAIR), F32)],
        aliases,
    )


def input_back(where, dh1, parts, qk, vo, small):
    seq_len = dh1.shape[0]
    seg_len = seq_len // 4
    operands = [by_rows(dh1), by_rows(parts), *(whole(x) for x in flat(qk))]
    operands += [(x, (1, *x.shape[1:]), lambda i: (0, 0, 0, 0)) for x in flat(vo)]
    results = [whole_out((seg_len, D), F32)] + [whole_out((seg_len, D), BF16)] * 3
    return call(
        functools.partial(input_back_kernel, seg_len),
        "input_back",
        where,
        ROW_STEPS,
        operands + [whole(x) for x in small],
        results + [whole_out((1, ROWS, 4 * D), BF16)],
        [((D, 3 * D), BF16), ((seq_len, D), F32), ((ROWS // 2, 4 * D), F32)],
    )


def join_small(joined, parts, top):
    *biases, first, second, active, hidden = parts
    units = [x[n : n + 1, :] for n in range(2) for x in biases]
    units += [first[n : n + 1, :] for n in (2, 0, 1)] + [second[n : n + 1, :] for n in (2, 0, 1)]
    by_joint = turn_row(active[...]) * top
    units += [by_joint[n : n + 1, :] for n in range(NJ)] + [hidden[...]]
    joined[...] = jnp.zeros_like(joined)
    at, width = 0, joined.shape[1]
    for unit in units:
        taken = 0
        while taken < unit.shape[1]:
            row, column = divmod(at, width)
            size = min(width - column, unit.shape[1] - taken)
            joined[row : row + 1, column : column + size] = unit[:, taken : taken + size]
            taken, at = taken + size, at + size


def two_parts(values):
    high = lax.reduce_precision(values, 8, 7)
    return jnp.concatenate([high, lax.reduce_precision(values - high, 8, 7)], axis=0).astype(BF16)


def of_parts(parts):
    half = parts.shape[0] // 2
    return parts[:half].astype(F32) + parts[half:].astype(F32)


def arrange_kernel(where, *refs):
    pieces, out, landed, widened, sem_in, sem_out = refs[:4], *refs[4:]
    loads = [pltpu.make_async_copy(x, landed.at[n], sem_in.at[n]) for n, x in enumerate(pieces[1:])]
    loads.append(pltpu.make_async_copy(pieces[0], widened.at[3], sem_in.at[3]))
    for load in loads:
        load.start()
    stores = []
    for n, load in enumerate(loads):
        load.wait()
        if n < 3:
            widened[n] = landed[n].astype(out.dtype)
        target = out.at[where[1] ^ ((n + 1) % 4), 0]
        stores.append(pltpu.make_async_copy(widened.at[n], target, sem_out.at[n]))
        stores[n].start()
    for store in stores:
        store.wait()


def arrange(where, pieces, kind):
    seg_len = pieces[1].shape[0]
    return pl.pallas_call(
        arrange_kernel,
        grid_spec=pltpu.PrefetchScalarGridSpec(
            num_scalar_prefetch=1,
            grid=(1,),
            in_specs=[pl.BlockSpec(memory_space=pl.ANY)] * 4,
            out_specs=pl.BlockSpec(memory_space=pl.ANY),
            scratch_shapes=[
                pltpu.VMEM((3, seg_len, D), BF16),
                pltpu.VMEM((4, seg_len, D), kind),
                pltpu.SemaphoreType.DMA((4,)),
                pltpu.SemaphoreType.DMA((4,)),
            ],
        ),
        out_shape=jax.ShapeDtypeStruct((4, 1, seg_len, D), kind),
        compiler_params=pltpu.CompilerParams(vmem_limit_bytes=VMEM_LIMIT),
        cost_estimate=NEXT_TO_NOTHING,
        name="arrange",
    )(where, *pieces)


def partner(value, axis, mask):
    pairs = [(source, source ^ mask) for source in range(lax.axis_size(axis))]
    return lax.ppermute(value, axis, pairs)


def over_core(value):
    return partner(value, "cam", 1)


def over_x(value):
    return partner(value, "cam", 2)


def over_y(value):
    return partner(value, "dp", 1)


def over_z(value, apart_by):
    return partner(value, "dp", 2 * apart_by)


def stages_of(order):
    return (over_x, over_y) if order == BY_X else (over_y, over_x)


def by_blocks():
    return lax.axis_size("dp") * lax.axis_size("cam") == BLOCKS


def doubled(held, stage, axis=0):
    return jnp.concatenate([held, stage(held)], axis=axis)


def gather_plain(shard, order):
    at = shard.ndim - 2
    full = lax.all_gather(shard, ("dp", "cam"), axis=at, tiled=True)
    full = full.reshape(*full.shape[:at], 2, 2, 2, 2, 2, ROWS, full.shape[-1])
    places = ["Zzyx".index(name) + at for name in order]
    full = jnp.moveaxis(full, (at + 4, *places), (0, *range(at + 1, at + 5)))
    full = full.reshape(2, *shard.shape[:at], HALF, *full.shape[-2:])
    return full[0], full[1]


def split_sides(shard, order, at):
    return tuple(tuple(jnp.split(x, 2, axis=at)) for x in gather_plain(shard, order))


def scatter_plain(sides, order):
    full = jnp.stack(sides).reshape(2, 2, 2, 2, 2, ROWS, sides[0].shape[-1])
    places = (4, *("Zzyx".index(name) for name in order))
    full = jnp.moveaxis(full, range(5), places).reshape(D, sides[0].shape[-1])
    return lax.psum_scatter(full.astype(F32), ("dp", "cam"), scatter_dimension=0, tiled=True)


def halve(held, received):
    half = held.shape[0] // 2

    def part(rows):
        return (held[rows].astype(F32) + received[rows].astype(F32)).astype(BF16)

    return part(slice(0, half)), part(slice(half, None))


def over_low_z(value):
    return over_z(value, 1)


def over_high_z(value):
    return over_z(value, 2)


def add_low(mine, other):
    return mine.astype(F32) + other.astype(F32)


def together(*values):
    return lax.optimization_barrier(values)


def joined(left, right):
    return jnp.concatenate([left, right], axis=-1)


def add_parts(mine, other):
    return two_parts(of_parts(mine[0]) + of_parts(other[0]))[None]


def after(value, *others):
    return lax.optimization_barrier((value, *others))[0]


def local(
    tokens,
    out_grad,
    joint_state,
    joint_mask,
    attn_master,
    attn_first,
    attn_second,
    attn_average,
    ffn_master,
    ffn_first,
    ffn_second,
    ffn_average,
    small_params,
    small_first,
    small_second,
    small_average,
):
    cam_index = lax.axis_index("cam")
    slot, group_index = cam_index % 4, cam_index // 4
    items_here, _, seg_len, _ = tokens.shape
    assert items_here == 4
    device = lax.axis_index("dp") * lax.axis_size("cam") + cam_index if by_blocks() else 0
    where = jnp.stack([jnp.int32(device), jnp.int32(slot)])

    def piece_for(array, n):
        return lax.dynamic_index_in_dim(array, slot ^ n, 0, keepdims=False)

    def trade(pieces):
        return [pieces[0]] + [partner(pieces[n], "cam", n) for n in range(1, 4)]

    blocks = by_blocks()
    sequence = trade([piece_for(tokens[:, 0], n) for n in range(4)])
    cotangents = [piece_for(out_grad[:, 0], n) for n in range(4)]
    attn_low = attn_master.astype(BF16)
    ffn_low = ffn_master.astype(BF16)
    vectors = small_params[: (8 + NJ) * D].reshape(8 + NJ, D)
    hidden_bias = small_params[(8 + NJ) * D :].reshape(1, -1)
    active = (joint_state * joint_mask.astype(F32))[slot, group_index].reshape(1, NJ)
    here = where
    if blocks:
        held = doubled(attn_low[:, None], over_high_z, 1)
        held, ffn_low = together(held, ffn_low)
        wide = doubled(ffn_low[:, None], over_high_z, 1)
        held = doubled(held, over_low_z, 1)
        qk, vo = doubled(held[:2], over_y, 1), doubled(held[2:], over_x, 1)
        qk, vo = together(qk, vo)
        qk, vo, wide, cotangents[1], *sequence = together(qk, vo, wide, cotangents[1], *sequence)
        qk, vo = (qk, over_x(qk)), (vo, over_y(vo))
        qk = (qk, tuple(over_core(x) for x in qk))
        vo = (vo, tuple(over_core(x) for x in vo))
        wide = doubled(wide, over_low_z, 1)
        wide, qk_far, vo_far, here, vectors, active = together(
            wide, qk[1][1], vo[1][1], here, vectors, active
        )
        qk, vo = (qk[0], (qk[1][0], qk_far)), (vo[0], (vo[1][0], vo_far))
        up, down = doubled(wide[0], over_y), doubled(wide[1], over_x)
    else:
        qk, vo = split_sides(attn_low[:2], BY_X, 1), split_sides(attn_low[2:], BY_Y, 1)
        up, down = split_sides(ffn_low[0], BY_X, 0), split_sides(ffn_low[1], BY_Y, 0)

    rounded, top_rows, *heads = attend(0, 1, here, [*sequence, active], qk, vo, vectors, seg_len)
    here = where
    if blocks:
        here, up, down, *heads = together(where, up, down, *heads)
        up, down = (up, over_x(up)), (down, over_y(down))
        far = over_core(up[0]), over_core(down[0])
    *heads, logs = attend(1, PAIRS - 1, here, [rounded, *heads], qk, vo, vectors, seg_len)
    here = where
    if blocks:
        here, up_got, down_got, logs, *far = together(where, up[1], down[1], logs, *far)
        up = ((up[0], up_got), (far[0], over_core(up_got)))
        down = ((down[0], down_got), (far[1], over_core(down_got)))
    h1, normed, y1 = project(here, rounded, top_rows, heads[3], vo, vectors)
    cotangents = trade([after(x, y1) for x in cotangents])
    gated, slope, forward = feed_forward(where, y1, up, down, hidden_bias)
    *results, dh2, df, grads_two, down_keep, down_send = second_norm(
        where, normed, forward, gated, vectors, cotangents
    )
    outputs = trade(results)
    down_got = over_core(down_send) if blocks else down_send
    up_keep, up_send, hidden_grad, above = feed_back(where, dh2, df, y1, slope, up, down)
    here, up_send, down_got, *outputs = together(where, up_send, down_got, *outputs)

    def back(pair, here, rows, *filled):
        return attend_back(pair, here, heads, da, logs, rows, *filled)

    up_got = up_send
    if blocks:
        up_got = over_core(up_send)
        down_keep, down_send = halve(down_keep, down_got)
        up_keep, up_send = halve(up_keep, up_got)
        here, up_send, down_send = together(here, up_send, down_send)
        up_got, down_got = over_x(up_send), over_y(down_send)
    dh1, da, grads_one, out_keep, out_send = first_norm_back(here, above, h1, heads[3], vo, vectors)
    *a_sides, parts, bias_0, turned = back(0, where, rounded)
    here = where
    if blocks:
        up_got, down_got, bias_0 = together(up_got, down_got, bias_0)
        up_keep, up_send = halve(up_keep, up_got)
        down_keep, down_send = halve(down_keep, down_got)
        here, up_send, down_send = together(where, up_send, down_send)
        up_got, down_got = over_y(up_send), over_x(down_send)
    a_keep, a_send, parts, bias_1 = back(1, here, turned, a_sides, (parts,))
    here = where
    if blocks:
        up_got, down_got, bias_1 = together(up_got, down_got, bias_1)
        up_keep, up_send = halve(up_keep, up_got)
        down_keep, down_send = halve(down_keep, down_got)
        keep, send = jnp.stack([up_keep, down_keep], 1), jnp.stack([up_send, down_send], 1)
        here, send, a_send, out_send = together(where, send, a_send, out_send)
        got, a_got, out_got = over_low_z(send), over_core(a_send), over_core(out_send)
    b_keep, b_send, parts, bias_2 = back(2, here, turned, (), (parts,))
    here = where
    if blocks:
        got, a_got, out_got, bias_2 = together(got, a_got, out_got, bias_2)
        keep, send = halve(keep, got)
        a_keep, a_send = halve(joined(a_keep, out_keep), joined(a_got, out_got))
        here, send, a_send = together(where, send, a_send)
        got, a_got = over_high_z(send), over_y(a_send)
    b_keep, b_send, parts, bias_3 = back(3, here, turned, (b_keep, b_send), (parts,))
    small = (bias_0, bias_1, bias_2, bias_3, grads_one, grads_two, active, hidden_grad)
    here = where
    if blocks:
        here, got, a_got, b_send = together(where, got, a_got, b_send)
        b_got = over_core(b_send)
    own, *sends, tiny = input_back(here, dh1, parts, qk, vo, small)
    if blocks:
        b_got, tiny, *sends = together(b_got, tiny, *sends)
        grad_pieces = trade([own, *sends])
        tiny_got = over_core(tiny)
        b_keep, b_send = halve(b_keep, b_got)
        tiny = add_parts(tiny, tiny_got)
        ffn_shard = add_low(keep[0], got[0])
        b_got, tiny_got, ffn_shard, grad_pieces[2] = together(
            over_y(b_send), over_y(tiny), ffn_shard, grad_pieces[2]
        )
        a_keep, a_send = halve(a_keep, a_got)
        b_keep, b_send = halve(b_keep, b_got)
        keep, send = joined(a_keep, b_keep), joined(a_send, b_send)
        tiny = add_parts(tiny, tiny_got)
        send, outputs = together(jnp.concatenate([send, tiny]), together(*outputs))
        got, block_output, *grad_pieces = together(
            over_low_z(send), arrange(where, outputs, BF16), *grad_pieces
        )
        keep, send = halve(keep, got[:-1])
        tiny = add_parts(tiny, got[-1:])
        send, *grad_pieces = together(jnp.concatenate([send, tiny]), *grad_pieces)
        got, input_grad = together(over_high_z(send), arrange(where, grad_pieces, F32))
        keep, send = halve(keep, got[:-1])
        tiny = add_parts(tiny, got[-1:])
        got = over_x(jnp.concatenate([send, tiny]))
        attn_shard = add_low(keep[0], got[0])
        small_total = of_parts(tiny[0]) + of_parts(got[-1])
    else:
        grad_pieces = trade([own, *sends])
        small_total = lax.psum(of_parts(tiny[0]), ("dp", "cam"))
        ffn_shard = jnp.stack(
            [scatter_plain((up_keep, up_got), BY_X), scatter_plain((down_keep, down_got), BY_Y)]
        )
        attn_keep = joined(joined(a_keep, out_keep), b_keep)
        attn_send = joined(joined(a_send, out_send), b_send)
        attn_shard = scatter_plain((attn_keep, attn_send), BY_YZ)
        block_output, input_grad = arrange(where, outputs, BF16), arrange(where, grad_pieces, F32)
    small_total = small_total.reshape(-1)[: small_params.size]

    rows_here = attn_master.shape[1]
    split = 3 * PAIR * SIDE_PAIRS
    proj_grad = joined(attn_shard[:, :split], attn_shard[:, split + D :])
    proj_grad = jnp.moveaxis(proj_grad.reshape(rows_here, PAIRS, 3, PAIR), 2, 0).reshape(3, rows_here, D)
    attn_shard = jnp.concatenate([proj_grad, attn_shard[None, :, split : split + D]])
    new_attn = adam_update(
        attn_master, attn_shard, attn_first, attn_second, attn_average, rate_matrix, decay_matrix
    )
    new_ffn = adam_update(
        ffn_master, ffn_shard, ffn_first, ffn_second, ffn_average, rate_matrix, decay_matrix
    )
    new_small = adam_update(
        small_params, small_total, small_first, small_second, small_average, rate_small, 0.0
    )
    return (block_output, input_grad, *new_attn, *new_ffn, *new_small)


def solution(mesh):
    in_specs = (
        P("dp", "cam", None, None),
        P("dp", "cam", None, None),
        P("dp", None, None),
        P("dp", None, None),
        P(None, ("dp", "cam"), None),
        P(None, ("dp", "cam"), None),
        P(None, ("dp", "cam"), None),
        P(None, ("dp", "cam"), None),
        P(None, ("dp", "cam"), None),
        P(None, ("dp", "cam"), None),
        P(None, ("dp", "cam"), None),
        P(None, ("dp", "cam"), None),
        P(),
        P(),
        P(),
        P(),
    )
    out_specs = (
        P("dp", "cam", None, None),
        P("dp", "cam", None, None),
        P(None, ("dp", "cam"), None),
        P(None, ("dp", "cam"), None),
        P(None, ("dp", "cam"), None),
        P(None, ("dp", "cam"), None),
        P(None, ("dp", "cam"), None),
        P(None, ("dp", "cam"), None),
        P(None, ("dp", "cam"), None),
        P(None, ("dp", "cam"), None),
        P(),
        P(),
        P(),
        P(),
    )
    return jax.shard_map(local, mesh=mesh, in_specs=in_specs, out_specs=out_specs, check_vma=False)
```

```python
import functools

import jax
import jax.numpy as jnp
from jax import lax
from jax.experimental import pallas as pl
from jax.experimental.pallas import tpu as pltpu
from jax.sharding import PartitionSpec as P

D = 512
HEADS = 8
NJ = 14
ADAM_STEP = 10
HD = 64
PAIR = 2 * HD
PAIRS = HEADS // 2
BLOCKS = 32
ROWS = D // BLOCKS
HALF = BLOCKS // 2
CHUNK = 640
SIDE_PAIRS = 2
SIDE_COLS = 3 * PAIR * SIDE_PAIRS
SMALL_BLOCKS = 3
ROW_STEPS = 2

norm_eps = 1e-05
beta_first = 0.5
beta_second = 0.5
adam_eps = 1e-08
rate_matrix = 0.02
rate_small = 0.05
decay_matrix = 0.1
ema_decay = 0.75
log2e = 1.4426950408889634
score_scale = HD**-0.5
F32 = jnp.float32
BF16 = jnp.bfloat16
VMEM_LIMIT = 60 * 2**20
NEXT_TO_NOTHING = pl.CostEstimate(flops=1, bytes_accessed=1, transcendentals=0)


def adam_update(master, grad_total, first_old, second_old, average_old, rate, decay):
    first_new = beta_first * first_old + (1.0 - beta_first) * grad_total
    second_new = beta_second * second_old + (1.0 - beta_second) * grad_total * grad_total
    first_hat = first_new / (1.0 - beta_first**ADAM_STEP)
    second_hat = second_new / (1.0 - beta_second**ADAM_STEP)
    master_new = master - rate * (first_hat / (jnp.sqrt(second_hat) + adam_eps) + decay * master)
    average_new = ema_decay * average_old + (1.0 - ema_decay) * master_new
    return (master_new, first_new, second_new, average_new)


def dot(left, right, left_dim, right_dim):
    return lax.dot_general(
        left, right, (((left_dim,), (right_dim,)), ((), ())), preferred_element_type=F32
    )


DEVICE_BITS = {"x": 2, "y": 4, "z": 8, "Z": 16}
BY_X, BY_Y, BY_YZ = "xyzZ", "yxzZ", "yzxZ"


def apart(position, order, core):
    bits = (DEVICE_BITS[name] for n, name in enumerate(order) if position >> (3 - n) & 1)
    return core + sum(bits)


def row_blocks(device, order):
    for core in range(2):
        for position in range(HALF):
            start = (device ^ apart(position, order, core)) * ROWS
            yield core, position, pl.ds(pl.multiple_of(start, ROWS), ROWS)


def put_rows(target, sides, order, device, part=None, cols=slice(None)):
    for core, position, rows in row_blocks(device, order):
        which, at = divmod(position, HALF // len(sides[core]))
        array = sides[core][which]
        target[rows, :] = array[at] if part is None else array[part, at, :, cols]


def take_rows(source, sides, order, device):
    for core, position, rows in row_blocks(device, order):
        sides[core][position] = source[rows, :].astype(BF16)


def mean_last(values):
    return jnp.sum(values, axis=-1, keepdims=True) * (1.0 / D)


def normal_rows(values):
    centred = values - mean_last(values)
    inverse = lax.rsqrt(mean_last(centred * centred) + norm_eps)
    return centred * inverse, inverse


def normal_back(normal, inverse, grad):
    return inverse * (grad - mean_last(grad) - normal * mean_last(grad * normal))


def column_sum(values):
    return jnp.sum(values, axis=0, keepdims=True)


def small_row(vectors, n):
    pieces = D // PAIR
    return jnp.concatenate([vectors[pieces * n + m : pieces * n + m + 1, :] for m in range(pieces)], axis=1)


def active_joints(where, state, mask):
    here = pl.ds(where[2], 1)
    row = state[0, here, :] * mask[0, here, :].astype(F32)
    shape = (NJ, NJ)
    same = lax.broadcasted_iota(jnp.int32, shape, 0) == lax.broadcasted_iota(jnp.int32, shape, 1)
    return jnp.sum(jnp.where(same, row, 0.0), axis=1, keepdims=True)


def spread_heads(values, other):
    lane = lax.broadcasted_iota(jnp.int32, (1, PAIR), 1)
    low = lane < HD
    return jnp.where(low, values, other), jnp.where(low, other, values)


def attend_kernel(base, seg_len, where, *refs):
    first = base == 0
    if first:
        pieces, joints, refs = refs[:4], refs[4:6], refs[6:]
    else:
        rounded, refs = refs[0], refs[7:]
    sides, vectors, refs = (refs[0:2], refs[2:4]), refs[4], refs[5:]
    if first:
        rounded, top_rows, refs = refs[0], refs[1], refs[2:]
    q_out, k_out, v_out, a_out, l_out, weight, logs = refs
    device, slot = where[0], where[1]

    if first:

        @pl.when(pl.program_id(0) == 0)
        def _():
            for k in range(4):
                start = pl.multiple_of((slot ^ k) * seg_len, 16)
                rounded[pl.ds(start, seg_len), :] = pieces[k][...]
            joint_rows = jnp.concatenate([small_row(vectors, 8 + n) for n in range(NJ)], axis=0)
            joint = column_sum(active_joints(where, *joints) * joint_rows)
            top = rounded[:16, :].astype(F32)
            at = lax.broadcasted_iota(jnp.int32, (16, 1), 0)
            top = jnp.where(at == 1, top + joint, top)
            top_rows[...] = top[:8]
            rounded[:16, :] = top.astype(BF16)

    for part in range(3):
        put_rows(weight.at[:, part * PAIR : (part + 1) * PAIR], sides, BY_X, device, part)
    pair = pl.program_id(0) + base
    bias_q, bias_v = vectors[pl.ds(pair, 1), :], vectors[pl.ds(PAIRS + pair, 1), :]
    projected = dot(rounded[...], weight[...], 1, 0)
    q_out[...] = (projected[:, :PAIR] + bias_q).astype(BF16)
    keys = projected[:, PAIR : 2 * PAIR].astype(BF16)
    values = (projected[:, 2 * PAIR :] + bias_v).astype(BF16)
    k_out[...] = keys
    v_out[...] = values
    lane = lax.broadcasted_iota(jnp.int32, (1, PAIR), 1)
    low = lane < HD
    value_heads = spread_heads(values, jnp.ones_like(values))
    scale = log2e * score_scale
    for step in range(4):
        rows = pl.ds(step * seg_len, seg_len)
        query = q_out[rows, :]
        mixed, tops = [], []
        for query_head, value_head in zip(spread_heads(query, jnp.zeros_like(query)), value_heads):
            scores = dot(query_head, keys, 1, 1)
            top = jnp.max(scores, axis=1, keepdims=True) * scale
            probs = jnp.exp2(scores * scale - top).astype(BF16)
            mixed.append(dot(probs, value_head, 1, 0))
            tops.append(top)
        total = pltpu.roll(jnp.where(low, mixed[1], mixed[0]), HD, 1)
        a_out[rows, :] = (jnp.where(low, mixed[0], mixed[1]) / total).astype(BF16)
        logs[rows, :] = jnp.where(low, tops[0], tops[1]) + jnp.log2(total)
    turned = logs[...].T
    l_out[0:1, :] = turned[0:1]
    l_out[1:2, :] = turned[HD : HD + 1]


def gate_both(values):
    def low(constant):
        return jnp.asarray(constant, BF16)

    values = values.astype(BF16)
    size = jnp.abs(values)
    fraction = low(1.0) / (low(1.0) + low(0.3275911 * 0.5**0.5) * size)
    bell = jnp.exp2(values * values * low(-0.5 * log2e))
    series = low(0.5 * 1.061405429) * fraction - low(0.5 * 1.453152027)
    series = series * fraction + low(0.5 * 1.421413741)
    series = series * fraction - low(0.5 * 0.284496736)
    series = series * fraction + low(0.5 * 0.254829592)
    tail = series * fraction * bell
    bend = size * bell * low(0.3989422804014327) - tail
    slope = jnp.where(values > low(0.0), low(1.0) + bend, -bend)
    return jnp.maximum(values, low(0.0)) - size * tail, slope


def project_kernel(seg_len, where, *refs):
    rounded, top_rows, mixed, sides, vectors = *refs[:3], (refs[3:5], refs[5:7]), refs[7]
    h1_out, normed_out, y1_out, w_out = refs[8:]
    out_scale = (4 * seg_len / 3.0) ** 0.5

    @pl.when(pl.program_id(0) == 0)
    def _():
        put_rows(w_out, sides, BY_X, where[0], 0)

    summed = rounded[...].astype(F32)
    top = jnp.where(pl.program_id(0) == 0, top_rows[...], summed[:8])
    summed = jnp.concatenate([top, summed[8:]], axis=0)
    summed = summed + (dot(mixed[...], w_out[...], 1, 0) * out_scale + small_row(vectors, 2))
    h1_out[...] = summed
    normal, _ = normal_rows(summed)
    result = normal * small_row(vectors, 3) + small_row(vectors, 4)
    normed_out[...] = result
    y1_out[...] = result.astype(BF16)


def forward_kernel(seg_len, where, *refs):
    y1, up_sides, down_sides = refs[0], (refs[1:3], refs[3:5]), (refs[5:7], refs[7:9])
    vectors, refs = refs[9], refs[10:]
    g_out, slope_out, total, w_up, w_down = refs
    device = where[0]

    @pl.when(pl.program_id(0) == 0)
    def _():
        total[...] = jnp.zeros_like(total)

    put_rows(w_up, up_sides, BY_X, device)
    put_rows(w_down, down_sides, BY_Y, device)
    lanes = vectors.shape[1]
    first_row = (8 + NJ) * (D // lanes) + pl.program_id(0) * (CHUNK // lanes)
    hidden_bias = [vectors[pl.ds(first_row + n, 1), :] for n in range(CHUNK // lanes)]
    hidden_bias = jnp.concatenate(hidden_bias, axis=1)
    for step in range(4):
        rows = pl.ds(step * seg_len, seg_len)
        inner = dot(y1[rows, :], w_up[...], 1, 0) + hidden_bias
        active, slope = gate_both(inner)
        active = active.astype(BF16)
        g_out[rows, :] = active
        slope_out[rows, :] = slope.astype(BF16)
        total[rows, :] += dot(active, w_down[...], 1, 1)


def second_kernel(seg_len, where, *refs):
    normed, forward, active, vectors, cotangents, refs = *refs[:4], refs[4:8], refs[8:]
    pieces, dh2_out, df_out, vector_grads, refs = refs[:4], refs[4], refs[5], refs[6], refs[7:]
    down_grads, df_turned, grad = refs[:2], refs[2], refs[3]
    device, slot = where[0], where[1]

    @pl.when(pl.program_id(0) == 0)
    def _():
        gain_grad = shift_grad = bias_grad = 0.0
        for k in range(4):
            rows = pl.ds(pl.multiple_of((slot ^ k) * seg_len, 16), seg_len)
            normal, inverse = normal_rows(normed[rows, :] + (forward[rows, :] + small_row(vectors, 5)))
            pieces[k][...] = (normal * small_row(vectors, 6) + small_row(vectors, 7)).astype(BF16)
            cotangent = cotangents[k][...].astype(F32)
            gain_grad += column_sum(cotangent * normal)
            shift_grad += column_sum(cotangent)
            middle = normal_back(normal, inverse, cotangent * small_row(vectors, 6))
            dh2_out[rows, :] = middle
            rounded = middle.astype(BF16)
            df_out[rows, :] = rounded
            bias_grad += column_sum(rounded.astype(F32))
        vector_grads[0:1, :] = gain_grad
        vector_grads[1:2, :] = shift_grad
        vector_grads[2:3, :] = bias_grad
        df_turned[...] = df_out[...].T

    grad[...] = dot(df_turned[...], active[...], 1, 0)
    take_rows(grad, down_grads, BY_Y, device)


def backward_kernel(seg_len, where, *refs):
    dh2, df, y1, slope, refs = *refs[:4], refs[4:]
    up_sides, down_sides, refs = (refs[0:2], refs[2:4]), (refs[4:6], refs[6:8]), refs[8:]
    up_grads, hidden_grad, total, refs = refs[:2], refs[2], refs[3], refs[4:]
    y1_turned, dz, w_up, w_down, grad = refs
    device = where[0]

    @pl.when(pl.program_id(0) == 0)
    def _():
        y1_turned[...] = y1[...].T
        total[...] = dh2[...]

    put_rows(w_up, up_sides, BY_X, device)
    put_rows(w_down, down_sides, BY_Y, device)
    bias_grad = 0.0
    for step in range(4):
        rows = pl.ds(step * seg_len, seg_len)
        inner = (dot(df[rows, :], w_down[...], 1, 0) * slope[rows, :].astype(F32)).astype(BF16)
        dz[rows, :] = inner
        bias_grad += column_sum(inner.astype(F32))
        total[rows, :] += dot(inner, w_up[...], 1, 1)
    hidden_grad[...] = bias_grad
    grad[...] = dot(y1_turned[...], dz[...], 1, 0)
    take_rows(grad, up_grads, BY_X, device)


def first_kernel(seg_len, where, *refs):
    above_in, h1, mixed, sides, vectors = *refs[:3], (refs[3:5], refs[5:7]), refs[7]
    dh1_out, da_out, vector_grads, grad_sides, w_out, grad = *refs[8:11], refs[11:13], *refs[13:]
    device, step = where[0], pl.program_id(0)
    out_scale = (4 * seg_len / 3.0) ** 0.5

    @pl.when(step == 0)
    def _():
        put_rows(w_out, sides, BY_X, device, 0)
        vector_grads[...] = jnp.zeros_like(vector_grads)
        grad[...] = jnp.zeros_like(grad)

    normal, inverse = normal_rows(h1[...])
    above = above_in[...]
    vector_grads[0:1, :] += column_sum(above * normal)
    vector_grads[1:2, :] += column_sum(above)
    summed = normal_back(normal, inverse, above * small_row(vectors, 3))
    dh1_out[...] = summed
    rounded = summed.astype(BF16)
    vector_grads[2:3, :] += column_sum(rounded.astype(F32))
    da_out[...] = (dot(rounded, w_out[...], 1, 1) * out_scale).astype(BF16)
    grad[...] += dot(mixed[...], rounded, 0, 0) * out_scale

    @pl.when(step == pl.num_programs(0) - 1)
    def _():
        take_rows(grad, grad_sides, BY_YZ, device)


def attend_back_kernel(first, aliased, where, *refs):
    q, k, v, a, da, logs, refs = *refs[:6], refs[6:]
    rounded, (keep, send, parts, bias_grads), refs = refs[0], refs[1 + aliased : 5 + aliased], refs[5 + aliased :]
    if first:
        turned, refs = refs[0], refs[1:]

        @pl.when(pl.program_id(0) == 0)
        def _():
            turned[...] = rounded[...].T

    else:
        turned = rounded
    query_turned, grad = refs
    seq_len = q.shape[0]

    queries, mixed_grads = q[...], da[...]
    zeros = jnp.zeros_like(queries)
    query_heads = spread_heads(queries, zeros)
    grad_heads = spread_heads(mixed_grads, zeros)
    product = (mixed_grads.astype(F32) * a[...].astype(F32)).T
    inner = (column_sum(product[:HD]), column_sum(product[HD:]))
    start = 0
    while start < seq_len:
        size = min(256, seq_len - start)
        rows = pl.ds(start, size)
        none = jnp.zeros((size, PAIR), BF16)
        key_grad = value_grad = query_grad = 0.0
        heads = zip(spread_heads(k[rows, :], none), spread_heads(v[rows, :], none))
        for h, (key_head, value_head) in enumerate(heads):
            scores = dot(key_head, queries, 1, 1)
            probs = jnp.exp2(scores * (log2e * score_scale) - logs[h : h + 1, :])
            grads = (probs * (dot(value_head, mixed_grads, 1, 1) - inner[h])).astype(BF16)
            value_grad += dot(probs.astype(BF16), grad_heads[h], 1, 0)
            key_grad += dot(grads, query_heads[h], 1, 0)
            query_grad += dot(key_head, grads, 0, 0)
        parts[rows, PAIR : 2 * PAIR] = (key_grad * score_scale).astype(BF16)
        parts[rows, 2 * PAIR :] = value_grad.astype(BF16)
        if start == 0:
            query_turned[...] = query_grad
        else:
            query_turned[...] += query_grad
        start += size
    parts[:, :PAIR] = (query_turned[...].T * score_scale).astype(BF16)
    bias_grads[0:1, :] = column_sum(parts[:, :PAIR].astype(F32))
    bias_grads[1:2, :] = column_sum(parts[:, 2 * PAIR :].astype(F32))
    grad[...] = dot(turned[...], parts[...], 1, 0)
    take_rows(grad, (keep, send), BY_YZ, where[0])


def input_back_kernel(far, where, *refs):
    dh1, parts, weight, refs = refs[0:2], refs[2:4], refs[4], refs[5:]
    if far:
        top_dh1, top_parts, joints, small_parts = *refs[:2], refs[2:4], refs[4:10]
        sends, small_out, joined = refs[10:12], *refs[12:]
        top = top_dh1[...] + dot(top_parts[...], weight[...], 1, 1)
        join_small(joined, small_parts, active_joints(where, *joints) * top[1:2, :])
        for n in range(SMALL_BLOCKS):
            small_out[n] = two_parts(joined[n * (ROWS // 2) : (n + 1) * (ROWS // 2)])
    else:
        sends = refs
    for n, send in enumerate(sends):
        send[...] = (dh1[n][...] + dot(parts[n][...], weight[...], 1, 1)).astype(send.dtype)


def call(kernel, name, where, grid, operands, results, scratch, aliases=None):
    def spec(block, index):
        if block is None:
            return pl.BlockSpec(memory_space=pl.ANY)
        if index.__code__.co_argcount == 2:
            return pl.BlockSpec(block, index)
        return pl.BlockSpec(block, lambda i, _: index(i))

    return pl.pallas_call(
        kernel,
        grid_spec=pltpu.PrefetchScalarGridSpec(
            num_scalar_prefetch=1,
            grid=(grid,),
            in_specs=[spec(block, index) for _, block, index in operands],
            out_specs=[spec(block, index) for _, block, index in results],
            scratch_shapes=[pltpu.VMEM(shape, kind) for shape, kind in scratch],
        ),
        out_shape=[shape for shape, _, _ in results],
        input_output_aliases={source + 1: target for source, target in (aliases or {}).items()},
        compiler_params=pltpu.CompilerParams(vmem_limit_bytes=VMEM_LIMIT),
        cost_estimate=NEXT_TO_NOTHING,
        name=name,
    )(where, *(x for x, _, _ in operands))


def whole(x):
    return (x, x.shape, lambda i: (0,) * len(x.shape))


def shape_of(shape, kind):
    return jax.ShapeDtypeStruct(shape, kind)


def whole_out(shape, kind):
    return whole(shape_of(shape, kind))


def flat(sides):
    return [x for side in sides for x in side]


def pair_weights(sides, base):
    return [(x, (3, x.shape[1], ROWS, PAIR), lambda i: (0, 0, 0, i + base)) for x in flat(sides)]


def attend(base, pairs, where, source, sides, vectors, seg_len):
    seq_len = 4 * seg_len
    first = base == 0

    def column(x):
        return (x, (seq_len, PAIR), lambda i: (0, i + base))

    operands = [whole(x) for x in (source[:4] if first else source[:1])]
    if first:
        operands += [(x, (1, *x.shape[1:]), lambda i, at: (at[1], 0, 0)) for x in source[4:]]
    operands += [] if first else [(x, None, None) for x in source[1:]]
    operands += pair_weights(sides, base) + [whole(vectors)]
    results = [whole_out((seq_len, D), BF16), whole_out((8, D), F32)] if first else []
    results += [column(shape_of((seq_len, D), BF16))] * 4
    logs = shape_of((PAIRS, 2, seq_len), F32)
    results += [(logs, (None, 2, seq_len), lambda i: (i + base, 0, 0))]
    results += [(shape_of((D, 3 * D), BF16), (D, 3 * PAIR), lambda i: (0, i + base))]
    scratch = [((seq_len, PAIR), F32)]
    return call(
        functools.partial(attend_kernel, base, seg_len),
        f"attend_{base}",
        where,
        pairs,
        operands,
        results,
        scratch,
        {} if first else {1 + n: n for n in range(6)},
    )


def by_chunk(x):
    if x.ndim == 3:
        return (x, (x.shape[0], ROWS, CHUNK), lambda i: (0, 0, i))
    return (x, (x.shape[0], CHUNK), lambda i: (0, i))


def out_weight(sides):
    return [(x, (1, x.shape[1], ROWS, D), lambda i: (3, 0, 0, 0)) for x in flat(sides)]


def by_rows(x):
    return (x, (x.shape[0] // ROW_STEPS, x.shape[1]), lambda i: (i, 0))


def project(where, rounded, top_rows, mixed, sides, vectors):
    seq_len = rounded.shape[0]
    return call(
        functools.partial(project_kernel, seq_len // 4),
        "project",
        where,
        ROW_STEPS,
        [by_rows(rounded), whole(top_rows), by_rows(mixed), *out_weight(sides), whole(vectors)],
        [by_rows(shape_of((seq_len, D), kind)) for kind in (F32, F32, BF16)],
        [((D, D), BF16)],
    )


def feed_forward(where, y1, up, down, vectors):
    seq_len = y1.shape[0]
    hidden = up[0][0].shape[-1]
    wide = by_chunk(shape_of((seq_len, hidden), BF16))
    return call(
        functools.partial(forward_kernel, seq_len // 4),
        "feed_forward",
        where,
        hidden // CHUNK,
        [whole(y1)] + [by_chunk(x) for x in (*flat(up), *flat(down))] + [whole(vectors)],
        [wide, wide, whole_out((seq_len, D), F32)],
        [((D, CHUNK), BF16)] * 2,
    )


def second_norm(where, normed, forward, active, vectors, cotangents):
    seq_len, hidden = active.shape
    seg_len = seq_len // 4
    operands = [whole(normed), whole(forward), by_chunk(active), whole(vectors)]
    results = [whole_out((seg_len, D), BF16)] * 4
    results += [whole_out((seq_len, D), F32), whole_out((seq_len, D), BF16), whole_out((8, D), F32)]
    results += [by_chunk(shape_of((HALF, ROWS, hidden), BF16))] * 2
    return call(
        functools.partial(second_kernel, seg_len),
        "second_norm",
        where,
        hidden // CHUNK,
        operands + [whole(x) for x in cotangents],
        results,
        [((D, seq_len), BF16), ((D, CHUNK), F32)],
    )


def feed_back(where, dh2, df, y1, slope, up, down):
    seq_len, hidden = slope.shape
    operands = [whole(dh2), whole(df), whole(y1)] + [by_chunk(x) for x in (slope, *flat(up), *flat(down))]
    results = [by_chunk(shape_of((HALF, ROWS, hidden), BF16))] * 2
    results += [by_chunk(shape_of((1, hidden), F32)), whole_out((seq_len, D), F32)]
    scratch = [((D, seq_len), BF16), ((seq_len, CHUNK), BF16)]
    scratch += [((D, CHUNK), BF16)] * 2 + [((D, CHUNK), F32)]
    return call(
        functools.partial(backward_kernel, seq_len // 4),
        "feed_back",
        where,
        hidden // CHUNK,
        operands,
        results,
        scratch,
    )


def first_norm_back(where, above, h1, mixed, sides, vectors):
    seq_len = h1.shape[0]
    results = [by_rows(shape_of((seq_len, D), kind)) for kind in (F32, BF16)]
    results += [whole_out((8, D), F32)]
    results += [whole_out((HALF, ROWS, D), BF16)] * 2
    return call(
        functools.partial(first_kernel, seq_len // 4),
        "first_norm_back",
        where,
        ROW_STEPS,
        [by_rows(x) for x in (above, h1, mixed)] + [*out_weight(sides), whole(vectors)],
        results,
        [((D, D), BF16), ((D, D), F32)],
    )


def attend_back(base, pairs, where, heads, da, logs, rounded, sides=(), parts=()):
    first = base == 0
    seq_len = da.shape[0]
    operands = [(x, (seq_len, PAIR), lambda i: (0, i + base)) for x in (*heads, da)]
    operands += [(logs, (None, 2, seq_len), lambda i: (i + base, 0, 0)), whole(rounded)]
    aliases = {len(operands) + n: n for n in range(len(sides))}
    aliases |= {len(operands) + len(sides) + n: 2 for n in range(len(parts))}
    operands += [(x, None, None) for x in (*sides, *parts)]
    side = shape_of((HALF, ROWS, SIDE_COLS), BF16)
    results = [(side, (HALF, ROWS, 3 * PAIR), lambda i: (0, 0, (i + base) % SIDE_PAIRS))] * 2
    results += [(shape_of((seq_len, 3 * D), BF16), (seq_len, 3 * PAIR), lambda i: (0, i + base))]
    results += [(shape_of((8, pairs * PAIR), F32), (8, PAIR), lambda i: (0, i))]
    results += [whole_out((D, seq_len), BF16)] if first else []
    return call(
        functools.partial(attend_back_kernel, first, len(sides) + len(parts)),
        f"attend_back_{base}",
        where,
        pairs,
        operands,
        results,
        [((PAIR, seq_len), F32), ((D, 3 * PAIR), F32)],
        aliases,
    )


def input_back(first, where, dh1, parts, weight, joints=(), small=()):
    seg_len = dh1.shape[0] // 4
    far = first == 2

    def segment(x, n):
        return pl.BlockSpec((seg_len, x.shape[1]), lambda i, at: (at[1] ^ (first + n), 0))

    def full(x):
        return pl.BlockSpec(x.shape, lambda i, _: (0,) * len(x.shape))

    operands = [dh1, dh1, parts, parts, weight]
    specs = [segment(x, n) for x in (dh1, parts) for n in range(2)] + [full(weight)]
    results = [shape_of((seg_len, D), BF16 if far or n else F32) for n in range(2)]
    scratch = []
    if far:
        operands += [dh1, parts, *joints, *small]
        specs += [pl.BlockSpec((ROWS, x.shape[1]), lambda i, _: (0, 0)) for x in (dh1, parts)]
        specs += [pl.BlockSpec((1, *x.shape[1:]), lambda i, at: (at[1], 0, 0)) for x in joints]
        specs += [full(x) for x in small]
        results += [shape_of((SMALL_BLOCKS, ROWS, SIDE_COLS), BF16)]
        scratch += [pltpu.VMEM((SMALL_BLOCKS * ROWS // 2, SIDE_COLS), F32)]
    return pl.pallas_call(
        functools.partial(input_back_kernel, far),
        grid_spec=pltpu.PrefetchScalarGridSpec(
            num_scalar_prefetch=1,
            grid=(1,),
            in_specs=specs,
            out_specs=[full(x) for x in results],
            scratch_shapes=scratch,
        ),
        out_shape=results,
        compiler_params=pltpu.CompilerParams(vmem_limit_bytes=VMEM_LIMIT),
        cost_estimate=NEXT_TO_NOTHING,
        name=f"input_back_{first}",
    )(where, *operands)


def join_small(joined, parts, by_joint):
    *biases, first, second, hidden = parts
    units = [x[n : n + 1, :] for n in range(2) for x in biases]
    units += [first[n : n + 1, :] for n in (2, 0, 1)] + [second[n : n + 1, :] for n in (2, 0, 1)]
    units += [by_joint[n : n + 1, :] for n in range(NJ)] + [hidden[...]]
    joined[...] = jnp.zeros_like(joined)
    at, width = 0, joined.shape[1]
    for unit in units:
        taken = 0
        while taken < unit.shape[1]:
            row, column = divmod(at, width)
            size = min(width - column, unit.shape[1] - taken)
            joined[row : row + 1, column : column + size] = unit[:, taken : taken + size]
            taken, at = taken + size, at + size


def two_parts(values):
    high = lax.reduce_precision(values, 8, 7)
    return jnp.concatenate([high, lax.reduce_precision(values - high, 8, 7)], axis=-2).astype(BF16)


def of_parts(parts):
    half = parts.shape[-2] // 2
    return parts[..., :half, :].astype(F32) + parts[..., half:, :].astype(F32)


def arrange_kernel(where, *refs):
    pieces, out, landed, widened, sem_in, sem_out = refs[:4], *refs[4:]
    loads = [pltpu.make_async_copy(x, landed.at[n], sem_in.at[n]) for n, x in enumerate(pieces[1:])]
    loads.append(pltpu.make_async_copy(pieces[0], widened.at[3], sem_in.at[3]))
    for load in loads:
        load.start()
    stores = []
    for n, load in enumerate(loads):
        load.wait()
        if n < 3:
            widened[n] = landed[n].astype(out.dtype)
        target = out.at[where[1] ^ ((n + 1) % 4), 0]
        stores.append(pltpu.make_async_copy(widened.at[n], target, sem_out.at[n]))
        stores[n].start()
    for store in stores:
        store.wait()


def arrange(where, pieces, kind):
    seg_len = pieces[1].shape[0]
    return pl.pallas_call(
        arrange_kernel,
        grid_spec=pltpu.PrefetchScalarGridSpec(
            num_scalar_prefetch=1,
            grid=(1,),
            in_specs=[pl.BlockSpec(memory_space=pl.ANY)] * 4,
            out_specs=pl.BlockSpec(memory_space=pl.ANY),
            scratch_shapes=[
                pltpu.VMEM((3, seg_len, D), BF16),
                pltpu.VMEM((4, seg_len, D), kind),
                pltpu.SemaphoreType.DMA((4,)),
                pltpu.SemaphoreType.DMA((4,)),
            ],
        ),
        out_shape=jax.ShapeDtypeStruct((4, 1, seg_len, D), kind),
        compiler_params=pltpu.CompilerParams(vmem_limit_bytes=VMEM_LIMIT),
        cost_estimate=NEXT_TO_NOTHING,
        name="arrange",
    )(where, *pieces)


def partner(value, axis, mask):
    pairs = [(source, source ^ mask) for source in range(lax.axis_size(axis))]
    return lax.ppermute(value, axis, pairs)


def over_core(value):
    return partner(value, "cam", 1)


def over_x(value):
    return partner(value, "cam", 2)


def over_y(value):
    return partner(value, "dp", 1)


def over_y_and_core(value):
    pairs = [(source, source ^ 5) for source in range(BLOCKS)]
    return lax.ppermute(value, ("dp", "cam"), pairs)


def over_z(value, apart_by):
    return partner(value, "dp", 2 * apart_by)


def stages_of(order):
    return (over_x, over_y) if order == BY_X else (over_y, over_x)


def by_blocks():
    return lax.axis_size("dp") * lax.axis_size("cam") == BLOCKS


def doubled(held, stage, axis=0):
    return jnp.concatenate([held, stage(held)], axis=axis)


def gather_plain(shard, order):
    at = shard.ndim - 2
    full = lax.all_gather(shard, ("dp", "cam"), axis=at, tiled=True)
    full = full.reshape(*full.shape[:at], 2, 2, 2, 2, 2, ROWS, full.shape[-1])
    places = ["Zzyx".index(name) + at for name in order]
    full = jnp.moveaxis(full, (at + 4, *places), (0, *range(at + 1, at + 5)))
    full = full.reshape(2, *shard.shape[:at], HALF, *full.shape[-2:])
    return full[0], full[1]


def split_sides(shard, order, at):
    return tuple(tuple(jnp.split(x, 2, axis=at)) for x in gather_plain(shard, order))


def scatter_plain(sides, order):
    full = jnp.stack(sides).reshape(2, 2, 2, 2, 2, ROWS, sides[0].shape[-1])
    places = (4, *("Zzyx".index(name) for name in order))
    full = jnp.moveaxis(full, range(5), places).reshape(D, sides[0].shape[-1])
    return lax.psum_scatter(full.astype(F32), ("dp", "cam"), scatter_dimension=0, tiled=True)


def halve(held, received):
    half = held.shape[0] // 2

    def part(rows):
        return (held[rows].astype(F32) + received[rows].astype(F32)).astype(BF16)

    return part(slice(0, half)), part(slice(half, None))


def over_low_z(value):
    return over_z(value, 1)


def over_high_z(value):
    return over_z(value, 2)


def add_low(mine, other):
    return mine.astype(F32) + other.astype(F32)


def together(*values):
    return lax.optimization_barrier(values)


def joined(left, right):
    return jnp.concatenate([left, right], axis=-1)


def add_parts(mine, other):
    return two_parts(of_parts(mine) + of_parts(other))


def after(value, *others):
    return lax.optimization_barrier((value, *others))[0]


def local(
    tokens,
    out_grad,
    joint_state,
    joint_mask,
    attn_master,
    attn_first,
    attn_second,
    attn_average,
    ffn_master,
    ffn_first,
    ffn_second,
    ffn_average,
    small_params,
    small_first,
    small_second,
    small_average,
):
    cam_index = lax.axis_index("cam")
    slot, group_index = cam_index % 4, cam_index // 4
    items_here, _, seg_len, _ = tokens.shape
    assert items_here == 4
    device = lax.axis_index("dp") * lax.axis_size("cam") + cam_index if by_blocks() else 0
    where = jnp.stack([jnp.int32(device), jnp.int32(slot), jnp.int32(group_index)])

    def pieces_of(array):
        return [lax.dynamic_index_in_dim(array[:, 0], slot ^ n, 0, keepdims=False) for n in range(4)]

    def new_of_ffn(gradient):
        return adam_update(
            ffn_master, gradient, ffn_first, ffn_second, ffn_average, rate_matrix, decay_matrix
        )

    def trade(pieces):
        return [pieces[0]] + [partner(pieces[n], "cam", n) for n in range(1, 4)]

    blocks = by_blocks()
    sequence = trade(pieces_of(tokens))
    cotangents = pieces_of(out_grad)
    attn_low = attn_master.astype(BF16)
    ffn_low = ffn_master.astype(BF16)
    vectors = small_params.reshape(-1, PAIR)
    joints = joint_state, joint_mask
    here = where
    if blocks:
        held = doubled(attn_low[:, None], over_high_z, 1)
        held, ffn_low = together(held, ffn_low)
        wide = doubled(ffn_low[:, None], over_high_z, 1)
        held = doubled(held, over_low_z, 1)
        held = doubled(held, over_y, 1)
        held, wide, here, cotangents[1], *sequence = together(
            held, wide, here, cotangents[1], *sequence
        )
        near = held, over_x(held)
        far = tuple(over_core(x) for x in near)
        wide = doubled(wide, over_low_z, 1)
        wide, here, vectors, *far = together(wide, here, vectors, *far)
        sides = near, far
        up, down = doubled(wide[0], over_y), doubled(wide[1], over_x)
    else:
        sides = split_sides(attn_low, BY_X, 1)
        up, down = split_sides(ffn_low[0], BY_X, 0), split_sides(ffn_low[1], BY_Y, 0)

    rounded, top_rows, *heads = attend(0, 1, here, [*sequence, *joints], sides, vectors, seg_len)
    here = where
    if blocks:
        here, up, down, *heads = together(where, up, down, *heads)
        up, down = (up, over_x(up)), (down, over_y(down))
        far = over_core(up[0]), over_core(down[0])
    *heads, logs, weight = attend(1, PAIRS - 1, here, [rounded, *heads], sides, vectors, seg_len)
    here = where
    if blocks:
        here, up_got, down_got, logs, *far = together(where, up[1], down[1], logs, *far)
        up = ((up[0], up_got), (far[0], over_core(up_got)))
        down = ((down[0], down_got), (far[1], over_core(down_got)))
    h1, normed, y1 = project(here, rounded, top_rows, heads[3], sides, vectors)
    cotangents = trade([after(x, y1) for x in cotangents])
    gated, slope, forward = feed_forward(where, y1, up, down, vectors)
    *results, dh2, df, grads_two, down_keep, down_send = second_norm(
        where, normed, forward, gated, vectors, cotangents
    )
    outputs = trade(results)
    down_got = over_core(down_send) if blocks else down_send
    up_keep, up_send, hidden_grad, above = feed_back(where, dh2, df, y1, slope, up, down)
    here, up_send, down_got, *outputs = together(where, up_send, down_got, *outputs)

    def back(base, pairs, here, rows, *filled):
        return attend_back(base, pairs, here, heads, da, logs, rows, *filled)

    up_got = over_core(up_send) if blocks else up_send
    dh1, da, grads_one, out_keep, out_send = first_norm_back(here, above, h1, heads[3], sides, vectors)
    here = where
    if blocks:
        up_got, down_got, da = together(up_got, down_got, da)
        up_keep, up_send = halve(up_keep, up_got)
        down_keep, down_send = halve(down_keep, down_got)
        here, up_send, down_send, out_send = together(where, up_send, down_send, out_send)
        up_got, down_got, out_got = over_x(up_send), over_y(down_send), over_core(out_send)
    a_keep, a_send, parts, bias_a, turned = back(0, 2, here, rounded)
    here = where
    if blocks:
        up_got, down_got, out_got, bias_a = together(up_got, down_got, out_got, bias_a)
        up_keep, up_send = halve(up_keep, up_got)
        down_keep, down_send = halve(down_keep, down_got)
        here, up_send, down_send, a_send = together(where, up_send, down_send, a_send)
        up_got, down_got, a_got = over_y(up_send), over_x(down_send), over_core(a_send)
    b_keep, b_send, parts, bias_2 = back(2, 1, here, turned, (), (parts,))
    here = where
    if blocks:
        up_got, down_got, a_got, bias_2 = together(up_got, down_got, a_got, bias_2)
        up_keep, up_send = halve(up_keep, up_got)
        down_keep, down_send = halve(down_keep, down_got)
        keep, send = jnp.stack([up_keep, down_keep], 1), jnp.stack([up_send, down_send], 1)
        a_keep, a_send = halve(joined(a_keep, out_keep), joined(a_got, out_got))
        here, send, a_send = together(where, send, a_send)
        got, a_got = over_low_z(send), over_y(a_send)
    b_keep, b_send, parts, bias_3 = back(3, 1, here, turned, (b_keep, b_send), (parts,))
    small = (bias_a, bias_2, bias_3, grads_one, grads_two, hidden_grad)
    here = where
    if blocks:
        got, a_got, bias_3 = together(got, a_got, bias_3)
        keep, send = halve(keep, got)
        a_keep, a_send = halve(a_keep, a_got)
        here, send, a_send, b_send = together(where, send, a_send, b_send)
        got, a_got, b_got = over_high_z(send), over_low_z(a_send), over_core(b_send)
    *sends, tiny = input_back(2, here, dh1, parts, weight, joints, small)
    here = where
    if blocks:
        b_got, tiny, *sends = together(b_got, tiny, *sends)
        b_keep, b_send = halve(b_keep, b_got)
        here, b_send = together(where, b_send)
        b_got, tiny_y = over_y(b_send), over_y(tiny)
        tiny_core, tiny_both = over_core(tiny), over_y_and_core(tiny)
        far_piece = partner(sends[0], "cam", 2)
    near = input_back(0, here, dh1, parts, weight)
    if blocks:
        own, far_piece, a_got, tiny_core, tiny_y, tiny_both, b_got, got = together(
            near[0], far_piece, a_got, tiny_core, tiny_y, tiny_both, b_got, got
        )
        tiny = of_parts(tiny) + of_parts(tiny_core)
        tiny = two_parts(tiny + (of_parts(tiny_y) + of_parts(tiny_both)))
        grad_pieces = [own, over_core(near[1]), far_piece, partner(sends[1], "cam", 3)]
        new_ffn = new_of_ffn(add_low(keep[0], got[0]))
        a_keep, a_send = halve(a_keep, a_got)
        b_keep, b_send = halve(b_keep, b_got)
        send, a_send, new_ffn, outputs = together(
            jnp.concatenate([b_send, tiny]), a_send, together(*new_ffn), together(*outputs)
        )
        got, a_got, block_output, *grad_pieces = together(
            over_low_z(send), over_x(a_send), arrange(where, outputs, BF16), *grad_pieces
        )
        for stage in (over_x, over_high_z):
            half = b_send.shape[0]
            b_keep, b_send = halve(b_keep, got[:half])
            tiny = add_parts(tiny, got[half:])
            send = jnp.concatenate([b_send, tiny])
            if stage is over_x:
                a_keep, a_send = halve(a_keep, a_got)
                send, a_send = together(send, a_send)
                got, a_got = together(over_x(send), over_high_z(a_send))
            else:
                send, *grad_pieces = together(send, *grad_pieces)
                got, input_grad = together(over_high_z(send), arrange(where, grad_pieces, F32))
        attn_shard = joined(add_low(a_keep[0], a_got[0]), add_low(b_keep[0], got[0]))
        small_total = of_parts(tiny) + of_parts(got[1:])
    else:
        grad_pieces = trade([*near, *sends])
        small_total = lax.psum(of_parts(tiny), ("dp", "cam"))
        ffn_grads = (scatter_plain((up_keep, up_got), BY_X), scatter_plain((down_keep, down_got), BY_Y))
        new_ffn = new_of_ffn(jnp.stack(ffn_grads))
        attn_keep = joined(joined(a_keep, out_keep), b_keep)
        attn_send = joined(joined(a_send, out_send), b_send)
        attn_shard = scatter_plain((attn_keep, attn_send), BY_YZ)
        block_output, input_grad = arrange(where, outputs, BF16), arrange(where, grad_pieces, F32)
    small_total = small_total.reshape(-1)[: small_params.size]

    rows_here = attn_master.shape[1]
    split = 3 * PAIR * SIDE_PAIRS
    proj_grad = joined(attn_shard[:, :split], attn_shard[:, split + D :])
    proj_grad = jnp.moveaxis(proj_grad.reshape(rows_here, PAIRS, 3, PAIR), 2, 0).reshape(3, rows_here, D)
    attn_shard = jnp.concatenate([proj_grad, attn_shard[None, :, split : split + D]])
    new_attn = adam_update(
        attn_master, attn_shard, attn_first, attn_second, attn_average, rate_matrix, decay_matrix
    )
    new_small = adam_update(
        small_params, small_total, small_first, small_second, small_average, rate_small, 0.0
    )
    return (block_output, input_grad, *new_attn, *new_ffn, *new_small)


def solution(mesh):
    in_specs = (
        P("dp", "cam", None, None),
        P("dp", "cam", None, None),
        P("dp", None, None),
        P("dp", None, None),
        P(None, ("dp", "cam"), None),
        P(None, ("dp", "cam"), None),
        P(None, ("dp", "cam"), None),
        P(None, ("dp", "cam"), None),
        P(None, ("dp", "cam"), None),
        P(None, ("dp", "cam"), None),
        P(None, ("dp", "cam"), None),
        P(None, ("dp", "cam"), None),
        P(),
        P(),
        P(),
        P(),
    )
    out_specs = (
        P("dp", "cam", None, None),
        P("dp", "cam", None, None),
        P(None, ("dp", "cam"), None),
        P(None, ("dp", "cam"), None),
        P(None, ("dp", "cam"), None),
        P(None, ("dp", "cam"), None),
        P(None, ("dp", "cam"), None),
        P(None, ("dp", "cam"), None),
        P(None, ("dp", "cam"), None),
        P(None, ("dp", "cam"), None),
        P(),
        P(),
        P(),
        P(),
    )
    return jax.shard_map(local, mesh=mesh, in_specs=in_specs, out_specs=out_specs, check_vma=False)
```

```python
import functools

import jax
import jax.numpy as jnp
from jax import lax
from jax.experimental import pallas as pl
from jax.experimental.pallas import tpu as pltpu
from jax.sharding import PartitionSpec as P

D = 512
HEADS = 8
NJ = 14
ADAM_STEP = 10
HD = 64
PAIR = 2 * HD
PAIRS = HEADS // 2
BLOCKS = 32
ROWS = D // BLOCKS
HALF = BLOCKS // 2
CHUNK = 640
SIDE_PAIRS = 2
SIDE_COLS = 3 * PAIR * SIDE_PAIRS
SMALL_BLOCKS = 3
ROW_STEPS = 2

norm_eps = 1e-05
beta_first = 0.5
beta_second = 0.5
adam_eps = 1e-08
rate_matrix = 0.02
rate_small = 0.05
decay_matrix = 0.1
ema_decay = 0.75
log2e = 1.4426950408889634
score_scale = HD**-0.5
F32 = jnp.float32
BF16 = jnp.bfloat16
VMEM_LIMIT = 60 * 2**20
NEXT_TO_NOTHING = pl.CostEstimate(flops=1, bytes_accessed=1, transcendentals=0)


def adam_update(master, grad_total, first_old, second_old, average_old, rate, decay):
    first_new = beta_first * first_old + (1.0 - beta_first) * grad_total
    second_new = beta_second * second_old + (1.0 - beta_second) * grad_total * grad_total
    first_hat = first_new / (1.0 - beta_first**ADAM_STEP)
    second_hat = second_new / (1.0 - beta_second**ADAM_STEP)
    master_new = master - rate * (first_hat / (jnp.sqrt(second_hat) + adam_eps) + decay * master)
    average_new = ema_decay * average_old + (1.0 - ema_decay) * master_new
    return (master_new, first_new, second_new, average_new)


def dot(left, right, left_dim, right_dim):
    return lax.dot_general(
        left, right, (((left_dim,), (right_dim,)), ((), ())), preferred_element_type=F32
    )


DEVICE_BITS = {"x": 2, "y": 4, "z": 8, "Z": 16}
BY_X, BY_Y, BY_YZ = "xyzZ", "yxzZ", "yzxZ"


def apart(position, order, core):
    bits = (DEVICE_BITS[name] for n, name in enumerate(order) if position >> (3 - n) & 1)
    return core + sum(bits)


def row_blocks(device, order):
    for core in range(2):
        for position in range(HALF):
            start = (device ^ apart(position, order, core)) * ROWS
            yield core, position, pl.ds(pl.multiple_of(start, ROWS), ROWS)


def put_rows(target, sides, order, device, part=None, cols=slice(None)):
    for core, position, rows in row_blocks(device, order):
        which, at = divmod(position, HALF // len(sides[core]))
        array = sides[core][which]
        target[rows, :] = array[at] if part is None else array[part, at, :, cols]


def take_rows(source, sides, order, device):
    for core, position, rows in row_blocks(device, order):
        sides[core][position] = source[rows, :].astype(BF16)


def mean_last(values):
    return jnp.sum(values, axis=-1, keepdims=True) * (1.0 / D)


def normal_rows(values):
    centred = values - mean_last(values)
    inverse = lax.rsqrt(mean_last(centred * centred) + norm_eps)
    return centred * inverse, inverse


def normal_back(normal, inverse, grad):
    return inverse * (grad - mean_last(grad) - normal * mean_last(grad * normal))


def column_sum(values):
    return jnp.sum(values, axis=0, keepdims=True)


def small_row(vectors, n):
    pieces = D // PAIR
    return jnp.concatenate([vectors[pieces * n + m : pieces * n + m + 1, :] for m in range(pieces)], axis=1)


def active_joints(where, state, mask):
    here = pl.ds(where[2], 1)
    row = state[0, here, :] * mask[0, here, :].astype(F32)
    shape = (NJ, NJ)
    same = lax.broadcasted_iota(jnp.int32, shape, 0) == lax.broadcasted_iota(jnp.int32, shape, 1)
    return jnp.sum(jnp.where(same, row, 0.0), axis=1, keepdims=True)


def spread_heads(values, other):
    lane = lax.broadcasted_iota(jnp.int32, (1, PAIR), 1)
    low = lane < HD
    return jnp.where(low, values, other), jnp.where(low, other, values)


def attend_kernel(base, seg_len, where, *refs):
    first = base == 0
    if first:
        pieces, joints, refs = refs[:4], refs[4:6], refs[6:]
    else:
        rounded, refs = refs[0], refs[7:]
    sides, vectors, refs = (refs[0:2], refs[2:4]), refs[4], refs[5:]
    if first:
        rounded, top_rows, refs = refs[0], refs[1], refs[2:]
    q_out, k_out, v_out, a_out, l_out, weight, logs = refs
    device, slot = where[0], where[1]

    if first:

        @pl.when(pl.program_id(0) == 0)
        def _():
            for k in range(4):
                start = pl.multiple_of((slot ^ k) * seg_len, 16)
                rounded[pl.ds(start, seg_len), :] = pieces[k][...]
            joint_rows = jnp.concatenate([small_row(vectors, 8 + n) for n in range(NJ)], axis=0)
            joint = column_sum(active_joints(where, *joints) * joint_rows)
            top = rounded[:16, :].astype(F32)
            at = lax.broadcasted_iota(jnp.int32, (16, 1), 0)
            top = jnp.where(at == 1, top + joint, top)
            top_rows[...] = top[:8]
            rounded[:16, :] = top.astype(BF16)

    for part in range(3):
        put_rows(weight.at[:, part * PAIR : (part + 1) * PAIR], sides, BY_X, device, part)
    pair = pl.program_id(0) + base
    bias_q, bias_v = vectors[pl.ds(pair, 1), :], vectors[pl.ds(PAIRS + pair, 1), :]
    projected = dot(rounded[...], weight[...], 1, 0)
    q_out[...] = (projected[:, :PAIR] + bias_q).astype(BF16)
    keys = projected[:, PAIR : 2 * PAIR].astype(BF16)
    values = (projected[:, 2 * PAIR :] + bias_v).astype(BF16)
    k_out[...] = keys
    v_out[...] = values
    lane = lax.broadcasted_iota(jnp.int32, (1, PAIR), 1)
    low = lane < HD
    value_heads = spread_heads(values, jnp.ones_like(values))
    scale = log2e * score_scale
    for step in range(4):
        rows = pl.ds(step * seg_len, seg_len)
        query = q_out[rows, :]
        mixed, tops = [], []
        for query_head, value_head in zip(spread_heads(query, jnp.zeros_like(query)), value_heads):
            scores = dot(query_head, keys, 1, 1)
            top = jnp.max(scores, axis=1, keepdims=True) * scale
            probs = jnp.exp2(scores * scale - top).astype(BF16)
            mixed.append(dot(probs, value_head, 1, 0))
            tops.append(top)
        total = pltpu.roll(jnp.where(low, mixed[1], mixed[0]), HD, 1)
        a_out[rows, :] = (jnp.where(low, mixed[0], mixed[1]) / total).astype(BF16)
        logs[rows, :] = jnp.where(low, tops[0], tops[1]) + jnp.log2(total)
    turned = logs[...].T
    l_out[0:1, :] = turned[0:1]
    l_out[1:2, :] = turned[HD : HD + 1]


def gate_both(values):
    def low(constant):
        return jnp.asarray(constant, BF16)

    values = values.astype(BF16)
    size = jnp.abs(values)
    fraction = low(1.0) / (low(1.0) + low(0.3275911 * 0.5**0.5) * size)
    bell = jnp.exp2(values * values * low(-0.5 * log2e))
    series = low(0.5 * 1.061405429) * fraction - low(0.5 * 1.453152027)
    series = series * fraction + low(0.5 * 1.421413741)
    series = series * fraction - low(0.5 * 0.284496736)
    series = series * fraction + low(0.5 * 0.254829592)
    tail = series * fraction * bell
    bend = size * bell * low(0.3989422804014327) - tail
    slope = jnp.where(values > low(0.0), low(1.0) + bend, -bend)
    return jnp.maximum(values, low(0.0)) - size * tail, slope


def project_kernel(seg_len, where, *refs):
    rounded, top_rows, mixed, sides, vectors = *refs[:3], (refs[3:5], refs[5:7]), refs[7]
    h1_out, normed_out, y1_out, w_out = refs[8:]
    out_scale = (4 * seg_len / 3.0) ** 0.5

    @pl.when(pl.program_id(0) == 0)
    def _():
        put_rows(w_out, sides, BY_X, where[0], 0)

    summed = rounded[...].astype(F32)
    top = jnp.where(pl.program_id(0) == 0, top_rows[...], summed[:8])
    summed = jnp.concatenate([top, summed[8:]], axis=0)
    summed = summed + (dot(mixed[...], w_out[...], 1, 0) * out_scale + small_row(vectors, 2))
    h1_out[...] = summed
    normal, _ = normal_rows(summed)
    result = normal * small_row(vectors, 3) + small_row(vectors, 4)
    normed_out[...] = result
    y1_out[...] = result.astype(BF16)


def forward_kernel(seg_len, where, *refs):
    y1, up_sides, down_sides = refs[0], (refs[1:3], refs[3:5]), (refs[5:7], refs[7:9])
    vectors, normed_in, g_out, slope_out, total, w_up, w_down, normed, arrived = refs[9:]
    load = pltpu.make_async_copy(normed_in, normed, arrived)
    device = where[0]

    @pl.when(pl.program_id(0) == 0)
    def _():
        total[...] = jnp.zeros_like(total)
        load.start()

    put_rows(w_up, up_sides, BY_X, device)
    put_rows(w_down, down_sides, BY_Y, device)
    lanes = vectors.shape[1]
    first_row = (8 + NJ) * (D // lanes) + pl.program_id(0) * (CHUNK // lanes)
    hidden_bias = [vectors[pl.ds(first_row + n, 1), :] for n in range(CHUNK // lanes)]
    hidden_bias = jnp.concatenate(hidden_bias, axis=1)
    for step in range(4):
        rows = pl.ds(step * seg_len, seg_len)
        inner = dot(y1[rows, :], w_up[...], 1, 0) + hidden_bias
        active, slope = gate_both(inner)
        active = active.astype(BF16)
        g_out[rows, :] = active
        slope_out[rows, :] = slope.astype(BF16)
        total[rows, :] += dot(active, w_down[...], 1, 1)

    @pl.when(pl.program_id(0) == pl.num_programs(0) - 1)
    def _():
        load.wait()
        total[...] += normed[...] + small_row(vectors, 5)


def second_kernel(seg_len, where, *refs):
    forward, active, vectors, cotangents, refs = *refs[:3], refs[3:7], refs[7:]
    pieces, dh2_out, df_out, vector_grads, refs = refs[:4], refs[4], refs[5], refs[6], refs[7:]
    down_grads, grad = refs[:2], refs[2]
    device, slot = where[0], where[1]

    @pl.when(pl.program_id(0) == 0)
    def _():
        gain_grad = shift_grad = bias_grad = 0.0
        for k in range(4):
            rows = pl.ds(pl.multiple_of((slot ^ k) * seg_len, 16), seg_len)
            normal, inverse = normal_rows(forward[rows, :])
            pieces[k][...] = (normal * small_row(vectors, 6) + small_row(vectors, 7)).astype(BF16)
            cotangent = cotangents[k][...].astype(F32)
            gain_grad += column_sum(cotangent * normal)
            shift_grad += column_sum(cotangent)
            middle = normal_back(normal, inverse, cotangent * small_row(vectors, 6))
            dh2_out[rows, :] = middle
            rounded = middle.astype(BF16)
            df_out[rows, :] = rounded
            bias_grad += column_sum(rounded.astype(F32))
        vector_grads[0:1, :] = gain_grad
        vector_grads[1:2, :] = shift_grad
        vector_grads[2:3, :] = bias_grad

    grad[...] = dot(df_out[...], active[...], 0, 0)
    take_rows(grad, down_grads, BY_Y, device)


def backward_kernel(seg_len, where, *refs):
    dh2, df, y1, slope, refs = *refs[:4], refs[4:]
    up_sides, down_sides, refs = (refs[0:2], refs[2:4]), (refs[4:6], refs[6:8]), refs[8:]
    up_grads, hidden_grad, total, refs = refs[:2], refs[2], refs[3], refs[4:]
    dz, w_up, w_down, grad = refs
    device = where[0]

    @pl.when(pl.program_id(0) == 0)
    def _():
        total[...] = dh2[...]

    put_rows(w_up, up_sides, BY_X, device)
    put_rows(w_down, down_sides, BY_Y, device)
    bias_grad = 0.0
    for step in range(4):
        rows = pl.ds(step * seg_len, seg_len)
        inner = (dot(df[rows, :], w_down[...], 1, 0) * slope[rows, :].astype(F32)).astype(BF16)
        dz[rows, :] = inner
        bias_grad += column_sum(inner.astype(F32))
        total[rows, :] += dot(inner, w_up[...], 1, 1)
    hidden_grad[...] = bias_grad
    grad[...] = dot(y1[...], dz[...], 0, 0)
    take_rows(grad, up_grads, BY_X, device)


def first_kernel(seg_len, where, *refs):
    above_in, h1, mixed, sides, vectors = *refs[:3], (refs[3:5], refs[5:7]), refs[7]
    dh1_out, da_out, vector_grads, grad_sides, w_out, grad = *refs[8:11], refs[11:13], *refs[13:]
    device, step = where[0], pl.program_id(0)
    out_scale = (4 * seg_len / 3.0) ** 0.5

    @pl.when(step == 0)
    def _():
        put_rows(w_out, sides, BY_X, device, 0)
        vector_grads[...] = jnp.zeros_like(vector_grads)
        grad[...] = jnp.zeros_like(grad)

    normal, inverse = normal_rows(h1[...])
    above = above_in[...]
    vector_grads[0:1, :] += column_sum(above * normal)
    vector_grads[1:2, :] += column_sum(above)
    summed = normal_back(normal, inverse, above * small_row(vectors, 3))
    dh1_out[...] = summed
    rounded = summed.astype(BF16)
    vector_grads[2:3, :] += column_sum(rounded.astype(F32))
    da_out[...] = (dot(rounded, w_out[...], 1, 1) * out_scale).astype(BF16)
    grad[...] += dot(mixed[...], rounded, 0, 0) * out_scale

    @pl.when(step == pl.num_programs(0) - 1)
    def _():
        take_rows(grad, grad_sides, BY_YZ, device)


def attend_back_kernel(aliased, where, *refs):
    q, k, v, a, da, logs, refs = *refs[:6], refs[6:]
    rounded, (keep, send, parts, bias_grads) = refs[0], refs[1 + aliased : 5 + aliased]
    query_turned, grad = refs[5 + aliased :]
    seq_len = q.shape[0]

    queries, mixed_grads = q[...], da[...]
    zeros = jnp.zeros_like(queries)
    query_heads = spread_heads(queries, zeros)
    grad_heads = spread_heads(mixed_grads, zeros)
    product = (mixed_grads.astype(F32) * a[...].astype(F32)).T
    inner = (column_sum(product[:HD]), column_sum(product[HD:]))
    start = 0
    while start < seq_len:
        size = min(256, seq_len - start)
        rows = pl.ds(start, size)
        none = jnp.zeros((size, PAIR), BF16)
        key_grad = value_grad = query_grad = 0.0
        heads = zip(spread_heads(k[rows, :], none), spread_heads(v[rows, :], none))
        for h, (key_head, value_head) in enumerate(heads):
            scores = dot(key_head, queries, 1, 1)
            probs = jnp.exp2(scores * (log2e * score_scale) - logs[h : h + 1, :])
            grads = (probs * (dot(value_head, mixed_grads, 1, 1) - inner[h])).astype(BF16)
            value_grad += dot(probs.astype(BF16), grad_heads[h], 1, 0)
            key_grad += dot(grads, query_heads[h], 1, 0)
            query_grad += dot(key_head, grads, 0, 0)
        parts[rows, PAIR : 2 * PAIR] = (key_grad * score_scale).astype(BF16)
        parts[rows, 2 * PAIR :] = value_grad.astype(BF16)
        if start == 0:
            query_turned[...] = query_grad
        else:
            query_turned[...] += query_grad
        start += size
    parts[:, :PAIR] = (query_turned[...].T * score_scale).astype(BF16)
    bias_grads[0:1, :] = column_sum(parts[:, :PAIR].astype(F32))
    bias_grads[1:2, :] = column_sum(parts[:, 2 * PAIR :].astype(F32))
    grad[...] = dot(rounded[...], parts[...], 0, 0)
    take_rows(grad, (keep, send), BY_YZ, where[0])


def input_back_kernel(far, where, *refs):
    dh1, parts, weight, refs = refs[0:2], refs[2:4], refs[4], refs[5:]
    if far:
        top_dh1, top_parts, joints, small_parts = *refs[:2], refs[2:4], refs[4:10]
        sends, small_out, joined = refs[10:12], *refs[12:]
        top = top_dh1[...] + dot(top_parts[...], weight[...], 1, 1)
        join_small(joined, small_parts, active_joints(where, *joints) * top[1:2, :])
        for n in range(SMALL_BLOCKS):
            small_out[n] = two_parts(joined[n * (ROWS // 2) : (n + 1) * (ROWS // 2)])
    else:
        sends = refs
    for n, send in enumerate(sends):
        send[...] = (dh1[n][...] + dot(parts[n][...], weight[...], 1, 1)).astype(send.dtype)


def call(kernel, name, where, grid, operands, results, scratch, aliases=None):
    def spec(block, index):
        if block is None:
            return pl.BlockSpec(memory_space=pl.ANY)
        if index.__code__.co_argcount == 2:
            return pl.BlockSpec(block, index)
        return pl.BlockSpec(block, lambda i, _: index(i))

    return pl.pallas_call(
        kernel,
        grid_spec=pltpu.PrefetchScalarGridSpec(
            num_scalar_prefetch=1,
            grid=(grid,),
            in_specs=[spec(block, index) for _, block, index in operands],
            out_specs=[spec(block, index) for _, block, index in results],
            scratch_shapes=[pltpu.VMEM(*x) if isinstance(x, tuple) else x for x in scratch],
        ),
        out_shape=[shape for shape, _, _ in results],
        input_output_aliases={source + 1: target for source, target in (aliases or {}).items()},
        compiler_params=pltpu.CompilerParams(vmem_limit_bytes=VMEM_LIMIT),
        cost_estimate=NEXT_TO_NOTHING,
        name=name,
    )(where, *(x for x, _, _ in operands))


def whole(x):
    return (x, x.shape, lambda i: (0,) * len(x.shape))


def shape_of(shape, kind):
    return jax.ShapeDtypeStruct(shape, kind)


def whole_out(shape, kind):
    return whole(shape_of(shape, kind))


def flat(sides):
    return [x for side in sides for x in side]


def pair_weights(sides, base):
    return [(x, (3, x.shape[1], ROWS, PAIR), lambda i: (0, 0, 0, i + base)) for x in flat(sides)]


def attend(base, pairs, where, source, sides, vectors, seg_len):
    seq_len = 4 * seg_len
    first = base == 0

    def column(x):
        return (x, (seq_len, PAIR), lambda i: (0, i + base))

    operands = [whole(x) for x in (source[:4] if first else source[:1])]
    if first:
        operands += [(x, (1, *x.shape[1:]), lambda i, at: (at[1], 0, 0)) for x in source[4:]]
    operands += [] if first else [(x, None, None) for x in source[1:]]
    operands += pair_weights(sides, base) + [whole(vectors)]
    results = [whole_out((seq_len, D), BF16), whole_out((8, D), F32)] if first else []
    results += [column(shape_of((seq_len, D), BF16))] * 4
    logs = shape_of((PAIRS, 2, seq_len), F32)
    results += [(logs, (None, 2, seq_len), lambda i: (i + base, 0, 0))]
    results += [(shape_of((D, 3 * D), BF16), (D, 3 * PAIR), lambda i: (0, i + base))]
    scratch = [((seq_len, PAIR), F32)]
    return call(
        functools.partial(attend_kernel, base, seg_len),
        f"attend_{base}",
        where,
        pairs,
        operands,
        results,
        scratch,
        {} if first else {1 + n: n for n in range(6)},
    )


def by_chunk(x):
    if x.ndim == 3:
        return (x, (x.shape[0], ROWS, CHUNK), lambda i: (0, 0, i))
    return (x, (x.shape[0], CHUNK), lambda i: (0, i))


def out_weight(sides):
    return [(x, (1, x.shape[1], ROWS, D), lambda i: (3, 0, 0, 0)) for x in flat(sides)]


def by_rows(x):
    return (x, (x.shape[0] // ROW_STEPS, x.shape[1]), lambda i: (i, 0))


def project(where, rounded, top_rows, mixed, sides, vectors):
    seq_len = rounded.shape[0]
    return call(
        functools.partial(project_kernel, seq_len // 4),
        "project",
        where,
        ROW_STEPS,
        [by_rows(rounded), whole(top_rows), by_rows(mixed), *out_weight(sides), whole(vectors)],
        [by_rows(shape_of((seq_len, D), kind)) for kind in (F32, F32, BF16)],
        [((D, D), BF16)],
    )


def feed_forward(where, y1, normed, up, down, vectors):
    seq_len = y1.shape[0]
    hidden = up[0][0].shape[-1]
    wide = by_chunk(shape_of((seq_len, hidden), BF16))
    return call(
        functools.partial(forward_kernel, seq_len // 4),
        "feed_forward",
        where,
        hidden // CHUNK,
        [whole(y1)] + [by_chunk(x) for x in (*flat(up), *flat(down))] + [whole(vectors), (normed, None, None)],
        [wide, wide, whole_out((seq_len, D), F32)],
        [((D, CHUNK), BF16)] * 2 + [((seq_len, D), F32), pltpu.SemaphoreType.DMA(())],
    )


def second_norm(where, forward, active, vectors, cotangents):
    seq_len, hidden = active.shape
    seg_len = seq_len // 4
    operands = [whole(forward), by_chunk(active), whole(vectors)]
    results = [whole_out((seg_len, D), BF16)] * 4
    results += [whole_out((seq_len, D), F32), whole_out((seq_len, D), BF16), whole_out((8, D), F32)]
    results += [by_chunk(shape_of((HALF, ROWS, hidden), BF16))] * 2
    return call(
        functools.partial(second_kernel, seg_len),
        "second_norm",
        where,
        hidden // CHUNK,
        operands + [whole(x) for x in cotangents],
        results,
        [((D, CHUNK), F32)],
    )


def feed_back(where, dh2, df, y1, slope, up, down):
    seq_len, hidden = slope.shape
    operands = [whole(dh2), whole(df), whole(y1)] + [by_chunk(x) for x in (slope, *flat(up), *flat(down))]
    results = [by_chunk(shape_of((HALF, ROWS, hidden), BF16))] * 2
    results += [by_chunk(shape_of((1, hidden), F32)), whole_out((seq_len, D), F32)]
    scratch = [((seq_len, CHUNK), BF16)] + [((D, CHUNK), BF16)] * 2 + [((D, CHUNK), F32)]
    return call(
        functools.partial(backward_kernel, seq_len // 4),
        "feed_back",
        where,
        hidden // CHUNK,
        operands,
        results,
        scratch,
    )


def first_norm_back(where, above, h1, mixed, sides, vectors):
    seq_len = h1.shape[0]
    results = [by_rows(shape_of((seq_len, D), kind)) for kind in (F32, BF16)]
    results += [whole_out((8, D), F32)]
    results += [whole_out((HALF, ROWS, D), BF16)] * 2
    return call(
        functools.partial(first_kernel, seq_len // 4),
        "first_norm_back",
        where,
        ROW_STEPS,
        [by_rows(x) for x in (above, h1, mixed)] + [*out_weight(sides), whole(vectors)],
        results,
        [((D, D), BF16), ((D, D), F32)],
    )


def attend_back(base, pairs, where, heads, da, logs, rounded, sides=(), parts=()):
    seq_len = da.shape[0]
    operands = [(x, (seq_len, PAIR), lambda i: (0, i + base)) for x in (*heads, da)]
    operands += [(logs, (None, 2, seq_len), lambda i: (i + base, 0, 0)), whole(rounded)]
    aliases = {len(operands) + n: n for n in range(len(sides))}
    aliases |= {len(operands) + len(sides) + n: 2 for n in range(len(parts))}
    operands += [(x, None, None) for x in (*sides, *parts)]
    side = shape_of((HALF, ROWS, SIDE_COLS), BF16)
    results = [(side, (HALF, ROWS, 3 * PAIR), lambda i: (0, 0, (i + base) % SIDE_PAIRS))] * 2
    results += [(shape_of((seq_len, 3 * D), BF16), (seq_len, 3 * PAIR), lambda i: (0, i + base))]
    results += [(shape_of((8, pairs * PAIR), F32), (8, PAIR), lambda i: (0, i))]
    return call(
        functools.partial(attend_back_kernel, len(sides) + len(parts)),
        f"attend_back_{base}",
        where,
        pairs,
        operands,
        results,
        [((PAIR, seq_len), F32), ((D, 3 * PAIR), F32)],
        aliases,
    )


def input_back(first, where, dh1, parts, weight, joints=(), small=()):
    seg_len = dh1.shape[0] // 4
    far = first == 2

    def segment(x, n):
        return pl.BlockSpec((seg_len, x.shape[1]), lambda i, at: (at[1] ^ (first + n), 0))

    def full(x):
        return pl.BlockSpec(x.shape, lambda i, _: (0,) * len(x.shape))

    operands = [dh1, dh1, parts, parts, weight]
    specs = [segment(x, n) for x in (dh1, parts) for n in range(2)] + [full(weight)]
    results = [shape_of((seg_len, D), BF16 if far or n else F32) for n in range(2)]
    scratch = []
    if far:
        operands += [dh1, parts, *joints, *small]
        specs += [pl.BlockSpec((ROWS, x.shape[1]), lambda i, _: (0, 0)) for x in (dh1, parts)]
        specs += [pl.BlockSpec((1, *x.shape[1:]), lambda i, at: (at[1], 0, 0)) for x in joints]
        specs += [full(x) for x in small]
        results += [shape_of((SMALL_BLOCKS, ROWS, SIDE_COLS), BF16)]
        scratch += [pltpu.VMEM((SMALL_BLOCKS * ROWS // 2, SIDE_COLS), F32)]
    return pl.pallas_call(
        functools.partial(input_back_kernel, far),
        grid_spec=pltpu.PrefetchScalarGridSpec(
            num_scalar_prefetch=1,
            grid=(1,),
            in_specs=specs,
            out_specs=[full(x) for x in results],
            scratch_shapes=scratch,
        ),
        out_shape=results,
        compiler_params=pltpu.CompilerParams(vmem_limit_bytes=VMEM_LIMIT),
        cost_estimate=NEXT_TO_NOTHING,
        name=f"input_back_{first}",
    )(where, *operands)


def join_small(joined, parts, by_joint):
    *biases, first, second, hidden = parts
    units = [x[n : n + 1, :] for n in range(2) for x in biases]
    units += [first[n : n + 1, :] for n in (2, 0, 1)] + [second[n : n + 1, :] for n in (2, 0, 1)]
    units += [by_joint[n : n + 1, :] for n in range(NJ)] + [hidden[...]]
    joined[...] = jnp.zeros_like(joined)
    at, width = 0, joined.shape[1]
    for unit in units:
        taken = 0
        while taken < unit.shape[1]:
            row, column = divmod(at, width)
            size = min(width - column, unit.shape[1] - taken)
            joined[row : row + 1, column : column + size] = unit[:, taken : taken + size]
            taken, at = taken + size, at + size


def two_parts(values):
    high = lax.reduce_precision(values, 8, 7)
    return jnp.concatenate([high, lax.reduce_precision(values - high, 8, 7)], axis=-2).astype(BF16)


def of_parts(parts):
    half = parts.shape[-2] // 2
    return parts[..., :half, :].astype(F32) + parts[..., half:, :].astype(F32)


def arrange_kernel(where, *refs):
    pieces, out, landed, widened, sem_in, sem_out = refs[:4], *refs[4:]
    loads = [pltpu.make_async_copy(x, landed.at[n], sem_in.at[n]) for n, x in enumerate(pieces[1:])]
    loads.append(pltpu.make_async_copy(pieces[0], widened.at[3], sem_in.at[3]))
    for load in loads:
        load.start()
    stores = []
    for n, load in enumerate(loads):
        load.wait()
        if n < 3:
            widened[n] = landed[n].astype(out.dtype)
        target = out.at[where[1] ^ ((n + 1) % 4), 0]
        stores.append(pltpu.make_async_copy(widened.at[n], target, sem_out.at[n]))
        stores[n].start()
    for store in stores:
        store.wait()


def arrange(where, pieces, kind):
    seg_len = pieces[1].shape[0]
    return pl.pallas_call(
        arrange_kernel,
        grid_spec=pltpu.PrefetchScalarGridSpec(
            num_scalar_prefetch=1,
            grid=(1,),
            in_specs=[pl.BlockSpec(memory_space=pl.ANY)] * 4,
            out_specs=pl.BlockSpec(memory_space=pl.ANY),
            scratch_shapes=[
                pltpu.VMEM((3, seg_len, D), BF16),
                pltpu.VMEM((4, seg_len, D), kind),
                pltpu.SemaphoreType.DMA((4,)),
                pltpu.SemaphoreType.DMA((4,)),
            ],
        ),
        out_shape=jax.ShapeDtypeStruct((4, 1, seg_len, D), kind),
        compiler_params=pltpu.CompilerParams(vmem_limit_bytes=VMEM_LIMIT),
        cost_estimate=NEXT_TO_NOTHING,
        name="arrange",
    )(where, *pieces)


def partner(value, axis, mask):
    pairs = [(source, source ^ mask) for source in range(lax.axis_size(axis))]
    return lax.ppermute(value, axis, pairs)


def over_core(value):
    return partner(value, "cam", 1)


def over_x(value):
    return partner(value, "cam", 2)


def over_y(value):
    return partner(value, "dp", 1)


def over_y_and_core(value):
    pairs = [(source, source ^ 5) for source in range(BLOCKS)]
    return lax.ppermute(value, ("dp", "cam"), pairs)


def over_z(value, apart_by):
    return partner(value, "dp", 2 * apart_by)


def stages_of(order):
    return (over_x, over_y) if order == BY_X else (over_y, over_x)


def by_blocks():
    return lax.axis_size("dp") * lax.axis_size("cam") == BLOCKS


def doubled(held, stage, axis=0):
    return jnp.concatenate([held, stage(held)], axis=axis)


def gather_plain(shard, order):
    at = shard.ndim - 2
    full = lax.all_gather(shard, ("dp", "cam"), axis=at, tiled=True)
    full = full.reshape(*full.shape[:at], 2, 2, 2, 2, 2, ROWS, full.shape[-1])
    places = ["Zzyx".index(name) + at for name in order]
    full = jnp.moveaxis(full, (at + 4, *places), (0, *range(at + 1, at + 5)))
    full = full.reshape(2, *shard.shape[:at], HALF, *full.shape[-2:])
    return full[0], full[1]


def split_sides(shard, order, at):
    return tuple(tuple(jnp.split(x, 2, axis=at)) for x in gather_plain(shard, order))


def scatter_plain(sides, order):
    full = jnp.stack(sides).reshape(2, 2, 2, 2, 2, ROWS, sides[0].shape[-1])
    places = (4, *("Zzyx".index(name) for name in order))
    full = jnp.moveaxis(full, range(5), places).reshape(D, sides[0].shape[-1])
    return lax.psum_scatter(full.astype(F32), ("dp", "cam"), scatter_dimension=0, tiled=True)


def halve(held, received):
    half = held.shape[0] // 2

    def part(rows):
        return (held[rows].astype(F32) + received[rows].astype(F32)).astype(BF16)

    return part(slice(0, half)), part(slice(half, None))


def over_low_z(value):
    return over_z(value, 1)


def over_high_z(value):
    return over_z(value, 2)


def add_low(mine, other):
    return mine.astype(F32) + other.astype(F32)


def together(*values):
    return lax.optimization_barrier(values)


def joined(left, right):
    return jnp.concatenate([left, right], axis=-1)


def add_parts(mine, other):
    return two_parts(of_parts(mine) + of_parts(other))


def after(value, *others):
    return lax.optimization_barrier((value, *others))[0]


def local(
    tokens,
    out_grad,
    joint_state,
    joint_mask,
    attn_master,
    attn_first,
    attn_second,
    attn_average,
    ffn_master,
    ffn_first,
    ffn_second,
    ffn_average,
    small_params,
    small_first,
    small_second,
    small_average,
):
    cam_index = lax.axis_index("cam")
    slot, group_index = cam_index % 4, cam_index // 4
    items_here, _, seg_len, _ = tokens.shape
    assert items_here == 4
    device = lax.axis_index("dp") * lax.axis_size("cam") + cam_index if by_blocks() else 0
    where = jnp.stack([jnp.int32(device), jnp.int32(slot), jnp.int32(group_index)])

    def pieces_of(array):
        return [lax.dynamic_index_in_dim(array[:, 0], slot ^ n, 0, keepdims=False) for n in range(4)]

    def new_of_ffn(gradient):
        return adam_update(
            ffn_master, gradient, ffn_first, ffn_second, ffn_average, rate_matrix, decay_matrix
        )

    def trade(pieces):
        return [pieces[0]] + [partner(pieces[n], "cam", n) for n in range(1, 4)]

    blocks = by_blocks()
    sequence = trade(pieces_of(tokens))
    cotangents = pieces_of(out_grad)
    attn_low = attn_master.astype(BF16)
    ffn_low = ffn_master.astype(BF16)
    vectors = small_params.reshape(-1, PAIR)
    joints = joint_state, joint_mask
    here = where
    if blocks:
        held = doubled(attn_low[:, None], over_high_z, 1)
        held, ffn_low = together(held, ffn_low)
        wide = doubled(ffn_low[:, None], over_high_z, 1)
        held = doubled(held, over_low_z, 1)
        held = doubled(held, over_y, 1)
        wide, here, cotangents[1], *sequence = together(wide, here, cotangents[1], *sequence)
        near = held, over_x(held)
        far = tuple(over_core(x) for x in near)
        wide = doubled(wide, over_low_z, 1)
        wide, here, vectors, *far = together(wide, here, vectors, *far)
        sides = near, far
        up, down = doubled(wide[0], over_y), doubled(wide[1], over_x)
    else:
        sides = split_sides(attn_low, BY_X, 1)
        up, down = split_sides(ffn_low[0], BY_X, 0), split_sides(ffn_low[1], BY_Y, 0)

    rounded, top_rows, *heads = attend(0, 1, here, [*sequence, *joints], sides, vectors, seg_len)
    here = where
    if blocks:
        here, up, down, *heads = together(where, up, down, *heads)
        up, down = (up, over_x(up)), (down, over_y(down))
        far = over_core(up[0]), over_core(down[0])
    *heads, logs, weight = attend(1, PAIRS - 1, here, [rounded, *heads], sides, vectors, seg_len)
    here = where
    if blocks:
        here, up_got, down_got, logs, *far = together(where, up[1], down[1], logs, *far)
        up = ((up[0], up_got), (far[0], over_core(up_got)))
        down = ((down[0], down_got), (far[1], over_core(down_got)))
    h1, normed, y1 = project(here, rounded, top_rows, heads[3], sides, vectors)
    cotangents = trade([after(x, y1) for x in cotangents])
    gated, slope, forward = feed_forward(where, y1, normed, up, down, vectors)
    *results, dh2, df, grads_two, down_keep, down_send = second_norm(
        where, forward, gated, vectors, cotangents
    )
    outputs = trade(results)
    down_got = over_core(down_send) if blocks else down_send
    up_keep, up_send, hidden_grad, above = feed_back(where, dh2, df, y1, slope, up, down)
    here, up_send, down_got, *outputs = together(where, up_send, down_got, *outputs)

    def back(base, pairs, here, *filled):
        return attend_back(base, pairs, here, heads, da, logs, rounded, *filled)

    up_got = over_core(up_send) if blocks else up_send
    if blocks:
        down_keep, down_send = halve(down_keep, down_got)
        here, down_keep, down_send = together(here, down_keep, down_send)
    dh1, da, grads_one, out_keep, out_send = first_norm_back(here, above, h1, heads[3], sides, vectors)
    here = where
    if blocks:
        up_got, da = together(up_got, da)
        up_keep, up_send = halve(up_keep, up_got)
        here, up_send, down_send, out_send = together(where, up_send, down_send, out_send)
        up_got, down_got, out_got = over_x(up_send), over_y(down_send), over_core(out_send)
    a_keep, a_send, parts, bias_a = back(0, 2, here)
    here = where
    if blocks:
        up_got, down_got, out_got, bias_a = together(up_got, down_got, out_got, bias_a)
        up_keep, up_send = halve(up_keep, up_got)
        down_keep, down_send = halve(down_keep, down_got)
        here, up_send, down_send, a_send = together(where, up_send, down_send, a_send)
        up_got, down_got, a_got = over_y(up_send), over_x(down_send), over_core(a_send)
    b_keep, b_send, parts, bias_2 = back(2, 1, here, (), (parts,))
    here = where
    if blocks:
        up_got, down_got, a_got, bias_2 = together(up_got, down_got, a_got, bias_2)
        up_keep, up_send = halve(up_keep, up_got)
        down_keep, down_send = halve(down_keep, down_got)
        keep, send = jnp.stack([up_keep, down_keep], 1), jnp.stack([up_send, down_send], 1)
        a_keep, a_send = halve(joined(a_keep, out_keep), joined(a_got, out_got))
        here, send, a_send = together(where, send, a_send)
        got, a_got = over_low_z(send), over_y(a_send)
    b_keep, b_send, parts, bias_3 = back(3, 1, here, (b_keep, b_send), (parts,))
    small = (bias_a, bias_2, bias_3, grads_one, grads_two, hidden_grad)
    here = where
    if blocks:
        got, a_got, bias_3 = together(got, a_got, bias_3)
        keep, send = halve(keep, got)
        a_keep, a_send = halve(a_keep, a_got)
        here, send, a_send, b_send = together(where, send, a_send, b_send)
        got, a_got, b_got = over_high_z(send), over_low_z(a_send), over_core(b_send)
    *sends, tiny = input_back(2, here, dh1, parts, weight, joints, small)
    here = where
    if blocks:
        b_got, tiny, *sends = together(b_got, tiny, *sends)
        b_keep, b_send = halve(b_keep, b_got)
        here, b_send = together(where, b_send)
        b_got, tiny_y = over_y(b_send), over_y(tiny)
        tiny_core, tiny_both = over_core(tiny), over_y_and_core(tiny)
        far_piece = partner(sends[0], "cam", 2)
    near = input_back(0, here, dh1, parts, weight)
    if blocks:
        own, far_piece, a_got, tiny_core, tiny_y, tiny_both, b_got, got = together(
            near[0], far_piece, a_got, tiny_core, tiny_y, tiny_both, b_got, got
        )
        new_ffn = new_of_ffn(add_low(keep[0], got[0]))
        tiny = of_parts(tiny) + of_parts(tiny_core)
        tiny = two_parts(tiny + (of_parts(tiny_y) + of_parts(tiny_both)))
        grad_pieces = [own, over_core(near[1]), far_piece, partner(sends[1], "cam", 3)]
        a_keep, a_send = halve(a_keep, a_got)
        b_keep, b_send = halve(b_keep, b_got)
        send, a_send, new_ffn, outputs = together(
            jnp.concatenate([b_send, tiny]), a_send, together(*new_ffn), together(*outputs)
        )
        got, a_got, block_output, *grad_pieces = together(
            over_low_z(send), over_x(a_send), arrange(where, outputs, BF16), *grad_pieces
        )
        for stage in (over_x, over_high_z):
            half = b_send.shape[0]
            b_keep, b_send = halve(b_keep, got[:half])
            tiny = add_parts(tiny, got[half:])
            send = jnp.concatenate([b_send, tiny])
            if stage is over_x:
                a_keep, a_send = halve(a_keep, a_got)
                send, a_send = together(send, a_send)
                got, a_got = together(over_x(send), over_high_z(a_send))
            else:
                send, *grad_pieces = together(send, *grad_pieces)
                got, input_grad = together(over_high_z(send), arrange(where, grad_pieces, F32))
        attn_shard = joined(add_low(a_keep[0], a_got[0]), add_low(b_keep[0], got[0]))
        small_total = of_parts(tiny) + of_parts(got[1:])
    else:
        grad_pieces = trade([*near, *sends])
        small_total = lax.psum(of_parts(tiny), ("dp", "cam"))
        ffn_grads = (scatter_plain((up_keep, up_got), BY_X), scatter_plain((down_keep, down_got), BY_Y))
        new_ffn = new_of_ffn(jnp.stack(ffn_grads))
        attn_keep = joined(joined(a_keep, out_keep), b_keep)
        attn_send = joined(joined(a_send, out_send), b_send)
        attn_shard = scatter_plain((attn_keep, attn_send), BY_YZ)
        block_output, input_grad = arrange(where, outputs, BF16), arrange(where, grad_pieces, F32)
    small_total = small_total.reshape(-1)[: small_params.size]

    rows_here = attn_master.shape[1]
    split = 3 * PAIR * SIDE_PAIRS
    proj_grad = joined(attn_shard[:, :split], attn_shard[:, split + D :])
    proj_grad = jnp.moveaxis(proj_grad.reshape(rows_here, PAIRS, 3, PAIR), 2, 0).reshape(3, rows_here, D)
    attn_shard = jnp.concatenate([proj_grad, attn_shard[None, :, split : split + D]])
    new_attn = adam_update(
        attn_master, attn_shard, attn_first, attn_second, attn_average, rate_matrix, decay_matrix
    )
    new_small = adam_update(
        small_params, small_total, small_first, small_second, small_average, rate_small, 0.0
    )
    return (block_output, input_grad, *new_attn, *new_ffn, *new_small)


def solution(mesh):
    in_specs = (
        P("dp", "cam", None, None),
        P("dp", "cam", None, None),
        P("dp", None, None),
        P("dp", None, None),
        P(None, ("dp", "cam"), None),
        P(None, ("dp", "cam"), None),
        P(None, ("dp", "cam"), None),
        P(None, ("dp", "cam"), None),
        P(None, ("dp", "cam"), None),
        P(None, ("dp", "cam"), None),
        P(None, ("dp", "cam"), None),
        P(None, ("dp", "cam"), None),
        P(),
        P(),
        P(),
        P(),
    )
    out_specs = (
        P("dp", "cam", None, None),
        P("dp", "cam", None, None),
        P(None, ("dp", "cam"), None),
        P(None, ("dp", "cam"), None),
        P(None, ("dp", "cam"), None),
        P(None, ("dp", "cam"), None),
        P(None, ("dp", "cam"), None),
        P(None, ("dp", "cam"), None),
        P(None, ("dp", "cam"), None),
        P(None, ("dp", "cam"), None),
        P(),
        P(),
        P(),
        P(),
    )
    return jax.shard_map(local, mesh=mesh, in_specs=in_specs, out_specs=out_specs, check_vma=False)
```

```python
import functools

import jax
import jax.numpy as jnp
from jax import lax
from jax.experimental import pallas as pl
from jax.experimental.pallas import tpu as pltpu
from jax.sharding import PartitionSpec as P

D = 512
HEADS = 8
NJ = 14
ADAM_STEP = 10
HD = 64
PAIR = 2 * HD
PAIRS = HEADS // 2
BLOCKS = 32
ROWS = D // BLOCKS
HALF = BLOCKS // 2
CHUNK = 640
SIDE_PAIRS = 2
SIDE_COLS = 3 * PAIR * SIDE_PAIRS
SMALL_BLOCKS = 3
ROW_STEPS = 2

norm_eps = 1e-05
beta_first = 0.5
beta_second = 0.5
adam_eps = 1e-08
rate_matrix = 0.02
rate_small = 0.05
decay_matrix = 0.1
ema_decay = 0.75
log2e = 1.4426950408889634
score_scale = HD**-0.5
F32 = jnp.float32
BF16 = jnp.bfloat16
VMEM_LIMIT = 32 * 2**20
VMEM_LIMIT_FORWARD = 60 * 2**20
NEXT_TO_NOTHING = pl.CostEstimate(flops=1, bytes_accessed=1, transcendentals=0)


def adam_update(master, grad_total, first_old, second_old, average_old, rate, decay):
    first_new = beta_first * first_old + (1.0 - beta_first) * grad_total
    second_new = beta_second * second_old + (1.0 - beta_second) * grad_total * grad_total
    first_hat = first_new / (1.0 - beta_first**ADAM_STEP)
    second_hat = second_new / (1.0 - beta_second**ADAM_STEP)
    master_new = master - rate * (first_hat / (jnp.sqrt(second_hat) + adam_eps) + decay * master)
    average_new = ema_decay * average_old + (1.0 - ema_decay) * master_new
    return (master_new, first_new, second_new, average_new)


def dot(left, right, left_dim, right_dim):
    return lax.dot_general(
        left, right, (((left_dim,), (right_dim,)), ((), ())), preferred_element_type=F32
    )


DEVICE_BITS = {"x": 2, "y": 4, "z": 8, "Z": 16}
BY_X, BY_Y, BY_YZ = "xyzZ", "yxzZ", "yzxZ"


def apart(position, order, core):
    bits = (DEVICE_BITS[name] for n, name in enumerate(order) if position >> (3 - n) & 1)
    return core + sum(bits)


def row_blocks(device, order):
    for core in range(2):
        for position in range(HALF):
            start = (device ^ apart(position, order, core)) * ROWS
            yield core, position, pl.ds(pl.multiple_of(start, ROWS), ROWS)


def put_rows(target, sides, order, device, part=None, cols=slice(None)):
    for core, position, rows in row_blocks(device, order):
        which, at = divmod(position, HALF // len(sides[core]))
        array = sides[core][which]
        target[rows, :] = array[at] if part is None else array[part, at, :, cols]


def take_rows(source, sides, order, device):
    for core, position, rows in row_blocks(device, order):
        sides[core][position] = source[rows, :].astype(BF16)


def mean_last(values):
    return jnp.sum(values, axis=-1, keepdims=True) * (1.0 / D)


def normal_rows(values):
    centred = values - mean_last(values)
    inverse = lax.rsqrt(mean_last(centred * centred) + norm_eps)
    return centred * inverse, inverse


def normal_back(normal, inverse, grad):
    return inverse * (grad - mean_last(grad) - normal * mean_last(grad * normal))


def column_sum(values):
    return jnp.sum(values, axis=0, keepdims=True)


def small_row(vectors, n):
    pieces = D // PAIR
    return jnp.concatenate([vectors[pieces * n + m : pieces * n + m + 1, :] for m in range(pieces)], axis=1)


def active_joints(where, state, mask):
    here = pl.ds(where[2], 1)
    row = state[0, here, :] * mask[0, here, :].astype(F32)
    shape = (NJ, NJ)
    same = lax.broadcasted_iota(jnp.int32, shape, 0) == lax.broadcasted_iota(jnp.int32, shape, 1)
    return jnp.sum(jnp.where(same, row, 0.0), axis=1, keepdims=True)


def spread_heads(values, other):
    lane = lax.broadcasted_iota(jnp.int32, (1, PAIR), 1)
    low = lane < HD
    return jnp.where(low, values, other), jnp.where(low, other, values)


def attend_kernel(base, seg_len, where, *refs):
    first = base == 0
    if first:
        pieces, joints, refs = refs[:4], refs[4:6], refs[6:]
    else:
        rounded, refs = refs[0], refs[7:]
    sides, vectors, refs = (refs[0:2], refs[2:4]), refs[4], refs[5:]
    if first:
        rounded, top_rows, refs = refs[0], refs[1], refs[2:]
    q_out, k_out, v_out, a_out, l_out, weight, logs = refs
    device, slot = where[0], where[1]

    if first:

        @pl.when(pl.program_id(0) == 0)
        def _():
            for k in range(4):
                start = pl.multiple_of((slot ^ k) * seg_len, 16)
                rounded[pl.ds(start, seg_len), :] = pieces[k][...]
            joint_rows = jnp.concatenate([small_row(vectors, 8 + n) for n in range(NJ)], axis=0)
            joint = column_sum(active_joints(where, *joints) * joint_rows)
            top = rounded[:16, :].astype(F32)
            at = lax.broadcasted_iota(jnp.int32, (16, 1), 0)
            top = jnp.where(at == 1, top + joint, top)
            top_rows[...] = top[:8]
            rounded[:16, :] = top.astype(BF16)

    for part in range(3):
        put_rows(weight.at[:, part * PAIR : (part + 1) * PAIR], sides, BY_X, device, part)
    pair = pl.program_id(0) + base
    bias_q, bias_v = vectors[pl.ds(pair, 1), :], vectors[pl.ds(PAIRS + pair, 1), :]
    projected = dot(rounded[...], weight[...], 1, 0)
    q_out[...] = (projected[:, :PAIR] + bias_q).astype(BF16)
    keys = projected[:, PAIR : 2 * PAIR].astype(BF16)
    values = (projected[:, 2 * PAIR :] + bias_v).astype(BF16)
    k_out[...] = keys
    v_out[...] = values
    lane = lax.broadcasted_iota(jnp.int32, (1, PAIR), 1)
    low = lane < HD
    value_heads = spread_heads(values, jnp.ones_like(values))
    scale = log2e * score_scale
    for step in range(4):
        rows = pl.ds(step * seg_len, seg_len)
        query = q_out[rows, :]
        mixed, tops = [], []
        for query_head, value_head in zip(spread_heads(query, jnp.zeros_like(query)), value_heads):
            scores = dot(query_head, keys, 1, 1)
            top = jnp.max(scores, axis=1, keepdims=True) * scale
            probs = jnp.exp2(scores * scale - top).astype(BF16)
            mixed.append(dot(probs, value_head, 1, 0))
            tops.append(top)
        total = pltpu.roll(jnp.where(low, mixed[1], mixed[0]), HD, 1)
        a_out[rows, :] = (jnp.where(low, mixed[0], mixed[1]) / total).astype(BF16)
        logs[rows, :] = jnp.where(low, tops[0], tops[1]) + jnp.log2(total)
    turned = logs[...].T
    l_out[0:1, :] = turned[0:1]
    l_out[1:2, :] = turned[HD : HD + 1]


def gate_both(values):
    def low(constant):
        return jnp.asarray(constant, BF16)

    values = values.astype(BF16)
    size = jnp.abs(values)
    fraction = low(1.0) / (low(1.0) + low(0.3275911 * 0.5**0.5) * size)
    bell = jnp.exp2(values * values * low(-0.5 * log2e))
    series = low(0.5 * 1.061405429) * fraction - low(0.5 * 1.453152027)
    series = series * fraction + low(0.5 * 1.421413741)
    series = series * fraction - low(0.5 * 0.284496736)
    series = series * fraction + low(0.5 * 0.254829592)
    tail = series * fraction * bell
    bend = size * bell * low(0.3989422804014327) - tail
    slope = jnp.where(values > low(0.0), low(1.0) + bend, -bend)
    return jnp.maximum(values, low(0.0)) - size * tail, slope


def project_kernel(seg_len, where, *refs):
    rounded, top_rows, mixed, sides, vectors = *refs[:3], (refs[3:5], refs[5:7]), refs[7]
    h1_out, normed_out, y1_out, w_out = refs[8:]
    out_scale = (4 * seg_len / 3.0) ** 0.5

    @pl.when(pl.program_id(0) == 0)
    def _():
        put_rows(w_out, sides, BY_X, where[0], 0)

    summed = rounded[...].astype(F32)
    top = jnp.where(pl.program_id(0) == 0, top_rows[...], summed[:8])
    summed = jnp.concatenate([top, summed[8:]], axis=0)
    summed = summed + (dot(mixed[...], w_out[...], 1, 0) * out_scale + small_row(vectors, 2))
    h1_out[...] = summed
    normal, _ = normal_rows(summed)
    result = normal * small_row(vectors, 3) + small_row(vectors, 4)
    normed_out[...] = result
    y1_out[...] = result.astype(BF16)


def forward_kernel(seg_len, where, *refs):
    y1, up_sides, down_sides = refs[0], (refs[1:3], refs[3:5]), (refs[5:7], refs[7:9])
    vectors, normed_in, g_out, slope_out, total, w_up, w_down, normed, arrived = refs[9:]
    load = pltpu.make_async_copy(normed_in, normed, arrived)
    device = where[0]

    @pl.when(pl.program_id(0) == 0)
    def _():
        total[...] = jnp.zeros_like(total)
        load.start()

    put_rows(w_up, up_sides, BY_X, device)
    put_rows(w_down, down_sides, BY_Y, device)
    lanes = vectors.shape[1]
    first_row = (8 + NJ) * (D // lanes) + pl.program_id(0) * (CHUNK // lanes)
    hidden_bias = [vectors[pl.ds(first_row + n, 1), :] for n in range(CHUNK // lanes)]
    hidden_bias = jnp.concatenate(hidden_bias, axis=1)
    for step in range(4):
        rows = pl.ds(step * seg_len, seg_len)
        inner = dot(y1[rows, :], w_up[...], 1, 0) + hidden_bias
        active, slope = gate_both(inner)
        active = active.astype(BF16)
        g_out[rows, :] = active
        slope_out[rows, :] = slope.astype(BF16)
        total[rows, :] += dot(active, w_down[...], 1, 1)

    @pl.when(pl.program_id(0) == pl.num_programs(0) - 1)
    def _():
        load.wait()
        total[...] += normed[...] + small_row(vectors, 5)


def second_kernel(seg_len, where, *refs):
    forward, active, vectors, cotangents, refs = *refs[:3], refs[3:7], refs[7:]
    pieces, dh2_out, df_out, vector_grads, refs = refs[:4], refs[4], refs[5], refs[6], refs[7:]
    down_grads, grad = refs[:2], refs[2]
    device, slot = where[0], where[1]

    @pl.when(pl.program_id(0) == 0)
    def _():
        gain_grad = shift_grad = bias_grad = 0.0
        for k in range(4):
            rows = pl.ds(pl.multiple_of((slot ^ k) * seg_len, 16), seg_len)
            normal, inverse = normal_rows(forward[rows, :])
            pieces[k][...] = (normal * small_row(vectors, 6) + small_row(vectors, 7)).astype(BF16)
            cotangent = cotangents[k][...].astype(F32)
            gain_grad += column_sum(cotangent * normal)
            shift_grad += column_sum(cotangent)
            middle = normal_back(normal, inverse, cotangent * small_row(vectors, 6))
            dh2_out[rows, :] = middle
            rounded = middle.astype(BF16)
            df_out[rows, :] = rounded
            bias_grad += column_sum(rounded.astype(F32))
        vector_grads[0:1, :] = gain_grad
        vector_grads[1:2, :] = shift_grad
        vector_grads[2:3, :] = bias_grad

    grad[...] = dot(df_out[...], active[...], 0, 0)
    take_rows(grad, down_grads, BY_Y, device)


def backward_kernel(seg_len, where, *refs):
    dh2, df, y1, slope, refs = *refs[:4], refs[4:]
    up_sides, down_sides, refs = (refs[0:2], refs[2:4]), (refs[4:6], refs[6:8]), refs[8:]
    up_grads, hidden_grad, total, refs = refs[:2], refs[2], refs[3], refs[4:]
    dz, w_up, w_down, grad = refs
    device = where[0]

    @pl.when(pl.program_id(0) == 0)
    def _():
        total[...] = dh2[...]

    put_rows(w_up, up_sides, BY_X, device)
    put_rows(w_down, down_sides, BY_Y, device)
    bias_grad = 0.0
    for step in range(4):
        rows = pl.ds(step * seg_len, seg_len)
        inner = (dot(df[rows, :], w_down[...], 1, 0) * slope[rows, :].astype(F32)).astype(BF16)
        dz[rows, :] = inner
        bias_grad += column_sum(inner.astype(F32))
        total[rows, :] += dot(inner, w_up[...], 1, 1)
    hidden_grad[...] = bias_grad
    grad[...] = dot(y1[...], dz[...], 0, 0)
    take_rows(grad, up_grads, BY_X, device)


def first_kernel(seg_len, where, *refs):
    above_in, h1, mixed, sides, vectors = *refs[:3], (refs[3:5], refs[5:7]), refs[7]
    dh1_out, da_out, vector_grads, grad_sides, w_out, grad = *refs[8:11], refs[11:13], *refs[13:]
    device, step = where[0], pl.program_id(0)
    out_scale = (4 * seg_len / 3.0) ** 0.5

    @pl.when(step == 0)
    def _():
        put_rows(w_out, sides, BY_X, device, 0)
        vector_grads[...] = jnp.zeros_like(vector_grads)
        grad[...] = jnp.zeros_like(grad)

    normal, inverse = normal_rows(h1[...])
    above = above_in[...]
    vector_grads[0:1, :] += column_sum(above * normal)
    vector_grads[1:2, :] += column_sum(above)
    summed = normal_back(normal, inverse, above * small_row(vectors, 3))
    dh1_out[...] = summed
    rounded = summed.astype(BF16)
    vector_grads[2:3, :] += column_sum(rounded.astype(F32))
    da_out[...] = (dot(rounded, w_out[...], 1, 1) * out_scale).astype(BF16)
    grad[...] += dot(mixed[...], rounded, 0, 0) * out_scale

    @pl.when(step == pl.num_programs(0) - 1)
    def _():
        take_rows(grad, grad_sides, BY_YZ, device)


def attend_back_kernel(aliased, where, *refs):
    q, k, v, a, da, logs, refs = *refs[:6], refs[6:]
    rounded, (keep, send, parts, bias_grads) = refs[0], refs[1 + aliased : 5 + aliased]
    query_turned, grad = refs[5 + aliased :]
    seq_len = q.shape[0]

    queries, mixed_grads = q[...], da[...]
    zeros = jnp.zeros_like(queries)
    query_heads = spread_heads(queries, zeros)
    grad_heads = spread_heads(mixed_grads, zeros)
    product = (mixed_grads.astype(F32) * a[...].astype(F32)).T
    inner = (column_sum(product[:HD]), column_sum(product[HD:]))
    start = 0
    while start < seq_len:
        size = min(256, seq_len - start)
        rows = pl.ds(start, size)
        none = jnp.zeros((size, PAIR), BF16)
        key_grad = value_grad = query_grad = 0.0
        heads = zip(spread_heads(k[rows, :], none), spread_heads(v[rows, :], none))
        for h, (key_head, value_head) in enumerate(heads):
            scores = dot(key_head, queries, 1, 1)
            probs = jnp.exp2(scores * (log2e * score_scale) - logs[h : h + 1, :])
            grads = (probs * (dot(value_head, mixed_grads, 1, 1) - inner[h])).astype(BF16)
            value_grad += dot(probs.astype(BF16), grad_heads[h], 1, 0)
            key_grad += dot(grads, query_heads[h], 1, 0)
            query_grad += dot(key_head, grads, 0, 0)
        parts[rows, PAIR : 2 * PAIR] = (key_grad * score_scale).astype(BF16)
        parts[rows, 2 * PAIR :] = value_grad.astype(BF16)
        if start == 0:
            query_turned[...] = query_grad
        else:
            query_turned[...] += query_grad
        start += size
    parts[:, :PAIR] = (query_turned[...].T * score_scale).astype(BF16)
    bias_grads[0:1, :] = column_sum(parts[:, :PAIR].astype(F32))
    bias_grads[1:2, :] = column_sum(parts[:, 2 * PAIR :].astype(F32))
    grad[...] = dot(rounded[...], parts[...], 0, 0)
    take_rows(grad, (keep, send), BY_YZ, where[0])


def input_back_kernel(far, where, *refs):
    dh1, parts, weight, refs = refs[0:2], refs[2:4], refs[4], refs[5:]
    if far:
        top_dh1, top_parts, joints, small_parts = *refs[:2], refs[2:4], refs[4:10]
        sends, small_out, joined = refs[10:12], *refs[12:]
        top = top_dh1[...] + dot(top_parts[...], weight[...], 1, 1)
        join_small(joined, small_parts, active_joints(where, *joints) * top[1:2, :])
        for n in range(SMALL_BLOCKS):
            small_out[n] = two_parts(joined[n * (ROWS // 2) : (n + 1) * (ROWS // 2)])
    else:
        sends = refs
    for n, send in enumerate(sends):
        send[...] = (dh1[n][...] + dot(parts[n][...], weight[...], 1, 1)).astype(send.dtype)


def call(kernel, name, where, grid, operands, results, scratch, aliases=None, limit=VMEM_LIMIT):
    def spec(block, index):
        if block is None:
            return pl.BlockSpec(memory_space=pl.ANY)
        if index.__code__.co_argcount == 2:
            return pl.BlockSpec(block, index)
        return pl.BlockSpec(block, lambda i, _: index(i))

    return pl.pallas_call(
        kernel,
        grid_spec=pltpu.PrefetchScalarGridSpec(
            num_scalar_prefetch=1,
            grid=(grid,),
            in_specs=[spec(block, index) for _, block, index in operands],
            out_specs=[spec(block, index) for _, block, index in results],
            scratch_shapes=[pltpu.VMEM(*x) if isinstance(x, tuple) else x for x in scratch],
        ),
        out_shape=[shape for shape, _, _ in results],
        input_output_aliases={source + 1: target for source, target in (aliases or {}).items()},
        compiler_params=pltpu.CompilerParams(vmem_limit_bytes=limit),
        cost_estimate=NEXT_TO_NOTHING,
        name=name,
    )(where, *(x for x, _, _ in operands))


def whole(x):
    return (x, x.shape, lambda i: (0,) * len(x.shape))


def shape_of(shape, kind):
    return jax.ShapeDtypeStruct(shape, kind)


def whole_out(shape, kind):
    return whole(shape_of(shape, kind))


def flat(sides):
    return [x for side in sides for x in side]


def pair_weights(sides, base):
    return [(x, (3, x.shape[1], ROWS, PAIR), lambda i: (0, 0, 0, i + base)) for x in flat(sides)]


def attend(base, pairs, where, source, sides, vectors, seg_len):
    seq_len = 4 * seg_len
    first = base == 0

    def column(x):
        return (x, (seq_len, PAIR), lambda i: (0, i + base))

    operands = [whole(x) for x in (source[:4] if first else source[:1])]
    if first:
        operands += [(x, (1, *x.shape[1:]), lambda i, at: (at[1], 0, 0)) for x in source[4:]]
    operands += [] if first else [(x, None, None) for x in source[1:]]
    operands += pair_weights(sides, base) + [whole(vectors)]
    results = [whole_out((seq_len, D), BF16), whole_out((8, D), F32)] if first else []
    results += [column(shape_of((seq_len, D), BF16))] * 4
    logs = shape_of((PAIRS, 2, seq_len), F32)
    results += [(logs, (None, 2, seq_len), lambda i: (i + base, 0, 0))]
    results += [(shape_of((D, 3 * D), BF16), (D, 3 * PAIR), lambda i: (0, i + base))]
    scratch = [((seq_len, PAIR), F32)]
    return call(
        functools.partial(attend_kernel, base, seg_len),
        f"attend_{base}",
        where,
        pairs,
        operands,
        results,
        scratch,
        {} if first else {1 + n: n for n in range(6)},
        limit=VMEM_LIMIT_FORWARD,
    )


def by_chunk(x):
    if x.ndim == 3:
        return (x, (x.shape[0], ROWS, CHUNK), lambda i: (0, 0, i))
    return (x, (x.shape[0], CHUNK), lambda i: (0, i))


def out_weight(sides):
    return [(x, (1, x.shape[1], ROWS, D), lambda i: (3, 0, 0, 0)) for x in flat(sides)]


def by_rows(x):
    return (x, (x.shape[0] // ROW_STEPS, x.shape[1]), lambda i: (i, 0))


def project(where, rounded, top_rows, mixed, sides, vectors):
    seq_len = rounded.shape[0]
    return call(
        functools.partial(project_kernel, seq_len // 4),
        "project",
        where,
        ROW_STEPS,
        [by_rows(rounded), whole(top_rows), by_rows(mixed), *out_weight(sides), whole(vectors)],
        [by_rows(shape_of((seq_len, D), kind)) for kind in (F32, F32, BF16)],
        [((D, D), BF16)],
        limit=VMEM_LIMIT_FORWARD,
    )


def feed_forward(where, y1, normed, up, down, vectors):
    seq_len = y1.shape[0]
    hidden = up[0][0].shape[-1]
    wide = by_chunk(shape_of((seq_len, hidden), BF16))
    return call(
        functools.partial(forward_kernel, seq_len // 4),
        "feed_forward",
        where,
        hidden // CHUNK,
        [whole(y1)] + [by_chunk(x) for x in (*flat(up), *flat(down))] + [whole(vectors), (normed, None, None)],
        [wide, wide, whole_out((seq_len, D), F32)],
        [((D, CHUNK), BF16)] * 2 + [((seq_len, D), F32), pltpu.SemaphoreType.DMA(())],
        limit=VMEM_LIMIT_FORWARD,
    )


def second_norm(where, forward, active, vectors, cotangents):
    seq_len, hidden = active.shape
    seg_len = seq_len // 4
    operands = [whole(forward), by_chunk(active), whole(vectors)]
    results = [whole_out((seg_len, D), BF16)] * 4
    results += [whole_out((seq_len, D), F32), whole_out((seq_len, D), BF16), whole_out((8, D), F32)]
    results += [by_chunk(shape_of((HALF, ROWS, hidden), BF16))] * 2
    return call(
        functools.partial(second_kernel, seg_len),
        "second_norm",
        where,
        hidden // CHUNK,
        operands + [whole(x) for x in cotangents],
        results,
        [((D, CHUNK), F32)],
        limit=VMEM_LIMIT_FORWARD,
    )


def feed_back(where, dh2, df, y1, slope, up, down):
    seq_len, hidden = slope.shape
    operands = [whole(dh2), whole(df), whole(y1)] + [by_chunk(x) for x in (slope, *flat(up), *flat(down))]
    results = [by_chunk(shape_of((HALF, ROWS, hidden), BF16))] * 2
    results += [by_chunk(shape_of((1, hidden), F32)), whole_out((seq_len, D), F32)]
    scratch = [((seq_len, CHUNK), BF16)] + [((D, CHUNK), BF16)] * 2 + [((D, CHUNK), F32)]
    return call(
        functools.partial(backward_kernel, seq_len // 4),
        "feed_back",
        where,
        hidden // CHUNK,
        operands,
        results,
        scratch,
        limit=VMEM_LIMIT_FORWARD,
    )


def first_norm_back(where, above, h1, mixed, sides, vectors):
    seq_len = h1.shape[0]
    results = [by_rows(shape_of((seq_len, D), kind)) for kind in (F32, BF16)]
    results += [whole_out((8, D), F32)]
    results += [whole_out((HALF, ROWS, D), BF16)] * 2
    return call(
        functools.partial(first_kernel, seq_len // 4),
        "first_norm_back",
        where,
        ROW_STEPS,
        [by_rows(x) for x in (above, h1, mixed)] + [*out_weight(sides), whole(vectors)],
        results,
        [((D, D), BF16), ((D, D), F32)],
    )


def attend_back(base, pairs, where, heads, da, logs, rounded, sides=(), parts=()):
    seq_len = da.shape[0]
    operands = [(x, (seq_len, PAIR), lambda i: (0, i + base)) for x in (*heads, da)]
    operands += [(logs, (None, 2, seq_len), lambda i: (i + base, 0, 0)), whole(rounded)]
    aliases = {len(operands) + n: n for n in range(len(sides))}
    aliases |= {len(operands) + len(sides) + n: 2 for n in range(len(parts))}
    operands += [(x, None, None) for x in (*sides, *parts)]
    side = shape_of((HALF, ROWS, SIDE_COLS), BF16)
    results = [(side, (HALF, ROWS, 3 * PAIR), lambda i: (0, 0, (i + base) % SIDE_PAIRS))] * 2
    results += [(shape_of((seq_len, 3 * D), BF16), (seq_len, 3 * PAIR), lambda i: (0, i + base))]
    results += [(shape_of((8, pairs * PAIR), F32), (8, PAIR), lambda i: (0, i))]
    return call(
        functools.partial(attend_back_kernel, len(sides) + len(parts)),
        f"attend_back_{base}",
        where,
        pairs,
        operands,
        results,
        [((PAIR, seq_len), F32), ((D, 3 * PAIR), F32)],
        aliases,
    )


def input_back(first, where, dh1, parts, weight, joints=(), small=()):
    seg_len = dh1.shape[0] // 4
    far = first == 2

    def segment(x, n):
        return pl.BlockSpec((seg_len, x.shape[1]), lambda i, at: (at[1] ^ (first + n), 0))

    def full(x):
        return pl.BlockSpec(x.shape, lambda i, _: (0,) * len(x.shape))

    operands = [dh1, dh1, parts, parts, weight]
    specs = [segment(x, n) for x in (dh1, parts) for n in range(2)] + [full(weight)]
    results = [shape_of((seg_len, D), BF16 if far or n else F32) for n in range(2)]
    scratch = []
    if far:
        operands += [dh1, parts, *joints, *small]
        specs += [pl.BlockSpec((ROWS, x.shape[1]), lambda i, _: (0, 0)) for x in (dh1, parts)]
        specs += [pl.BlockSpec((1, *x.shape[1:]), lambda i, at: (at[1], 0, 0)) for x in joints]
        specs += [full(x) for x in small]
        results += [shape_of((SMALL_BLOCKS, ROWS, SIDE_COLS), BF16)]
        scratch += [pltpu.VMEM((SMALL_BLOCKS * ROWS // 2, SIDE_COLS), F32)]
    return pl.pallas_call(
        functools.partial(input_back_kernel, far),
        grid_spec=pltpu.PrefetchScalarGridSpec(
            num_scalar_prefetch=1,
            grid=(1,),
            in_specs=specs,
            out_specs=[full(x) for x in results],
            scratch_shapes=scratch,
        ),
        out_shape=results,
        compiler_params=pltpu.CompilerParams(vmem_limit_bytes=VMEM_LIMIT),
        cost_estimate=NEXT_TO_NOTHING,
        name=f"input_back_{first}",
    )(where, *operands)


def join_small(joined, parts, by_joint):
    *biases, first, second, hidden = parts
    units = [x[n : n + 1, :] for n in range(2) for x in biases]
    units += [first[n : n + 1, :] for n in (2, 0, 1)] + [second[n : n + 1, :] for n in (2, 0, 1)]
    units += [by_joint[n : n + 1, :] for n in range(NJ)] + [hidden[...]]
    joined[...] = jnp.zeros_like(joined)
    at, width = 0, joined.shape[1]
    for unit in units:
        taken = 0
        while taken < unit.shape[1]:
            row, column = divmod(at, width)
            size = min(width - column, unit.shape[1] - taken)
            joined[row : row + 1, column : column + size] = unit[:, taken : taken + size]
            taken, at = taken + size, at + size


def two_parts(values):
    high = lax.reduce_precision(values, 8, 7)
    return jnp.concatenate([high, lax.reduce_precision(values - high, 8, 7)], axis=-2).astype(BF16)


def of_parts(parts):
    half = parts.shape[-2] // 2
    return parts[..., :half, :].astype(F32) + parts[..., half:, :].astype(F32)


def arrange_kernel(where, *refs):
    pieces, out, landed, widened, sem_in, sem_out = refs[:4], *refs[4:]
    loads = [pltpu.make_async_copy(x, landed.at[n], sem_in.at[n]) for n, x in enumerate(pieces[1:])]
    loads.append(pltpu.make_async_copy(pieces[0], widened.at[3], sem_in.at[3]))
    for load in loads:
        load.start()
    stores = []
    for n, load in enumerate(loads):
        load.wait()
        if n < 3:
            widened[n] = landed[n].astype(out.dtype)
        target = out.at[where[1] ^ ((n + 1) % 4), 0]
        stores.append(pltpu.make_async_copy(widened.at[n], target, sem_out.at[n]))
        stores[n].start()
    for store in stores:
        store.wait()


def arrange(where, pieces, kind):
    seg_len = pieces[1].shape[0]
    return pl.pallas_call(
        arrange_kernel,
        grid_spec=pltpu.PrefetchScalarGridSpec(
            num_scalar_prefetch=1,
            grid=(1,),
            in_specs=[pl.BlockSpec(memory_space=pl.ANY)] * 4,
            out_specs=pl.BlockSpec(memory_space=pl.ANY),
            scratch_shapes=[
                pltpu.VMEM((3, seg_len, D), BF16),
                pltpu.VMEM((4, seg_len, D), kind),
                pltpu.SemaphoreType.DMA((4,)),
                pltpu.SemaphoreType.DMA((4,)),
            ],
        ),
        out_shape=jax.ShapeDtypeStruct((4, 1, seg_len, D), kind),
        compiler_params=pltpu.CompilerParams(vmem_limit_bytes=VMEM_LIMIT),
        cost_estimate=NEXT_TO_NOTHING,
        name="arrange",
    )(where, *pieces)


def partner(value, axis, mask):
    pairs = [(source, source ^ mask) for source in range(lax.axis_size(axis))]
    return lax.ppermute(value, axis, pairs)


def over_core(value):
    return partner(value, "cam", 1)


def over_x(value):
    return partner(value, "cam", 2)


def over_y(value):
    return partner(value, "dp", 1)


def over_y_and_core(value):
    pairs = [(source, source ^ 5) for source in range(BLOCKS)]
    return lax.ppermute(value, ("dp", "cam"), pairs)


def over_z(value, apart_by):
    return partner(value, "dp", 2 * apart_by)


def stages_of(order):
    return (over_x, over_y) if order == BY_X else (over_y, over_x)


def by_blocks():
    return lax.axis_size("dp") * lax.axis_size("cam") == BLOCKS


def doubled(held, stage, axis=0):
    return jnp.concatenate([held, stage(held)], axis=axis)


def gather_plain(shard, order):
    at = shard.ndim - 2
    full = lax.all_gather(shard, ("dp", "cam"), axis=at, tiled=True)
    full = full.reshape(*full.shape[:at], 2, 2, 2, 2, 2, ROWS, full.shape[-1])
    places = ["Zzyx".index(name) + at for name in order]
    full = jnp.moveaxis(full, (at + 4, *places), (0, *range(at + 1, at + 5)))
    full = full.reshape(2, *shard.shape[:at], HALF, *full.shape[-2:])
    return full[0], full[1]


def split_sides(shard, order, at):
    return tuple(tuple(jnp.split(x, 2, axis=at)) for x in gather_plain(shard, order))


def scatter_plain(sides, order):
    full = jnp.stack(sides).reshape(2, 2, 2, 2, 2, ROWS, sides[0].shape[-1])
    places = (4, *("Zzyx".index(name) for name in order))
    full = jnp.moveaxis(full, range(5), places).reshape(D, sides[0].shape[-1])
    return lax.psum_scatter(full.astype(F32), ("dp", "cam"), scatter_dimension=0, tiled=True)


def halve(held, received):
    half = held.shape[0] // 2

    def part(rows):
        return (held[rows].astype(F32) + received[rows].astype(F32)).astype(BF16)

    return part(slice(0, half)), part(slice(half, None))


def over_low_z(value):
    return over_z(value, 1)


def over_high_z(value):
    return over_z(value, 2)


def add_low(mine, other):
    return mine.astype(F32) + other.astype(F32)


def together(*values):
    return lax.optimization_barrier(values)


def joined(left, right):
    return jnp.concatenate([left, right], axis=-1)


def add_parts(mine, other):
    return two_parts(of_parts(mine) + of_parts(other))


def after(value, *others):
    return lax.optimization_barrier((value, *others))[0]


def local(
    tokens,
    out_grad,
    joint_state,
    joint_mask,
    attn_master,
    attn_first,
    attn_second,
    attn_average,
    ffn_master,
    ffn_first,
    ffn_second,
    ffn_average,
    small_params,
    small_first,
    small_second,
    small_average,
):
    cam_index = lax.axis_index("cam")
    slot, group_index = cam_index % 4, cam_index // 4
    items_here, _, seg_len, _ = tokens.shape
    assert items_here == 4
    device = lax.axis_index("dp") * lax.axis_size("cam") + cam_index if by_blocks() else 0
    where = jnp.stack([jnp.int32(device), jnp.int32(slot), jnp.int32(group_index)])

    def pieces_of(array):
        return [lax.dynamic_index_in_dim(array[:, 0], slot ^ n, 0, keepdims=False) for n in range(4)]

    def new_of_ffn(gradient):
        return adam_update(
            ffn_master, gradient, ffn_first, ffn_second, ffn_average, rate_matrix, decay_matrix
        )

    def trade(pieces):
        return [pieces[0]] + [partner(pieces[n], "cam", n) for n in range(1, 4)]

    blocks = by_blocks()
    sequence = trade(pieces_of(tokens))
    cotangents = pieces_of(out_grad)
    attn_low = attn_master.astype(BF16)
    ffn_low = ffn_master.astype(BF16)
    vectors = small_params.reshape(-1, PAIR)
    joints = joint_state, joint_mask
    here = where
    if blocks:
        held = doubled(attn_low[:, None], over_high_z, 1)
        held, ffn_low = together(held, ffn_low)
        wide = doubled(ffn_low[:, None], over_high_z, 1)
        held = doubled(held, over_low_z, 1)
        held = doubled(held, over_y, 1)
        wide, here, cotangents[1], *sequence = together(wide, here, cotangents[1], *sequence)
        near = held, over_x(held)
        far = tuple(over_core(x) for x in near)
        wide = doubled(wide, over_low_z, 1)
        wide, here, vectors, *far = together(wide, here, vectors, *far)
        sides = near, far
        up, down = doubled(wide[0], over_y), doubled(wide[1], over_x)
    else:
        sides = split_sides(attn_low, BY_X, 1)
        up, down = split_sides(ffn_low[0], BY_X, 0), split_sides(ffn_low[1], BY_Y, 0)

    rounded, top_rows, *heads = attend(0, 1, here, [*sequence, *joints], sides, vectors, seg_len)
    here = where
    if blocks:
        here, up, down, *heads = together(where, up, down, *heads)
        up, down = (up, over_x(up)), (down, over_y(down))
        far = over_core(up[0]), over_core(down[0])
    *heads, logs, weight = attend(1, PAIRS - 1, here, [rounded, *heads], sides, vectors, seg_len)
    here = where
    if blocks:
        here, up_got, down_got, logs, *far = together(where, up[1], down[1], logs, *far)
        up = ((up[0], up_got), (far[0], over_core(up_got)))
        down = ((down[0], down_got), (far[1], over_core(down_got)))
    h1, normed, y1 = project(here, rounded, top_rows, heads[3], sides, vectors)
    cotangents = trade([after(x, y1) for x in cotangents])
    gated, slope, forward = feed_forward(where, y1, normed, up, down, vectors)
    *results, dh2, df, grads_two, down_keep, down_send = second_norm(
        where, forward, gated, vectors, cotangents
    )
    outputs = trade(results)
    down_got = over_core(down_send) if blocks else down_send
    up_keep, up_send, hidden_grad, above = feed_back(where, dh2, df, y1, slope, up, down)
    here, up_send, down_got, *outputs = together(where, up_send, down_got, *outputs)

    def back(base, pairs, here, *filled):
        return attend_back(base, pairs, here, heads, da, logs, rounded, *filled)

    up_got = over_core(up_send) if blocks else up_send
    if blocks:
        down_keep, down_send = halve(down_keep, down_got)
        here, down_keep, down_send = together(here, down_keep, down_send)
    dh1, da, grads_one, out_keep, out_send = first_norm_back(here, above, h1, heads[3], sides, vectors)
    here = where
    if blocks:
        up_got, da = together(up_got, da)
        up_keep, up_send = halve(up_keep, up_got)
        here, up_send, down_send, out_send = together(where, up_send, down_send, out_send)
        up_got, down_got, out_got = over_x(up_send), over_y(down_send), over_core(out_send)
    a_keep, a_send, parts, bias_a = back(0, 2, here)
    here = where
    if blocks:
        up_got, down_got, out_got, bias_a = together(up_got, down_got, out_got, bias_a)
        up_keep, up_send = halve(up_keep, up_got)
        down_keep, down_send = halve(down_keep, down_got)
        here, up_send, down_send, a_send = together(where, up_send, down_send, a_send)
        up_got, down_got, a_got = over_y(up_send), over_x(down_send), over_core(a_send)
    b_keep, b_send, parts, bias_2 = back(2, 1, here, (), (parts,))
    here = where
    if blocks:
        up_got, down_got, a_got, bias_2 = together(up_got, down_got, a_got, bias_2)
        up_keep, up_send = halve(up_keep, up_got)
        down_keep, down_send = halve(down_keep, down_got)
        keep, send = jnp.stack([up_keep, down_keep], 1), jnp.stack([up_send, down_send], 1)
        a_keep, a_send = halve(joined(a_keep, out_keep), joined(a_got, out_got))
        here, send, a_send = together(where, send, a_send)
        got, a_got = over_low_z(send), over_y(a_send)
    b_keep, b_send, parts, bias_3 = back(3, 1, here, (b_keep, b_send), (parts,))
    small = (bias_a, bias_2, bias_3, grads_one, grads_two, hidden_grad)
    here = where
    if blocks:
        got, a_got, bias_3 = together(got, a_got, bias_3)
        keep, send = halve(keep, got)
        a_keep, a_send = halve(a_keep, a_got)
        here, send, a_send, b_send = together(where, send, a_send, b_send)
        got, a_got, b_got = over_high_z(send), over_low_z(a_send), over_core(b_send)
    *sends, tiny = input_back(2, here, dh1, parts, weight, joints, small)
    here = where
    if blocks:
        b_got, tiny, *sends = together(b_got, tiny, *sends)
        b_keep, b_send = halve(b_keep, b_got)
        here, b_send = together(where, b_send)
        b_got, tiny_y = over_y(b_send), over_y(tiny)
        tiny_core, tiny_both = over_core(tiny), over_y_and_core(tiny)
        far_piece = partner(sends[0], "cam", 2)
    near = input_back(0, here, dh1, parts, weight)
    if blocks:
        own, far_piece, a_got, tiny_core, tiny_y, tiny_both, b_got, got = together(
            near[0], far_piece, a_got, tiny_core, tiny_y, tiny_both, b_got, got
        )
        new_ffn = new_of_ffn(add_low(keep[0], got[0]))
        tiny = of_parts(tiny) + of_parts(tiny_core)
        tiny = two_parts(tiny + (of_parts(tiny_y) + of_parts(tiny_both)))
        grad_pieces = [own, over_core(near[1]), far_piece, partner(sends[1], "cam", 3)]
        a_keep, a_send = halve(a_keep, a_got)
        b_keep, b_send = halve(b_keep, b_got)
        send, a_send, new_ffn, outputs = together(
            jnp.concatenate([b_send, tiny]), a_send, together(*new_ffn), together(*outputs)
        )
        got, a_got, block_output, *grad_pieces = together(
            over_low_z(send), over_x(a_send), arrange(where, outputs, BF16), *grad_pieces
        )
        for stage in (over_x, over_high_z):
            half = b_send.shape[0]
            b_keep, b_send = halve(b_keep, got[:half])
            tiny = add_parts(tiny, got[half:])
            send = jnp.concatenate([b_send, tiny])
            if stage is over_x:
                a_keep, a_send = halve(a_keep, a_got)
                send, a_send = together(send, a_send)
                got, a_got = together(over_x(send), over_high_z(a_send))
            else:
                send, *grad_pieces = together(send, *grad_pieces)
                got, input_grad = together(over_high_z(send), arrange(where, grad_pieces, F32))
        attn_shard = joined(add_low(a_keep[0], a_got[0]), add_low(b_keep[0], got[0]))
        small_total = of_parts(tiny) + of_parts(got[1:])
    else:
        grad_pieces = trade([*near, *sends])
        small_total = lax.psum(of_parts(tiny), ("dp", "cam"))
        ffn_grads = (scatter_plain((up_keep, up_got), BY_X), scatter_plain((down_keep, down_got), BY_Y))
        new_ffn = new_of_ffn(jnp.stack(ffn_grads))
        attn_keep = joined(joined(a_keep, out_keep), b_keep)
        attn_send = joined(joined(a_send, out_send), b_send)
        attn_shard = scatter_plain((attn_keep, attn_send), BY_YZ)
        block_output, input_grad = arrange(where, outputs, BF16), arrange(where, grad_pieces, F32)
    small_total = small_total.reshape(-1)[: small_params.size]

    rows_here = attn_master.shape[1]
    split = 3 * PAIR * SIDE_PAIRS
    proj_grad = joined(attn_shard[:, :split], attn_shard[:, split + D :])
    proj_grad = jnp.moveaxis(proj_grad.reshape(rows_here, PAIRS, 3, PAIR), 2, 0).reshape(3, rows_here, D)
    attn_shard = jnp.concatenate([proj_grad, attn_shard[None, :, split : split + D]])
    new_attn = adam_update(
        attn_master, attn_shard, attn_first, attn_second, attn_average, rate_matrix, decay_matrix
    )
    new_small = adam_update(
        small_params, small_total, small_first, small_second, small_average, rate_small, 0.0
    )
    return (block_output, input_grad, *new_attn, *new_ffn, *new_small)


def solution(mesh):
    in_specs = (
        P("dp", "cam", None, None),
        P("dp", "cam", None, None),
        P("dp", None, None),
        P("dp", None, None),
        P(None, ("dp", "cam"), None),
        P(None, ("dp", "cam"), None),
        P(None, ("dp", "cam"), None),
        P(None, ("dp", "cam"), None),
        P(None, ("dp", "cam"), None),
        P(None, ("dp", "cam"), None),
        P(None, ("dp", "cam"), None),
        P(None, ("dp", "cam"), None),
        P(),
        P(),
        P(),
        P(),
    )
    out_specs = (
        P("dp", "cam", None, None),
        P("dp", "cam", None, None),
        P(None, ("dp", "cam"), None),
        P(None, ("dp", "cam"), None),
        P(None, ("dp", "cam"), None),
        P(None, ("dp", "cam"), None),
        P(None, ("dp", "cam"), None),
        P(None, ("dp", "cam"), None),
        P(None, ("dp", "cam"), None),
        P(None, ("dp", "cam"), None),
        P(),
        P(),
        P(),
        P(),
    )
    return jax.shard_map(local, mesh=mesh, in_specs=in_specs, out_specs=out_specs, check_vma=False)
```

```python
import functools

import jax
import jax.numpy as jnp
from jax import lax
from jax.experimental import pallas as pl
from jax.experimental.pallas import tpu as pltpu
from jax.sharding import PartitionSpec as P

D = 512
HEADS = 8
NJ = 14
ADAM_STEP = 10
HD = 64
PAIR = 2 * HD
PAIRS = HEADS // 2
BLOCKS = 32
ROWS = D // BLOCKS
HALF = BLOCKS // 2
CHUNK = 640
SIDE_PAIRS = 2
SIDE_COLS = 3 * PAIR * SIDE_PAIRS
SMALL_BLOCKS = 3
ROW_STEPS = 2

norm_eps = 1e-05
beta_first = 0.5
beta_second = 0.5
adam_eps = 1e-08
rate_matrix = 0.02
rate_small = 0.05
decay_matrix = 0.1
ema_decay = 0.75
log2e = 1.4426950408889634
score_scale = HD**-0.5
F32 = jnp.float32
BF16 = jnp.bfloat16
VMEM_LIMIT = 32 * 2**20
VMEM_LIMIT_FORWARD = 60 * 2**20
NEXT_TO_NOTHING = pl.CostEstimate(flops=1, bytes_accessed=1, transcendentals=0)


def adam_update(master, grad_total, first_old, second_old, average_old, rate, decay):
    first_new = beta_first * first_old + (1.0 - beta_first) * grad_total
    second_new = beta_second * second_old + (1.0 - beta_second) * grad_total * grad_total
    first_hat = first_new / (1.0 - beta_first**ADAM_STEP)
    second_hat = second_new / (1.0 - beta_second**ADAM_STEP)
    master_new = master - rate * (first_hat / (jnp.sqrt(second_hat) + adam_eps) + decay * master)
    average_new = ema_decay * average_old + (1.0 - ema_decay) * master_new
    return (master_new, first_new, second_new, average_new)


def dot(left, right, left_dim, right_dim):
    return lax.dot_general(
        left, right, (((left_dim,), (right_dim,)), ((), ())), preferred_element_type=F32
    )


DEVICE_BITS = {"x": 2, "y": 4, "z": 8, "Z": 16}
BY_X, BY_Y, BY_YZ = "xyzZ", "yxzZ", "yzxZ"


def apart(position, order, core):
    bits = (DEVICE_BITS[name] for n, name in enumerate(order) if position >> (3 - n) & 1)
    return core + sum(bits)


def row_blocks(device, order):
    for core in range(2):
        for position in range(HALF):
            start = (device ^ apart(position, order, core)) * ROWS
            yield core, position, pl.ds(pl.multiple_of(start, ROWS), ROWS)


def put_rows(target, sides, order, device, part=None, cols=slice(None)):
    for core, position, rows in row_blocks(device, order):
        which, at = divmod(position, HALF // len(sides[core]))
        array = sides[core][which]
        target[rows, :] = array[at] if part is None else array[part, at, :, cols]


def take_rows(source, sides, order, device):
    for core, position, rows in row_blocks(device, order):
        sides[core][position] = source[rows, :].astype(BF16)


def mean_last(values):
    return jnp.sum(values, axis=-1, keepdims=True) * (1.0 / D)


def normal_rows(values):
    centred = values - mean_last(values)
    inverse = lax.rsqrt(mean_last(centred * centred) + norm_eps)
    return centred * inverse, inverse


def normal_back(normal, inverse, grad):
    return inverse * (grad - mean_last(grad) - normal * mean_last(grad * normal))


def column_sum(values):
    return jnp.sum(values, axis=0, keepdims=True)


def small_row(vectors, n):
    pieces = D // PAIR
    return jnp.concatenate([vectors[pieces * n + m : pieces * n + m + 1, :] for m in range(pieces)], axis=1)


def active_joints(where, state, mask):
    here = pl.ds(where[2], 1)
    row = state[0, here, :] * mask[0, here, :].astype(F32)
    shape = (NJ, NJ)
    same = lax.broadcasted_iota(jnp.int32, shape, 0) == lax.broadcasted_iota(jnp.int32, shape, 1)
    return jnp.sum(jnp.where(same, row, 0.0), axis=1, keepdims=True)


def spread_heads(values, other):
    lane = lax.broadcasted_iota(jnp.int32, (1, PAIR), 1)
    low = lane < HD
    return jnp.where(low, values, other), jnp.where(low, other, values)


def attend_kernel(base, seg_len, where, *refs):
    first = base == 0
    if first:
        pieces, joints, refs = refs[:4], refs[4:6], refs[6:]
    else:
        rounded, refs = refs[0], refs[7:]
    sides, vectors, refs = (refs[0:2], refs[2:4]), refs[4], refs[5:]
    if first:
        rounded, top_rows, refs = refs[0], refs[1], refs[2:]
    q_out, k_out, v_out, a_out, l_out, weight, logs = refs
    device, slot = where[0], where[1]

    if first:

        @pl.when(pl.program_id(0) == 0)
        def _():
            for k in range(4):
                start = pl.multiple_of((slot ^ k) * seg_len, 16)
                rounded[pl.ds(start, seg_len), :] = pieces[k][...]
            joint_rows = jnp.concatenate([small_row(vectors, 8 + n) for n in range(NJ)], axis=0)
            joint = column_sum(active_joints(where, *joints) * joint_rows)
            top = rounded[:16, :].astype(F32)
            at = lax.broadcasted_iota(jnp.int32, (16, 1), 0)
            top = jnp.where(at == 1, top + joint, top)
            top_rows[...] = top[:8]
            rounded[:16, :] = top.astype(BF16)

    for part in range(3):
        put_rows(weight.at[:, part * PAIR : (part + 1) * PAIR], sides, BY_X, device, part)
    pair = pl.program_id(0) + base
    bias_q, bias_v = vectors[pl.ds(pair, 1), :], vectors[pl.ds(PAIRS + pair, 1), :]
    projected = dot(rounded[...], weight[...], 1, 0)
    q_out[...] = (projected[:, :PAIR] + bias_q).astype(BF16)
    keys = projected[:, PAIR : 2 * PAIR].astype(BF16)
    values = (projected[:, 2 * PAIR :] + bias_v).astype(BF16)
    k_out[...] = keys
    v_out[...] = values
    lane = lax.broadcasted_iota(jnp.int32, (1, PAIR), 1)
    low = lane < HD
    value_heads = spread_heads(values, jnp.ones_like(values))
    scale = log2e * score_scale
    for step in range(4):
        rows = pl.ds(step * seg_len, seg_len)
        query = q_out[rows, :]
        mixed, tops = [], []
        for query_head, value_head in zip(spread_heads(query, jnp.zeros_like(query)), value_heads):
            scores = dot(query_head, keys, 1, 1)
            top = jnp.max(scores, axis=1, keepdims=True) * scale
            probs = jnp.exp2(scores * scale - top).astype(BF16)
            mixed.append(dot(probs, value_head, 1, 0))
            tops.append(top)
        total = pltpu.roll(jnp.where(low, mixed[1], mixed[0]), HD, 1)
        a_out[rows, :] = (jnp.where(low, mixed[0], mixed[1]) / total).astype(BF16)
        logs[rows, :] = jnp.where(low, tops[0], tops[1]) + jnp.log2(total)
    turned = logs[...].T
    l_out[0:1, :] = turned[0:1]
    l_out[1:2, :] = turned[HD : HD + 1]


def gate_both(values):
    def low(constant):
        return jnp.asarray(constant, BF16)

    values = values.astype(BF16)
    size = jnp.abs(values)
    fraction = low(1.0) / (low(1.0) + low(0.3275911 * 0.5**0.5) * size)
    bell = jnp.exp2(values * values * low(-0.5 * log2e))
    series = low(0.5 * 1.061405429) * fraction - low(0.5 * 1.453152027)
    series = series * fraction + low(0.5 * 1.421413741)
    series = series * fraction - low(0.5 * 0.284496736)
    series = series * fraction + low(0.5 * 0.254829592)
    tail = series * fraction * bell
    bend = size * bell * low(0.3989422804014327) - tail
    slope = jnp.where(values > low(0.0), low(1.0) + bend, -bend)
    return jnp.maximum(values, low(0.0)) - size * tail, slope


def project_kernel(seg_len, where, *refs):
    rounded, top_rows, mixed, sides, vectors = *refs[:3], (refs[3:5], refs[5:7]), refs[7]
    h1_out, normed_out, y1_out, w_out = refs[8:]
    out_scale = (4 * seg_len / 3.0) ** 0.5

    @pl.when(pl.program_id(0) == 0)
    def _():
        put_rows(w_out, sides, BY_X, where[0], 0)

    summed = rounded[...].astype(F32)
    top = jnp.where(pl.program_id(0) == 0, top_rows[...], summed[:8])
    summed = jnp.concatenate([top, summed[8:]], axis=0)
    summed = summed + (dot(mixed[...], w_out[...], 1, 0) * out_scale + small_row(vectors, 2))
    h1_out[...] = summed
    normal, _ = normal_rows(summed)
    result = normal * small_row(vectors, 3) + small_row(vectors, 4)
    normed_out[...] = result
    y1_out[...] = result.astype(BF16)


def forward_kernel(seg_len, where, *refs):
    y1, up_sides, down_sides = refs[0], (refs[1:3], refs[3:5]), (refs[5:7], refs[7:9])
    vectors, normed_in, g_out, slope_out, total, w_up, w_down, normed, arrived = refs[9:]
    load = pltpu.make_async_copy(normed_in, normed, arrived)
    device = where[0]

    @pl.when(pl.program_id(0) == 0)
    def _():
        total[...] = jnp.zeros_like(total)
        load.start()

    put_rows(w_up, up_sides, BY_X, device)
    put_rows(w_down, down_sides, BY_Y, device)
    lanes = vectors.shape[1]
    first_row = (8 + NJ) * (D // lanes) + pl.program_id(0) * (CHUNK // lanes)
    hidden_bias = [vectors[pl.ds(first_row + n, 1), :] for n in range(CHUNK // lanes)]
    hidden_bias = jnp.concatenate(hidden_bias, axis=1)
    for step in range(4):
        rows = pl.ds(step * seg_len, seg_len)
        inner = dot(y1[rows, :], w_up[...], 1, 0) + hidden_bias
        active, slope = gate_both(inner)
        active = active.astype(BF16)
        g_out[rows, :] = active
        slope_out[rows, :] = slope.astype(BF16)
        total[rows, :] += dot(active, w_down[...], 1, 1)

    @pl.when(pl.program_id(0) == pl.num_programs(0) - 1)
    def _():
        load.wait()
        total[...] += normed[...] + small_row(vectors, 5)


def second_kernel(seg_len, where, *refs):
    forward, active, vectors, cotangents, refs = *refs[:3], refs[3:7], refs[7:]
    pieces, dh2_out, df_out, vector_grads, refs = refs[:4], refs[4], refs[5], refs[6], refs[7:]
    down_grads, grad = refs[:2], refs[2]
    device, slot = where[0], where[1]

    @pl.when(pl.program_id(0) == 0)
    def _():
        gain_grad = shift_grad = bias_grad = 0.0
        for k in range(4):
            rows = pl.ds(pl.multiple_of((slot ^ k) * seg_len, 16), seg_len)
            normal, inverse = normal_rows(forward[rows, :])
            pieces[k][...] = (normal * small_row(vectors, 6) + small_row(vectors, 7)).astype(BF16)
            cotangent = cotangents[k][...].astype(F32)
            gain_grad += column_sum(cotangent * normal)
            shift_grad += column_sum(cotangent)
            middle = normal_back(normal, inverse, cotangent * small_row(vectors, 6))
            dh2_out[rows, :] = middle
            rounded = middle.astype(BF16)
            df_out[rows, :] = rounded
            bias_grad += column_sum(rounded.astype(F32))
        vector_grads[0:1, :] = gain_grad
        vector_grads[1:2, :] = shift_grad
        vector_grads[2:3, :] = bias_grad

    grad[...] = dot(df_out[...], active[...], 0, 0)
    take_rows(grad, down_grads, BY_Y, device)


def backward_kernel(seg_len, where, *refs):
    dh2, df, y1, slope, refs = *refs[:4], refs[4:]
    up_sides, down_sides, refs = (refs[0:2], refs[2:4]), (refs[4:6], refs[6:8]), refs[8:]
    up_grads, hidden_grad, total, refs = refs[:2], refs[2], refs[3], refs[4:]
    dz, w_up, w_down, grad = refs
    device = where[0]

    @pl.when(pl.program_id(0) == 0)
    def _():
        total[...] = dh2[...]

    put_rows(w_up, up_sides, BY_X, device)
    put_rows(w_down, down_sides, BY_Y, device)
    bias_grad = 0.0
    for step in range(4):
        rows = pl.ds(step * seg_len, seg_len)
        inner = (dot(df[rows, :], w_down[...], 1, 0) * slope[rows, :].astype(F32)).astype(BF16)
        dz[rows, :] = inner
        bias_grad += column_sum(inner.astype(F32))
        total[rows, :] += dot(inner, w_up[...], 1, 1)
    hidden_grad[...] = bias_grad
    grad[...] = dot(y1[...], dz[...], 0, 0)
    take_rows(grad, up_grads, BY_X, device)


def first_kernel(seg_len, where, *refs):
    above_in, h1, mixed, sides, vectors = *refs[:3], (refs[3:5], refs[5:7]), refs[7]
    dh1_out, da_out, vector_grads, grad_sides, w_out, grad = *refs[8:11], refs[11:13], *refs[13:]
    device, step = where[0], pl.program_id(0)
    out_scale = (4 * seg_len / 3.0) ** 0.5

    @pl.when(step == 0)
    def _():
        put_rows(w_out, sides, BY_X, device, 0)
        vector_grads[...] = jnp.zeros_like(vector_grads)
        grad[...] = jnp.zeros_like(grad)

    normal, inverse = normal_rows(h1[...])
    above = above_in[...]
    vector_grads[0:1, :] += column_sum(above * normal)
    vector_grads[1:2, :] += column_sum(above)
    summed = normal_back(normal, inverse, above * small_row(vectors, 3))
    dh1_out[...] = summed
    rounded = summed.astype(BF16)
    vector_grads[2:3, :] += column_sum(rounded.astype(F32))
    da_out[...] = (dot(rounded, w_out[...], 1, 1) * out_scale).astype(BF16)
    grad[...] += dot(mixed[...], rounded, 0, 0) * out_scale

    @pl.when(step == pl.num_programs(0) - 1)
    def _():
        take_rows(grad, grad_sides, BY_YZ, device)


def attend_back_kernel(aliased, where, *refs):
    q, k, v, a, da, logs, refs = *refs[:6], refs[6:]
    rounded, (keep, send, parts, bias_grads) = refs[0], refs[1 + aliased : 5 + aliased]
    query_turned, grad = refs[5 + aliased :]
    seq_len = q.shape[0]

    queries, mixed_grads = q[...], da[...]
    zeros = jnp.zeros_like(queries)
    query_heads = spread_heads(queries, zeros)
    grad_heads = spread_heads(mixed_grads, zeros)
    product = (mixed_grads.astype(F32) * a[...].astype(F32)).T
    inner = (column_sum(product[:HD]), column_sum(product[HD:]))
    start = 0
    while start < seq_len:
        size = min(256, seq_len - start)
        rows = pl.ds(start, size)
        none = jnp.zeros((size, PAIR), BF16)
        key_grad = value_grad = query_grad = 0.0
        heads = zip(spread_heads(k[rows, :], none), spread_heads(v[rows, :], none))
        for h, (key_head, value_head) in enumerate(heads):
            scores = dot(key_head, queries, 1, 1)
            probs = jnp.exp2(scores * (log2e * score_scale) - logs[h : h + 1, :])
            grads = (probs * (dot(value_head, mixed_grads, 1, 1) - inner[h])).astype(BF16)
            value_grad += dot(probs.astype(BF16), grad_heads[h], 1, 0)
            key_grad += dot(grads, query_heads[h], 1, 0)
            query_grad += dot(key_head, grads, 0, 0)
        parts[rows, PAIR : 2 * PAIR] = (key_grad * score_scale).astype(BF16)
        parts[rows, 2 * PAIR :] = value_grad.astype(BF16)
        if start == 0:
            query_turned[...] = query_grad
        else:
            query_turned[...] += query_grad
        start += size
    parts[:, :PAIR] = (query_turned[...].T * score_scale).astype(BF16)
    bias_grads[0:1, :] = column_sum(parts[:, :PAIR].astype(F32))
    bias_grads[1:2, :] = column_sum(parts[:, 2 * PAIR :].astype(F32))
    grad[...] = dot(rounded[...], parts[...], 0, 0)
    take_rows(grad, (keep, send), BY_YZ, where[0])


def input_back_kernel(far, where, *refs):
    dh1, parts, weight, refs = refs[0:2], refs[2:4], refs[4], refs[5:]
    if far:
        top_dh1, top_parts, joints, small_parts = *refs[:2], refs[2:4], refs[4:10]
        sends, small_out, joined = refs[10:12], *refs[12:]
        top = top_dh1[...] + dot(top_parts[...], weight[...], 1, 1)
        join_small(joined, small_parts, active_joints(where, *joints) * top[1:2, :])
        for n in range(SMALL_BLOCKS):
            small_out[n] = two_parts(joined[n * (ROWS // 2) : (n + 1) * (ROWS // 2)])
    else:
        sends = refs
    for n, send in enumerate(sends):
        send[...] = (dh1[n][...] + dot(parts[n][...], weight[...], 1, 1)).astype(send.dtype)


def call(kernel, name, where, grid, operands, results, scratch, aliases=None, limit=VMEM_LIMIT):
    def spec(block, index):
        if block is None:
            return pl.BlockSpec(memory_space=pl.ANY)
        if index.__code__.co_argcount == 2:
            return pl.BlockSpec(block, index)
        return pl.BlockSpec(block, lambda i, _: index(i))

    return pl.pallas_call(
        kernel,
        grid_spec=pltpu.PrefetchScalarGridSpec(
            num_scalar_prefetch=1,
            grid=(grid,),
            in_specs=[spec(block, index) for _, block, index in operands],
            out_specs=[spec(block, index) for _, block, index in results],
            scratch_shapes=[pltpu.VMEM(*x) if isinstance(x, tuple) else x for x in scratch],
        ),
        out_shape=[shape for shape, _, _ in results],
        input_output_aliases={source + 1: target for source, target in (aliases or {}).items()},
        compiler_params=pltpu.CompilerParams(vmem_limit_bytes=limit),
        cost_estimate=NEXT_TO_NOTHING,
        name=name,
    )(where, *(x for x, _, _ in operands))


def whole(x):
    return (x, x.shape, lambda i: (0,) * len(x.shape))


def shape_of(shape, kind):
    return jax.ShapeDtypeStruct(shape, kind)


def whole_out(shape, kind):
    return whole(shape_of(shape, kind))


def flat(sides):
    return [x for side in sides for x in side]


def pair_weights(sides, base):
    return [(x, (3, x.shape[1], ROWS, PAIR), lambda i: (0, 0, 0, i + base)) for x in flat(sides)]


def attend(base, pairs, where, source, sides, vectors, seg_len):
    seq_len = 4 * seg_len
    first = base == 0

    def column(x):
        return (x, (seq_len, PAIR), lambda i: (0, i + base))

    operands = [whole(x) for x in (source[:4] if first else source[:1])]
    if first:
        operands += [(x, (1, *x.shape[1:]), lambda i, at: (at[1], 0, 0)) for x in source[4:]]
    operands += [] if first else [(x, None, None) for x in source[1:]]
    operands += pair_weights(sides, base) + [whole(vectors)]
    results = [whole_out((seq_len, D), BF16), whole_out((8, D), F32)] if first else []
    results += [column(shape_of((seq_len, D), BF16))] * 4
    logs = shape_of((PAIRS, 2, seq_len), F32)
    results += [(logs, (None, 2, seq_len), lambda i: (i + base, 0, 0))]
    results += [(shape_of((D, 3 * D), BF16), (D, 3 * PAIR), lambda i: (0, i + base))]
    scratch = [((seq_len, PAIR), F32)]
    return call(
        functools.partial(attend_kernel, base, seg_len),
        f"attend_{base}",
        where,
        pairs,
        operands,
        results,
        scratch,
        {} if first else {1 + n: n for n in range(6)},
        limit=VMEM_LIMIT_FORWARD,
    )


def by_chunk(x):
    if x.ndim == 3:
        return (x, (x.shape[0], ROWS, CHUNK), lambda i: (0, 0, i))
    return (x, (x.shape[0], CHUNK), lambda i: (0, i))


def out_weight(sides):
    return [(x, (1, x.shape[1], ROWS, D), lambda i: (3, 0, 0, 0)) for x in flat(sides)]


def by_rows(x):
    return (x, (x.shape[0] // ROW_STEPS, x.shape[1]), lambda i: (i, 0))


def project(where, rounded, top_rows, mixed, sides, vectors):
    seq_len = rounded.shape[0]
    return call(
        functools.partial(project_kernel, seq_len // 4),
        "project",
        where,
        ROW_STEPS,
        [by_rows(rounded), whole(top_rows), by_rows(mixed), *out_weight(sides), whole(vectors)],
        [by_rows(shape_of((seq_len, D), kind)) for kind in (F32, F32, BF16)],
        [((D, D), BF16)],
        limit=VMEM_LIMIT_FORWARD,
    )


def feed_forward(where, y1, normed, up, down, vectors):
    seq_len = y1.shape[0]
    hidden = up[0][0].shape[-1]
    wide = by_chunk(shape_of((seq_len, hidden), BF16))
    return call(
        functools.partial(forward_kernel, seq_len // 4),
        "feed_forward",
        where,
        hidden // CHUNK,
        [whole(y1)] + [by_chunk(x) for x in (*flat(up), *flat(down))] + [whole(vectors), (normed, None, None)],
        [wide, wide, whole_out((seq_len, D), F32)],
        [((D, CHUNK), BF16)] * 2 + [((seq_len, D), F32), pltpu.SemaphoreType.DMA(())],
        limit=VMEM_LIMIT_FORWARD,
    )


def second_norm(where, forward, active, vectors, cotangents):
    seq_len, hidden = active.shape
    seg_len = seq_len // 4
    operands = [whole(forward), by_chunk(active), whole(vectors)]
    results = [whole_out((seg_len, D), BF16)] * 4
    results += [whole_out((seq_len, D), F32), whole_out((seq_len, D), BF16), whole_out((8, D), F32)]
    results += [by_chunk(shape_of((HALF, ROWS, hidden), BF16))] * 2
    return call(
        functools.partial(second_kernel, seg_len),
        "second_norm",
        where,
        hidden // CHUNK,
        operands + [whole(x) for x in cotangents],
        results,
        [((D, CHUNK), F32)],
        limit=VMEM_LIMIT_FORWARD,
    )


def feed_back(where, dh2, df, y1, slope, up, down):
    seq_len, hidden = slope.shape
    operands = [whole(dh2), whole(df), whole(y1)] + [by_chunk(x) for x in (slope, *flat(up), *flat(down))]
    results = [by_chunk(shape_of((HALF, ROWS, hidden), BF16))] * 2
    results += [by_chunk(shape_of((1, hidden), F32)), whole_out((seq_len, D), F32)]
    scratch = [((seq_len, CHUNK), BF16)] + [((D, CHUNK), BF16)] * 2 + [((D, CHUNK), F32)]
    return call(
        functools.partial(backward_kernel, seq_len // 4),
        "feed_back",
        where,
        hidden // CHUNK,
        operands,
        results,
        scratch,
        limit=VMEM_LIMIT_FORWARD,
    )


def first_norm_back(where, above, h1, mixed, sides, vectors):
    seq_len = h1.shape[0]
    results = [by_rows(shape_of((seq_len, D), kind)) for kind in (F32, BF16)]
    results += [whole_out((8, D), F32)]
    results += [whole_out((HALF, ROWS, D), BF16)] * 2
    return call(
        functools.partial(first_kernel, seq_len // 4),
        "first_norm_back",
        where,
        ROW_STEPS,
        [by_rows(x) for x in (above, h1, mixed)] + [*out_weight(sides), whole(vectors)],
        results,
        [((D, D), BF16), ((D, D), F32)],
    )


def attend_back(base, pairs, where, heads, da, logs, rounded, sides=(), parts=()):
    seq_len = da.shape[0]
    operands = [(x, (seq_len, PAIR), lambda i: (0, i + base)) for x in (*heads, da)]
    operands += [(logs, (None, 2, seq_len), lambda i: (i + base, 0, 0)), whole(rounded)]
    aliases = {len(operands) + n: n for n in range(len(sides))}
    aliases |= {len(operands) + len(sides) + n: 2 for n in range(len(parts))}
    operands += [(x, None, None) for x in (*sides, *parts)]
    side = shape_of((HALF, ROWS, SIDE_COLS), BF16)
    results = [(side, (HALF, ROWS, 3 * PAIR), lambda i: (0, 0, (i + base) % SIDE_PAIRS))] * 2
    results += [(shape_of((seq_len, 3 * D), BF16), (seq_len, 3 * PAIR), lambda i: (0, i + base))]
    results += [(shape_of((8, pairs * PAIR), F32), (8, PAIR), lambda i: (0, i))]
    return call(
        functools.partial(attend_back_kernel, len(sides) + len(parts)),
        f"attend_back_{base}",
        where,
        pairs,
        operands,
        results,
        [((PAIR, seq_len), F32), ((D, 3 * PAIR), F32)],
        aliases,
    )


def input_back(first, where, dh1, parts, weight, joints=(), small=()):
    seg_len = dh1.shape[0] // 4
    far = first == 2

    def segment(x, n):
        return pl.BlockSpec((seg_len, x.shape[1]), lambda i, at: (at[1] ^ (first + n), 0))

    def full(x):
        return pl.BlockSpec(x.shape, lambda i, _: (0,) * len(x.shape))

    operands = [dh1, dh1, parts, parts, weight]
    specs = [segment(x, n) for x in (dh1, parts) for n in range(2)] + [full(weight)]
    results = [shape_of((seg_len, D), BF16 if far or n else F32) for n in range(2)]
    scratch = []
    if far:
        operands += [dh1, parts, *joints, *small]
        specs += [pl.BlockSpec((ROWS, x.shape[1]), lambda i, _: (0, 0)) for x in (dh1, parts)]
        specs += [pl.BlockSpec((1, *x.shape[1:]), lambda i, at: (at[1], 0, 0)) for x in joints]
        specs += [full(x) for x in small]
        results += [shape_of((SMALL_BLOCKS, ROWS, SIDE_COLS), BF16)]
        scratch += [pltpu.VMEM((SMALL_BLOCKS * ROWS // 2, SIDE_COLS), F32)]
    return pl.pallas_call(
        functools.partial(input_back_kernel, far),
        grid_spec=pltpu.PrefetchScalarGridSpec(
            num_scalar_prefetch=1,
            grid=(1,),
            in_specs=specs,
            out_specs=[full(x) for x in results],
            scratch_shapes=scratch,
        ),
        out_shape=results,
        compiler_params=pltpu.CompilerParams(vmem_limit_bytes=VMEM_LIMIT),
        cost_estimate=NEXT_TO_NOTHING,
        name=f"input_back_{first}",
    )(where, *operands)


def join_small(joined, parts, by_joint):
    *biases, first, second, hidden = parts
    units = [x[n : n + 1, :] for n in range(2) for x in biases]
    units += [first[n : n + 1, :] for n in (2, 0, 1)] + [second[n : n + 1, :] for n in (2, 0, 1)]
    units += [by_joint[n : n + 1, :] for n in range(NJ)] + [hidden[...]]
    joined[...] = jnp.zeros_like(joined)
    at, width = 0, joined.shape[1]
    for unit in units:
        taken = 0
        while taken < unit.shape[1]:
            row, column = divmod(at, width)
            size = min(width - column, unit.shape[1] - taken)
            joined[row : row + 1, column : column + size] = unit[:, taken : taken + size]
            taken, at = taken + size, at + size


def two_parts(values):
    high = lax.reduce_precision(values, 8, 7)
    return jnp.concatenate([high, lax.reduce_precision(values - high, 8, 7)], axis=-2).astype(BF16)


def of_parts(parts):
    half = parts.shape[-2] // 2
    return parts[..., :half, :].astype(F32) + parts[..., half:, :].astype(F32)


def arrange_kernel(where, *refs):
    pieces, out, landed, widened, sem_in, sem_out = refs[:4], *refs[4:]
    loads = [pltpu.make_async_copy(x, landed.at[n], sem_in.at[n]) for n, x in enumerate(pieces[1:])]
    loads.append(pltpu.make_async_copy(pieces[0], widened.at[3], sem_in.at[3]))
    for load in loads:
        load.start()
    stores = []
    for n, load in enumerate(loads):
        load.wait()
        if n < 3:
            widened[n] = landed[n].astype(out.dtype)
        target = out.at[where[1] ^ ((n + 1) % 4), 0]
        stores.append(pltpu.make_async_copy(widened.at[n], target, sem_out.at[n]))
        stores[n].start()
    for store in stores:
        store.wait()


def arrange(where, pieces, kind):
    seg_len = pieces[1].shape[0]
    return pl.pallas_call(
        arrange_kernel,
        grid_spec=pltpu.PrefetchScalarGridSpec(
            num_scalar_prefetch=1,
            grid=(1,),
            in_specs=[pl.BlockSpec(memory_space=pl.ANY)] * 4,
            out_specs=pl.BlockSpec(memory_space=pl.ANY),
            scratch_shapes=[
                pltpu.VMEM((3, seg_len, D), BF16),
                pltpu.VMEM((4, seg_len, D), kind),
                pltpu.SemaphoreType.DMA((4,)),
                pltpu.SemaphoreType.DMA((4,)),
            ],
        ),
        out_shape=jax.ShapeDtypeStruct((4, 1, seg_len, D), kind),
        compiler_params=pltpu.CompilerParams(vmem_limit_bytes=VMEM_LIMIT),
        cost_estimate=NEXT_TO_NOTHING,
        name="arrange",
    )(where, *pieces)


def partner(value, axis, mask):
    pairs = [(source, source ^ mask) for source in range(lax.axis_size(axis))]
    return lax.ppermute(value, axis, pairs)


def over_core(value):
    return partner(value, "cam", 1)


def over_x(value):
    return partner(value, "cam", 2)


def over_y(value):
    return partner(value, "dp", 1)


def over_y_and_core(value):
    pairs = [(source, source ^ 5) for source in range(BLOCKS)]
    return lax.ppermute(value, ("dp", "cam"), pairs)


def over_z(value, apart_by):
    return partner(value, "dp", 2 * apart_by)


def stages_of(order):
    return (over_x, over_y) if order == BY_X else (over_y, over_x)


def by_blocks():
    return lax.axis_size("dp") * lax.axis_size("cam") == BLOCKS


def doubled(held, stage, axis=0):
    return jnp.concatenate([held, stage(held)], axis=axis)


def gather_plain(shard, order):
    at = shard.ndim - 2
    full = lax.all_gather(shard, ("dp", "cam"), axis=at, tiled=True)
    full = full.reshape(*full.shape[:at], 2, 2, 2, 2, 2, ROWS, full.shape[-1])
    places = ["Zzyx".index(name) + at for name in order]
    full = jnp.moveaxis(full, (at + 4, *places), (0, *range(at + 1, at + 5)))
    full = full.reshape(2, *shard.shape[:at], HALF, *full.shape[-2:])
    return full[0], full[1]


def split_sides(shard, order, at):
    return tuple(tuple(jnp.split(x, 2, axis=at)) for x in gather_plain(shard, order))


def scatter_plain(sides, order):
    full = jnp.stack(sides).reshape(2, 2, 2, 2, 2, ROWS, sides[0].shape[-1])
    places = (4, *("Zzyx".index(name) for name in order))
    full = jnp.moveaxis(full, range(5), places).reshape(D, sides[0].shape[-1])
    return lax.psum_scatter(full.astype(F32), ("dp", "cam"), scatter_dimension=0, tiled=True)


def halve(held, received):
    half = held.shape[0] // 2

    def part(rows):
        return (held[rows].astype(F32) + received[rows].astype(F32)).astype(BF16)

    return part(slice(0, half)), part(slice(half, None))


def over_low_z(value):
    return over_z(value, 1)


def over_high_z(value):
    return over_z(value, 2)


def add_low(mine, other):
    return mine.astype(F32) + other.astype(F32)


def together(*values):
    return lax.optimization_barrier(values)


def joined(left, right):
    return jnp.concatenate([left, right], axis=-1)


def add_parts(mine, other):
    return two_parts(of_parts(mine) + of_parts(other))


def after(value, *others):
    return lax.optimization_barrier((value, *others))[0]


def local(
    tokens,
    out_grad,
    joint_state,
    joint_mask,
    attn_master,
    attn_first,
    attn_second,
    attn_average,
    ffn_master,
    ffn_first,
    ffn_second,
    ffn_average,
    small_params,
    small_first,
    small_second,
    small_average,
):
    cam_index = lax.axis_index("cam")
    slot, group_index = cam_index % 4, cam_index // 4
    items_here, _, seg_len, _ = tokens.shape
    assert items_here == 4
    device = lax.axis_index("dp") * lax.axis_size("cam") + cam_index if by_blocks() else 0
    where = jnp.stack([jnp.int32(device), jnp.int32(slot), jnp.int32(group_index)])

    def pieces_of(array):
        return [lax.dynamic_index_in_dim(array[:, 0], slot ^ n, 0, keepdims=False) for n in range(4)]

    def new_of_ffn(gradient):
        return adam_update(
            ffn_master, gradient, ffn_first, ffn_second, ffn_average, rate_matrix, decay_matrix
        )

    def trade(pieces):
        return [pieces[0]] + [partner(pieces[n], "cam", n) for n in range(1, 4)]

    blocks = by_blocks()
    sequence = trade(pieces_of(tokens))
    cotangents = pieces_of(out_grad)
    attn_low = attn_master.astype(BF16)
    ffn_low = ffn_master.astype(BF16)
    vectors = small_params.reshape(-1, PAIR)
    joints = joint_state, joint_mask
    here = where
    if blocks:
        held = doubled(attn_low[:, None], over_high_z, 1)
        held, ffn_low = together(held, ffn_low)
        wide = doubled(ffn_low[:, None], over_high_z, 1)
        held = doubled(held, over_low_z, 1)
        held = doubled(held, over_y, 1)
        wide, here, cotangents[1], *sequence = together(wide, here, cotangents[1], *sequence)
        near = held, over_x(held)
        far = tuple(over_core(x) for x in near)
        wide = doubled(wide, over_low_z, 1)
        wide, here, vectors, *far = together(wide, here, vectors, *far)
        sides = near, far
        up, down = doubled(wide[0], over_y), doubled(wide[1], over_x)
    else:
        sides = split_sides(attn_low, BY_X, 1)
        up, down = split_sides(ffn_low[0], BY_X, 0), split_sides(ffn_low[1], BY_Y, 0)

    rounded, top_rows, *heads = attend(0, 1, here, [*sequence, *joints], sides, vectors, seg_len)
    here = where
    if blocks:
        here, up, down, *heads = together(where, up, down, *heads)
        up, down = (up, over_x(up)), (down, over_y(down))
        far = over_core(up[0]), over_core(down[0])
    *heads, logs, weight = attend(1, PAIRS - 1, here, [rounded, *heads], sides, vectors, seg_len)
    here = where
    if blocks:
        here, up_got, down_got, logs, *far = together(where, up[1], down[1], logs, *far)
        up = ((up[0], up_got), (far[0], over_core(up_got)))
        down = ((down[0], down_got), (far[1], over_core(down_got)))
    h1, normed, y1 = project(here, rounded, top_rows, heads[3], sides, vectors)
    cotangents = trade([after(x, y1) for x in cotangents])
    gated, slope, forward = feed_forward(where, y1, normed, up, down, vectors)
    *results, dh2, df, grads_two, down_keep, down_send = second_norm(
        where, forward, gated, vectors, cotangents
    )
    outputs = trade(results)
    down_got = over_core(down_send) if blocks else down_send
    up_keep, up_send, hidden_grad, above = feed_back(where, dh2, df, y1, slope, up, down)
    here, up_send, down_got, *outputs = together(where, up_send, down_got, *outputs)

    def back(base, pairs, here, *filled):
        return attend_back(base, pairs, here, heads, da, logs, rounded, *filled)

    up_got = over_core(up_send) if blocks else up_send
    if blocks:
        down_keep, down_send = halve(down_keep, down_got)
        here, down_keep, down_send = together(here, down_keep, down_send)
    dh1, da, grads_one, out_keep, out_send = first_norm_back(here, above, h1, heads[3], sides, vectors)
    here = where
    if blocks:
        up_got, da = together(up_got, da)
        up_keep, up_send = halve(up_keep, up_got)
        here, up_send, down_send, out_send = together(where, up_send, down_send, out_send)
        up_got, down_got, out_got = over_x(up_send), over_y(down_send), over_core(out_send)
    a_keep, a_send, parts, bias_a = back(0, 2, here)
    here = where
    if blocks:
        up_got, down_got, out_got, bias_a = together(up_got, down_got, out_got, bias_a)
        up_keep, up_send = halve(up_keep, up_got)
        down_keep, down_send = halve(down_keep, down_got)
        here, up_send, down_send, a_send = together(where, up_send, down_send, a_send)
        up_got, down_got, a_got = over_y(up_send), over_x(down_send), over_core(a_send)
    b_keep, b_send, parts, bias_2 = back(2, 1, here, (), (parts,))
    here = where
    if blocks:
        up_got, down_got, a_got, bias_2 = together(up_got, down_got, a_got, bias_2)
        up_keep, up_send = halve(up_keep, up_got)
        down_keep, down_send = halve(down_keep, down_got)
        keep, send = jnp.stack([up_keep, down_keep], 1), jnp.stack([up_send, down_send], 1)
        a_keep, a_send = halve(joined(a_keep, out_keep), joined(a_got, out_got))
        here, send, a_send = together(where, send, a_send)
        got, a_got = over_low_z(send), over_y(a_send)
    b_keep, b_send, parts, bias_3 = back(3, 1, here, (b_keep, b_send), (parts,))
    small = (bias_a, bias_2, bias_3, grads_one, grads_two, hidden_grad)
    here = where
    if blocks:
        got, a_got, bias_3 = together(got, a_got, bias_3)
        keep, send = halve(keep, got)
        a_keep, a_send = halve(a_keep, a_got)
        here, send, a_send, b_send = together(where, send, a_send, b_send)
        got, a_got, b_got = over_high_z(send), over_low_z(a_send), over_core(b_send)
    *sends, tiny = input_back(2, here, dh1, parts, weight, joints, small)
    here = where
    if blocks:
        b_got, tiny, *sends = together(b_got, tiny, *sends)
        b_keep, b_send = halve(b_keep, b_got)
        here, b_send = together(where, b_send)
        b_got, tiny_y = over_y(b_send), over_y(tiny)
        tiny_core, tiny_both = over_core(tiny), over_y_and_core(tiny)
        far_piece = partner(sends[0], "cam", 2)
    near = input_back(0, here, dh1, parts, weight)
    if blocks:
        own, far_piece, a_got, tiny_core, tiny_y, tiny_both, b_got, got = together(
            near[0], far_piece, a_got, tiny_core, tiny_y, tiny_both, b_got, got
        )
        new_ffn = new_of_ffn(add_low(keep[0], got[0]))
        tiny = of_parts(tiny) + of_parts(tiny_core)
        tiny = two_parts(tiny + (of_parts(tiny_y) + of_parts(tiny_both)))
        grad_pieces = [own, over_core(near[1]), far_piece, partner(sends[1], "cam", 3)]
        a_keep, a_send = halve(a_keep, a_got)
        b_keep, b_send = halve(b_keep, b_got)
        send, a_send, new_ffn, outputs = together(
            jnp.concatenate([b_send, tiny]), a_send, together(*new_ffn), together(*outputs)
        )
        got, a_got, block_output, *grad_pieces = together(
            over_low_z(send), over_x(a_send), arrange(where, outputs, BF16), *grad_pieces
        )
        for stage in (over_x, over_high_z):
            half = b_send.shape[0]
            b_keep, b_send = halve(b_keep, got[:half])
            tiny = add_parts(tiny, got[half:])
            send = jnp.concatenate([b_send, tiny])
            if stage is over_x:
                a_keep, a_send = halve(a_keep, a_got)
                send, a_send = together(send, a_send)
                got, a_got = over_x(send), over_high_z(a_send)
            else:
                send, *grad_pieces = together(send, *grad_pieces)
                got, input_grad = together(over_high_z(send), arrange(where, grad_pieces, F32))
        attn_shard = joined(add_low(a_keep[0], a_got[0]), add_low(b_keep[0], got[0]))
        small_total = of_parts(tiny) + of_parts(got[1:])
    else:
        grad_pieces = trade([*near, *sends])
        small_total = lax.psum(of_parts(tiny), ("dp", "cam"))
        ffn_grads = (scatter_plain((up_keep, up_got), BY_X), scatter_plain((down_keep, down_got), BY_Y))
        new_ffn = new_of_ffn(jnp.stack(ffn_grads))
        attn_keep = joined(joined(a_keep, out_keep), b_keep)
        attn_send = joined(joined(a_send, out_send), b_send)
        attn_shard = scatter_plain((attn_keep, attn_send), BY_YZ)
        block_output, input_grad = arrange(where, outputs, BF16), arrange(where, grad_pieces, F32)
    small_total = small_total.reshape(-1)[: small_params.size]

    rows_here = attn_master.shape[1]
    split = 3 * PAIR * SIDE_PAIRS
    proj_grad = joined(attn_shard[:, :split], attn_shard[:, split + D :])
    proj_grad = jnp.moveaxis(proj_grad.reshape(rows_here, PAIRS, 3, PAIR), 2, 0).reshape(3, rows_here, D)
    attn_shard = jnp.concatenate([proj_grad, attn_shard[None, :, split : split + D]])
    new_attn = adam_update(
        attn_master, attn_shard, attn_first, attn_second, attn_average, rate_matrix, decay_matrix
    )
    new_small = adam_update(
        small_params, small_total, small_first, small_second, small_average, rate_small, 0.0
    )
    return (block_output, input_grad, *new_attn, *new_ffn, *new_small)


def solution(mesh):
    in_specs = (
        P("dp", "cam", None, None),
        P("dp", "cam", None, None),
        P("dp", None, None),
        P("dp", None, None),
        P(None, ("dp", "cam"), None),
        P(None, ("dp", "cam"), None),
        P(None, ("dp", "cam"), None),
        P(None, ("dp", "cam"), None),
        P(None, ("dp", "cam"), None),
        P(None, ("dp", "cam"), None),
        P(None, ("dp", "cam"), None),
        P(None, ("dp", "cam"), None),
        P(),
        P(),
        P(),
        P(),
    )
    out_specs = (
        P("dp", "cam", None, None),
        P("dp", "cam", None, None),
        P(None, ("dp", "cam"), None),
        P(None, ("dp", "cam"), None),
        P(None, ("dp", "cam"), None),
        P(None, ("dp", "cam"), None),
        P(None, ("dp", "cam"), None),
        P(None, ("dp", "cam"), None),
        P(None, ("dp", "cam"), None),
        P(None, ("dp", "cam"), None),
        P(),
        P(),
        P(),
        P(),
    )
    return jax.shard_map(local, mesh=mesh, in_specs=in_specs, out_specs=out_specs, check_vma=False)
```
